32 devices in a mesh: rcv: 4 (over y, core), src: 8 (over z, x).
Axes of the slice: x: 2, y: 2, z: 4, core: 2. Of those that a mesh axis runs over, the one named last changes fastest.
Arguments:
- pplus: bfloat16 [2048, 2, 1024], P('rcv', None, 'src'), may hold values from -0.125 to 0.125
- pminus: bfloat16 [2048, 2, 1024], P('rcv', None, 'src')
- band: int32 [8, 3], P('rcv'), may hold values from 0 to 7, as said below
Outputs:
- reflectivity: float32 [256, 8, 3, 2, 256], P('src', 'rcv')
- misfit: float32 [2048, 2, 1024], P('rcv', None, 'src')
The draws below stay inside these ranges and needn't reach their ends.
Inputs may be any that keep to these rules, and one draw needn't show every extreme that they name: `band`: row b names block b first and then 3 - 1 other distinct blocks, each at most 2 blocks from b.
All inputs are finite; a program needn't handle non-finite values.
Results may differ from the reference program's by a relative error of at most 0.024.
Values may be sent and summed in bfloat16 or wider, within the bound.
No kernel may reach another device: no remote copies, remote signals or barrier semaphores. Data moves between devices by JAX's collectives and lax.ppermute only.
A program may use at most 64 MiB of HBM per device.

```python
import jax
import jax.numpy as jnp
from jax import lax

BLOCK = 256
NEIGH = 3
HALO_BLK = 2
SRC_DEV = 128
ITERS = 2
NBLK = 8
RECEIVERS = 2048
SOURCES = 1024
N_SRC = 8


def draw_pminus(key, part):
    key_base, key_rough = jax.random.split(key, 2)
    position = jnp.arange(RECEIVERS, dtype=jnp.float32) / RECEIVERS
    rough = jnp.exp(jax.random.uniform(key_rough, (RECEIVERS, 1, 1), jnp.float32, -0.7, 0.7))
    scale = (1.0 + 2.0 * position)[:, None, None] * rough
    values = jax.random.normal(key_base, (RECEIVERS, 2, SOURCES), jnp.float32) * scale
    return values.astype(jnp.bfloat16)


def draw_band(key, part):
    block_rows = jnp.arange(NBLK, dtype=jnp.int32)
    offsets = jnp.concatenate([jnp.arange(-HALO_BLK, 0, dtype=jnp.int32), jnp.arange(1, HALO_BLK + 1, dtype=jnp.int32)])
    target = block_rows[:, None] + offsets[None, :]
    valid = (target >= 0) & (target < NBLK)
    scores = jax.random.randint(key, (NBLK, 2 * HALO_BLK), 0, 1 << 20, dtype=jnp.int32) * (2 * HALO_BLK)
    scores = scores + jnp.arange(2 * HALO_BLK, dtype=jnp.int32)[None, :]
    scores = jnp.where(valid, scores, -1)
    unused, picks = lax.top_k(scores, NEIGH - 1)
    chosen = jnp.take_along_axis(target, picks, axis=1)
    return jnp.concatenate([block_rows[:, None], chosen], axis=1).astype(jnp.int32)


def levels(stream_key, shape, shards, smallest, largest):
    gain, own = 1.0, jax.random.fold_in(stream_key, 6)
    for dim, blocks in shards:
        draws = jnp.exp(jax.random.uniform(jax.random.fold_in(own, dim), (blocks,), jnp.float32, smallest / len(shards), largest / len(shards)))
        gain = gain * jnp.repeat(draws, shape[dim] // blocks).reshape([-1 if axis == dim else 1 for axis in range(len(shape))])
    return gain


def normal_values(stream_key, extent, spread, limit, cuts=(), kind=jnp.bfloat16):
    entries = spread * jax.random.normal(stream_key, extent, jnp.float32)
    if cuts:
        entries = entries * levels(stream_key, extent, cuts, -0.22, 0.18)
    return jnp.clip(entries, -limit, limit).astype(kind)


def setup_inputs(seed: int = 0) -> dict:
    arg_keys = jax.random.split(jax.random.key(seed), 4)
    pplus = normal_values(arg_keys[0], (RECEIVERS, 2, SOURCES), (2 * SOURCES) ** -0.5, 0.125, ((0, 4), (2, 8)))
    pminus = draw_pminus(jax.random.fold_in(arg_keys[3], 71), 0)
    band = draw_band(jax.random.fold_in(arg_keys[3], 71), 0)
    return {"pplus": pplus, "pminus": pminus, "band": band}


def combine_parts(product, sources_all):
    shaped = product.reshape(product.shape[0], 2, 2, sources_all)
    real_part = shaped[:, 0, 0] - shaped[:, 1, 1]
    imag_part = shaped[:, 0, 1] + shaped[:, 1, 0]
    return jnp.stack([real_part, imag_part], axis=1)


def reference(pplus, pminus, band):
    nblocks = band.shape[0]
    merged = pplus.reshape(nblocks, BLOCK, 2 * SOURCES)
    grouped = pplus.reshape(nblocks, BLOCK, 2, N_SRC, SRC_DEV)

    def adjoint(field):
        def one_row(pair):
            rows_bf, indices = pair
            swapped = jnp.stack([rows_bf[:, 1], -rows_bf[:, 0]], axis=1)
            stacked = jnp.stack([rows_bf, swapped], axis=1).reshape(BLOCK, 2, 2, N_SRC, SRC_DEV)
            panels = grouped[indices]
            partial_sums = jnp.einsum('ntugs,kcugs->gnktc', stacked.astype(jnp.float32), panels.astype(jnp.float32))
            rounded = lax.optimization_barrier(partial_sums.astype(jnp.bfloat16))
            return jnp.sum(rounded.astype(jnp.float32), axis=0)
        return lax.map(one_row, (field.astype(jnp.bfloat16), band))

    def forward(direction):
        def one_row(pair):
            dir_rows, indices = pair
            panels = merged[indices]
            product = jnp.einsum('nktc,kcm->ntm', dir_rows.astype(jnp.bfloat16).astype(jnp.float32), panels.astype(jnp.float32))
            return combine_parts(product, SOURCES)
        return lax.map(one_row, (direction, band))

    misfit = pminus.astype(jnp.float32).reshape(nblocks, BLOCK, 2, SOURCES)
    gradient = adjoint(misfit)
    grad_sq = jnp.sum(gradient * gradient)
    direction = gradient
    solution = jnp.zeros_like(gradient)
    for turn_index in range(ITERS):
        image = forward(direction)
        image_sq = jnp.sum(image * image)
        step_size = grad_sq / image_sq
        solution = solution + step_size * direction
        misfit = misfit - step_size * image
        if turn_index + 1 < ITERS:
            gradient = adjoint(misfit)
            grad_next = jnp.sum(gradient * gradient)
            direction = gradient + (grad_next / grad_sq) * direction
            grad_sq = grad_next
    reflectivity = jnp.transpose(solution, (1, 0, 2, 3, 4))
    return reflectivity, misfit.reshape(RECEIVERS, 2, SOURCES)
```

```python
import functools

import jax
import jax.numpy as jnp
from jax import lax
from jax.experimental import pallas as pl
from jax.experimental.pallas import tpu as pltpu
from jax.sharding import PartitionSpec as P

BLOCK = 256
NEIGH = 3
HALO_BLK = 2
ROWS_X = 2


def ring_order(count):
    if count % ROWS_X or count < 2 * ROWS_X:
        return list(range(count))
    half = count // ROWS_X
    return [ROWS_X * p for p in range(half)] + [ROWS_X * p + 1 for p in reversed(range(half))]


def maps_kernel(n_src, groups, *refs):
    n_grp = len(groups)
    table, where, field = refs[:3]
    own = refs[3 : 3 + n_src]
    left = refs[3 + n_src : 3 + n_src + n_grp]
    right = refs[3 + n_src + n_grp : 3 + n_src + 2 * n_grp]
    grad_out, hess_out, image_out, image2_out, sums_out = refs[3 + n_src + 2 * n_grp : 8 + n_src + 2 * n_grp]
    panel, lhs, image0, sems = refs[8 + n_src + 2 * n_grp :]
    blocks_here = panel.shape[0]
    rows = lhs.shape[1] // 2
    cols = field.shape[2]
    half = cols // 2

    def copies(slot, act):
        grp = next(i for i, g in enumerate(groups) if slot in g)
        base = groups[grp].index(slot) * blocks_here * BLOCK
        for i in range(blocks_here):
            for k in range(NEIGH):
                place = table[i * NEIGH + k]
                dst = panel.at[i, pl.ds(k * BLOCK, BLOCK), pl.ds(slot * cols, cols)]

                def one(src, start, dst=dst):
                    c = pltpu.make_async_copy(src.at[pl.ds(pl.multiple_of(start, BLOCK), BLOCK), :], dst, sems.at[slot])
                    c.start()

                if act == "wait":
                    pltpu.make_async_copy(own[slot].at[pl.ds(0, BLOCK), :], dst, sems.at[slot]).wait()
                    continue

                @pl.when(place < HALO_BLK)
                def _():
                    one(left[grp], base + place * BLOCK)

                @pl.when((place >= HALO_BLK) & (place < HALO_BLK + blocks_here))
                def _():
                    one(own[slot], (place - HALO_BLK) * BLOCK)

                @pl.when(place >= HALO_BLK + blocks_here)
                def _():
                    one(right[grp], base + (place - HALO_BLK - blocks_here) * BLOCK)

    for slot in range(n_src):
        copies(slot, "start")

    for slot in range(n_src):
        for i in range(blocks_here):
            rows_bf = field[where[slot], i * rows : (i + 1) * rows, :]
            lhs[i, :rows, slot * cols : (slot + 1) * cols] = rows_bf
            lhs[i, rows:, slot * cols : slot * cols + half] = rows_bf[:, half:]
            lhs[i, rows:, slot * cols + half : (slot + 1) * cols] = -rows_bf[:, :half]

    for slot in range(n_src):
        copies(slot, "wait")

    def fold(x):
        total = x[:, :128]
        for c in range(128, x.shape[1], 128):
            total = total + x[:, c : c + 128]
        return jnp.sum(total, axis=0, keepdims=True)

    def adjoint(i):
        return lax.dot_general(lhs[i], panel[i], (((1,), (1,)), ((), ())), preferred_element_type=jnp.float32)

    def forward(i, x_bf, slot):
        prod = jnp.dot(
            x_bf, panel[i, :, slot * cols : (slot + 1) * cols], preferred_element_type=jnp.float32
        )
        return prod[:rows, :half] - prod[rows:, half:], prod[:rows, half:] + prod[rows:, :half]

    zero = jnp.zeros((1, 128), jnp.float32)
    gg, qq, gh, hh, qw, ww = zero, zero, zero, zero, zero, zero
    for i in range(blocks_here):
        g0 = adjoint(i)
        grad_out[i] = g0
        gg += fold(g0 * g0)
        g_bf = g0.astype(jnp.bfloat16)
        for slot in range(n_src):
            re, im = forward(i, g_bf, slot)
            qq += fold(re * re + im * im)
            image0[i, :, slot * cols : slot * cols + half] = re
            image0[i, :, slot * cols + half : (slot + 1) * cols] = im
            re_bf, im_bf = re.astype(jnp.bfloat16), im.astype(jnp.bfloat16)
            lhs[i, :rows, slot * cols : slot * cols + half] = re_bf
            lhs[i, :rows, slot * cols + half : (slot + 1) * cols] = im_bf
            lhs[i, rows:, slot * cols : slot * cols + half] = im_bf
            lhs[i, rows:, slot * cols + half : (slot + 1) * cols] = -re_bf
            image_out[where[slot], i * rows : (i + 1) * rows, :half] = re_bf
            image_out[where[slot], i * rows : (i + 1) * rows, half:] = im_bf
    for i in range(blocks_here):
        h0 = adjoint(i)
        hess_out[i] = h0
        gh += fold(h0 * grad_out[i])
        hh += fold(h0 * h0)
        h_bf = h0.astype(jnp.bfloat16)
        for slot in range(n_src):
            re, im = forward(i, h_bf, slot)
            ww += fold(re * re + im * im)
            q_re = image0[i, :, slot * cols : slot * cols + half]
            q_im = image0[i, :, slot * cols + half : (slot + 1) * cols]
            qw += fold(re * q_re + im * q_im)
            image2_out[where[slot], i * rows : (i + 1) * rows, :half] = re.astype(jnp.bfloat16)
            image2_out[where[slot], i * rows : (i + 1) * rows, half:] = im.astype(jnp.bfloat16)
    sums_out[...] = jnp.concatenate([gg, qq, gh, hh, qw, ww, zero, zero], axis=0)


def per_device(n_rcv, n_src, pplus, pminus, band):
    blocks_here = band.shape[0]
    rows = BLOCK // n_src
    cols = 2 * pplus.shape[2]
    me_rcv, me_src = lax.axis_index("rcv"), lax.axis_index("src")
    order = ring_order(n_src)
    pos = [order.index(s) for s in range(n_src)]
    ahead = [(order[p], order[(p + 1) % n_src]) for p in range(n_src)]
    behind = [(d, s) for s, d in ahead]
    up = [(r, r + 1) for r in range(n_rcv - 1)]
    down = [(r + 1, r) for r in range(n_rcv - 1)]

    own = pplus.reshape(blocks_here * BLOCK, cols)
    chunks, shifts, groups = [own], [0], [[0]]
    fwd = bwd = own
    for step in range(1, n_src // 2 + 1):
        group = []
        fwd = lax.ppermute(fwd, "src", ahead)
        group.append(len(chunks))
        chunks.append(fwd)
        shifts.append(-step)
        if len(chunks) < n_src:
            bwd = lax.ppermute(bwd, "src", behind)
            group.append(len(chunks))
            chunks.append(bwd)
            shifts.append(step)
        groups.append(group)
    left, right = [], []
    for group in groups:
        both = jnp.concatenate([chunks[c] for c in group], axis=0) if len(group) > 1 else chunks[group[0]]
        left.append(lax.ppermute(both, "rcv", up))
        right.append(lax.ppermute(both, "rcv", down))

    my_pos = jnp.asarray(pos, jnp.int32)[me_src]
    where = jnp.asarray(order, jnp.int32)[jnp.mod(my_pos + jnp.asarray(shifts, jnp.int32), n_src)]
    table = (band - (me_rcv * blocks_here - HALO_BLK)).reshape(-1)

    start = pminus.reshape(blocks_here, n_src, rows, cols)
    field = lax.all_to_all(
        jnp.transpose(start, (1, 0, 2, 3)).reshape(n_src, blocks_here * rows, cols), "src", 0, 0, tiled=True
    )

    any_spec = pl.BlockSpec(memory_space=pl.ANY)
    smem, vmem = pl.BlockSpec(memory_space=pltpu.SMEM), pl.BlockSpec(memory_space=pltpu.VMEM)
    band_cols = NEIGH * BLOCK
    need = 4 * blocks_here * band_cols * n_src * cols + (24 << 20)
    grad, hess, image, image2, sums = pl.pallas_call(
        functools.partial(maps_kernel, n_src, groups),
        out_shape=(
            jax.ShapeDtypeStruct((blocks_here, 2 * rows, band_cols), jnp.float32),
            jax.ShapeDtypeStruct((blocks_here, 2 * rows, band_cols), jnp.float32),
            jax.ShapeDtypeStruct((n_src, blocks_here * rows, cols), jnp.bfloat16),
            jax.ShapeDtypeStruct((n_src, blocks_here * rows, cols), jnp.bfloat16),
            jax.ShapeDtypeStruct((8, 128), jnp.float32),
        ),
        in_specs=[smem, smem, vmem] + [any_spec] * (n_src + 2 * len(groups)),
        out_specs=[vmem] * 5,
        scratch_shapes=[
            pltpu.VMEM((blocks_here, band_cols, n_src * cols), jnp.bfloat16),
            pltpu.VMEM((blocks_here, 2 * rows, n_src * cols), jnp.bfloat16),
            pltpu.VMEM((blocks_here, rows, n_src * cols), jnp.float32),
            pltpu.SemaphoreType.DMA((n_src,)),
        ],
        compiler_params=pltpu.CompilerParams(vmem_limit_bytes=min(need, 56 << 20)),
        name="maps",
    )(table, where, field, *chunks, *left, *right)

    image = lax.all_to_all(image, "src", 0, 0, tiled=True)
    image2 = lax.all_to_all(image2, "src", 0, 0, tiled=True)
    everyone = lax.all_to_all(
        jnp.broadcast_to(sums[None], (n_rcv * n_src,) + sums.shape), ("rcv", "src"), 0, 0, tiled=True
    )
    gg, qq, gh, hh, qw, ww = [jnp.sum(everyone[:, i]) for i in range(6)]
    step0 = gg / qq
    grad_next = gg - 2 * step0 * gh + step0 * step0 * hh
    ratio = grad_next / gg
    near = 1 + ratio
    image_sq = near * near * qq - 2 * near * step0 * qw + step0 * step0 * ww
    step1 = grad_next / image_sq
    c1 = step0 + step1 * near
    c2 = -step0 * step1

    refl = (c1 * grad + c2 * hess).reshape(blocks_here, 2, rows, NEIGH, BLOCK)
    refl = jnp.transpose(refl, (2, 0, 3, 1, 4))
    moved = c1 * image.astype(jnp.float32) + c2 * image2.astype(jnp.float32)
    moved = jnp.transpose(moved.reshape(n_src, blocks_here, rows, cols), (1, 0, 2, 3))
    misfit = pminus.astype(jnp.float32) - moved.reshape(pminus.shape)
    return refl, misfit


def solution(mesh):
    return jax.shard_map(
        functools.partial(per_device, mesh.shape["rcv"], mesh.shape["src"]),
        mesh=mesh,
        in_specs=(P("rcv", None, "src"), P("rcv", None, "src"), P("rcv", None)),
        out_specs=(P("src", "rcv", None, None, None), P("rcv", None, "src")),
        check_vma=False,
    )
```

```python
import functools

import jax
import jax.numpy as jnp
from jax import lax
from jax.experimental import pallas as pl
from jax.experimental.pallas import tpu as pltpu
from jax.sharding import PartitionSpec as P

BLOCK = 256
NEIGH = 3
HALO_BLK = 2
ROWS_X = 2


def ring_order(count):
    if count % ROWS_X or count < 2 * ROWS_X:
        return list(range(count))
    half = count // ROWS_X
    return [ROWS_X * p for p in range(half)] + [ROWS_X * p + 1 for p in reversed(range(half))]


def ring_place(count, index, shift):
    if count % ROWS_X or count < 2 * ROWS_X:
        return lax.rem(index + shift + count, count)
    half, odd = count // ROWS_X, lax.rem(index, ROWS_X)
    step = (index - odd) // ROWS_X
    place = lax.rem(jnp.where(odd == 1, count - 1 - step, step) + shift + count, count)
    return jnp.where(place < half, ROWS_X * place, ROWS_X * (count - 1 - place) + 1)


def maps_kernel(n_src, shifts, *refs):
    me, band, field = refs[:3]
    own, near, far = refs[3 : 3 + n_src], refs[3 + n_src : 3 + 2 * n_src], refs[3 + 2 * n_src : 3 + 3 * n_src]
    grad_out, hess_out, image_out, image2_out, sums_out = refs[3 + 3 * n_src : 8 + 3 * n_src]
    panel, lhs, sems = refs[8 + 3 * n_src :]
    blocks_here = panel.shape[0]
    rows = lhs.shape[1] // 2
    cols = field.shape[2]
    half = cols // 2
    me_rcv, me_src = me[0], me[1]
    odd = lax.rem(me_rcv, 2)
    where = [ring_place(n_src, me_src, shift) for shift in shifts]

    for i in range(blocks_here):
        for k in range(NEIGH):
            offset = band[i, k] - me_rcv * blocks_here
            here = (offset >= 0) & (offset < blocks_here)
            toward = jnp.where(offset < 0, 1, 0)
            inside = jnp.where(offset < 0, offset + HALO_BLK, jnp.where(here, offset, offset - blocks_here))
            start = pl.multiple_of(inside * BLOCK, BLOCK)

            def fetch(group, i=i, k=k, start=start):
                for slot in range(n_src):
                    pltpu.make_async_copy(
                        group[slot].at[pl.ds(start, BLOCK), :],
                        panel.at[i, pl.ds(k * BLOCK, BLOCK), pl.ds(slot * cols, cols)],
                        sems.at[slot],
                    ).start()

            @pl.when(here)
            def _():
                fetch(own)

            @pl.when(jnp.logical_not(here) & (toward == odd))
            def _():
                fetch(near)

            @pl.when(jnp.logical_not(here) & (toward != odd))
            def _():
                fetch(far)

    for slot in range(n_src):
        for i in range(blocks_here):
            rows_bf = field[where[slot], i * rows : (i + 1) * rows, :]
            lhs[i, :rows, slot * cols : (slot + 1) * cols] = rows_bf
            lhs[i, rows:, slot * cols : slot * cols + half] = rows_bf[:, half:]
            lhs[i, rows:, slot * cols + half : (slot + 1) * cols] = -rows_bf[:, :half]

    for slot in range(n_src):
        for i in range(blocks_here):
            for k in range(NEIGH):
                pltpu.make_async_copy(
                    own[slot].at[pl.ds(0, BLOCK), :],
                    panel.at[i, pl.ds(k * BLOCK, BLOCK), pl.ds(slot * cols, cols)],
                    sems.at[slot],
                ).wait()

    def fold(x):
        total = x[:, :128]
        for c in range(128, x.shape[1], 128):
            total = total + x[:, c : c + 128]
        return jnp.sum(total, axis=0, keepdims=True)

    def adjoint(i):
        return lax.dot_general(lhs[i], panel[i], (((1,), (1,)), ((), ())), preferred_element_type=jnp.float32)

    def forward(i, x_bf, slot):
        prod = jnp.dot(
            x_bf, panel[i, :, slot * cols : (slot + 1) * cols], preferred_element_type=jnp.float32
        )
        return prod[:rows, :half] - prod[rows:, half:], prod[:rows, half:] + prod[rows:, :half]

    zero = jnp.zeros((1, 128), jnp.float32)
    gg, qq, gh, hh, qw, ww = zero, zero, zero, zero, zero, zero
    for i in range(blocks_here):
        mine = slice(i * rows, (i + 1) * rows)
        g0 = adjoint(i)
        grad_out[i] = g0
        gg += fold(g0 * g0)
        g_bf = g0.astype(jnp.bfloat16)
        for slot in range(n_src):
            re, im = forward(i, g_bf, slot)
            qq += fold(re * re + im * im)
            image_out[where[slot], mine, :half] = re
            image_out[where[slot], mine, half:] = im
            re_bf, im_bf = re.astype(jnp.bfloat16), im.astype(jnp.bfloat16)
            lhs[i, :rows, slot * cols : slot * cols + half] = re_bf
            lhs[i, :rows, slot * cols + half : (slot + 1) * cols] = im_bf
            lhs[i, rows:, slot * cols : slot * cols + half] = im_bf
            lhs[i, rows:, slot * cols + half : (slot + 1) * cols] = -re_bf
    for i in range(blocks_here):
        mine = slice(i * rows, (i + 1) * rows)
        h0 = adjoint(i)
        hess_out[i] = h0
        gh += fold(h0 * grad_out[i])
        hh += fold(h0 * h0)
        h_bf = h0.astype(jnp.bfloat16)
        for slot in range(n_src):
            re, im = forward(i, h_bf, slot)
            ww += fold(re * re + im * im)
            qw += fold(re * image_out[where[slot], mine, :half] + im * image_out[where[slot], mine, half:])
            image2_out[where[slot], mine, :half] = re
            image2_out[where[slot], mine, half:] = im
    sums_out[...] = jnp.concatenate([gg, qq, gh, hh, qw, ww, zero, zero], axis=0)


def combine_kernel(everyone, grad, hess, image, image2, refl_out, moved_out):
    total = jnp.sum(jnp.sum(everyone[...], axis=0), axis=1, keepdims=True)
    gg, qq, gh, hh, qw, ww = [total[i : i + 1] for i in range(6)]
    step0 = gg / qq
    grad_next = gg - 2 * step0 * gh + step0 * step0 * hh
    near = 1 + grad_next / gg
    image_sq = near * near * qq - 2 * near * step0 * qw + step0 * step0 * ww
    step1 = grad_next / image_sq
    c1 = step0 + step1 * near
    c2 = -step0 * step1
    for i in range(grad.shape[0]):
        refl_out[i] = c1 * grad[i] + c2 * hess[i]
    for s in range(image.shape[0]):
        moved_out[s] = (c1 * image[s] + c2 * image2[s]).astype(jnp.bfloat16)


def per_device(n_rcv, n_src, pplus, pminus, band):
    blocks_here = band.shape[0]
    rows = BLOCK // n_src
    cols = 2 * pplus.shape[2]
    order = ring_order(n_src)
    ahead = [(order[p], order[(p + 1) % n_src]) for p in range(n_src)]
    behind = [(d, s) for s, d in ahead]

    def swaps(first):
        pairs = [(r, r + 1) for r in range(first, n_rcv - 1, 2)]
        return pairs + [(d, s) for s, d in pairs]

    own = pplus.reshape(blocks_here * BLOCK, cols)
    chunks, shifts = [own], [0]
    fwd = bwd = own
    for step in range(1, n_src // 2 + 1):
        fwd = lax.ppermute(fwd, "src", ahead)
        chunks.append(fwd)
        shifts.append(-step)
        if len(chunks) < n_src:
            bwd = lax.ppermute(bwd, "src", behind)
            chunks.append(bwd)
            shifts.append(step)
    near = [lax.ppermute(c, "rcv", swaps(0)) for c in chunks]
    far = [lax.ppermute(c, "rcv", swaps(1)) for c in chunks]

    me = jnp.stack([lax.axis_index("rcv"), lax.axis_index("src")]).astype(jnp.int32)
    start = lax.optimization_barrier(pminus.reshape(blocks_here * BLOCK, cols))
    start = jnp.transpose(start.reshape(blocks_here, n_src, rows, cols), (1, 0, 2, 3))
    field = lax.all_to_all(start.reshape(n_src, blocks_here * rows, cols), "src", 0, 0, tiled=True)

    any_spec = pl.BlockSpec(memory_space=pl.ANY)
    smem, vmem = pl.BlockSpec(memory_space=pltpu.SMEM), pl.BlockSpec(memory_space=pltpu.VMEM)
    band_cols = NEIGH * BLOCK
    need = 2 * blocks_here * band_cols * n_src * cols + (24 << 20)
    grad, hess, image, image2, sums = pl.pallas_call(
        functools.partial(maps_kernel, n_src, shifts),
        out_shape=(
            jax.ShapeDtypeStruct((blocks_here, 2 * rows, band_cols), jnp.float32),
            jax.ShapeDtypeStruct((blocks_here, 2 * rows, band_cols), jnp.float32),
            jax.ShapeDtypeStruct((n_src, blocks_here * rows, cols), jnp.float32),
            jax.ShapeDtypeStruct((n_src, blocks_here * rows, cols), jnp.float32),
            jax.ShapeDtypeStruct((8, 128), jnp.float32),
        ),
        in_specs=[smem, smem, vmem] + [any_spec] * (3 * n_src),
        out_specs=[vmem] * 5,
        scratch_shapes=[
            pltpu.VMEM((blocks_here, band_cols, n_src * cols), jnp.bfloat16),
            pltpu.VMEM((blocks_here, 2 * rows, n_src * cols), jnp.bfloat16),
            pltpu.SemaphoreType.DMA((n_src,)),
        ],
        compiler_params=pltpu.CompilerParams(vmem_limit_bytes=min(need, 56 << 20)),
        name="maps",
    )(me, band, field, *chunks, *near, *far)

    everyone = lax.all_to_all(
        jnp.broadcast_to(sums[None], (n_rcv * n_src,) + sums.shape), ("rcv", "src"), 0, 0, tiled=True
    )
    refl, moved = pl.pallas_call(
        combine_kernel,
        out_shape=(
            jax.ShapeDtypeStruct(grad.shape, jnp.float32),
            jax.ShapeDtypeStruct(image.shape, jnp.bfloat16),
        ),
        in_specs=[vmem] * 5,
        out_specs=[vmem] * 2,
        compiler_params=pltpu.CompilerParams(vmem_limit_bytes=32 << 20),
        name="combine",
    )(everyone, grad, hess, image, image2)
    moved = lax.all_to_all(moved, "src", 0, 0, tiled=True)

    refl = jnp.transpose(refl.reshape(blocks_here, 2, rows, NEIGH, BLOCK), (2, 0, 3, 1, 4))
    moved = jnp.transpose(moved.reshape(n_src, blocks_here, rows, cols), (1, 0, 2, 3)).astype(jnp.float32)
    misfit = pminus.astype(jnp.float32) - moved.reshape(pminus.shape)
    return refl, misfit


def solution(mesh):
    return jax.shard_map(
        functools.partial(per_device, mesh.shape["rcv"], mesh.shape["src"]),
        mesh=mesh,
        in_specs=(P("rcv", None, "src"), P("rcv", None, "src"), P("rcv", None)),
        out_specs=(P("src", "rcv", None, None, None), P("rcv", None, "src")),
        check_vma=False,
    )
```

```python
import functools

import jax
import jax.numpy as jnp
from jax import lax
from jax.experimental import pallas as pl
from jax.experimental.pallas import tpu as pltpu
from jax.sharding import PartitionSpec as P

BLOCK = 256
NEIGH = 3
HALO_BLK = 2
ROWS_X = 2


def ring_order(count):
    if count % ROWS_X or count < 2 * ROWS_X:
        return list(range(count))
    half = count // ROWS_X
    return [ROWS_X * p for p in range(half)] + [ROWS_X * p + 1 for p in reversed(range(half))]


def ring_place(count, index, shift):
    if count % ROWS_X or count < 2 * ROWS_X:
        return lax.rem(index + shift + count, count)
    half, odd = count // ROWS_X, lax.rem(index, ROWS_X)
    step = (index - odd) // ROWS_X
    place = lax.rem(jnp.where(odd == 1, count - 1 - step, step) + shift + count, count)
    return jnp.where(place < half, ROWS_X * place, ROWS_X * (count - 1 - place) + 1)


def join_kernel(*refs):
    parts, out, sems = refs[:-2], refs[-2], refs[-1]
    size = parts[0].shape[0]
    copies = [
        pltpu.make_async_copy(part, out.at[pl.ds(i * size, size), :], sems.at[i]) for i, part in enumerate(parts)
    ]
    for copy in copies:
        copy.start()
    for copy in copies:
        copy.wait()


def join(parts):
    if len(parts) == 1:
        return parts[0]
    rows, cols = parts[0].shape
    return pl.pallas_call(
        join_kernel,
        out_shape=jax.ShapeDtypeStruct((len(parts) * rows, cols), parts[0].dtype),
        in_specs=[pl.BlockSpec(memory_space=pl.ANY)] * len(parts),
        out_specs=pl.BlockSpec(memory_space=pl.ANY),
        scratch_shapes=[pltpu.SemaphoreType.DMA((len(parts),))],
        name="join",
    )(*parts)


def maps_kernel(n_src, shifts, batches, *refs):
    me, band, field = refs[:3]
    n_bat = len(batches)
    own, near, far = refs[3 : 3 + n_src], refs[3 + n_src : 3 + n_src + n_bat], refs[3 + n_src + n_bat : 3 + n_src + 2 * n_bat]
    grad_out, hess_out, image_out, image2_out, sums_out = refs[3 + n_src + 2 * n_bat : 8 + n_src + 2 * n_bat]
    panel, lhs, sems = refs[8 + n_src + 2 * n_bat :]
    blocks_here = panel.shape[0]
    rows = lhs.shape[1] // 2
    cols = field.shape[2]
    half = cols // 2
    me_rcv, me_src = me[0], me[1]
    odd = lax.rem(me_rcv, 2)
    where = [ring_place(n_src, me_src, shift) for shift in shifts]

    for i in range(blocks_here):
        for k in range(NEIGH):
            offset = band[i, k] - me_rcv * blocks_here
            here = (offset >= 0) & (offset < blocks_here)
            toward = jnp.where(offset < 0, 1, 0)
            inside = jnp.where(offset < 0, offset + HALO_BLK, jnp.where(here, offset, offset - blocks_here))
            start = pl.multiple_of(inside * BLOCK, BLOCK)

            def fetch(arrays, groups, i=i, k=k, start=start):
                for array, group in zip(arrays, groups):
                    for place, slot in enumerate(group):
                        pltpu.make_async_copy(
                            array.at[pl.ds(start + place * blocks_here * BLOCK, BLOCK), :],
                            panel.at[i, pl.ds(k * BLOCK, BLOCK), pl.ds(slot * cols, cols)],
                            sems.at[slot],
                        ).start()

            @pl.when(here)
            def _():
                fetch(own, [[slot] for slot in range(n_src)])

            @pl.when(jnp.logical_not(here) & (toward == odd))
            def _():
                fetch(near, batches)

            @pl.when(jnp.logical_not(here) & (toward != odd))
            def _():
                fetch(far, batches)

    for slot in range(n_src):
        for i in range(blocks_here):
            rows_bf = field[where[slot], i * rows : (i + 1) * rows, :]
            lhs[i, :rows, slot * cols : (slot + 1) * cols] = rows_bf
            lhs[i, rows:, slot * cols : slot * cols + half] = rows_bf[:, half:]
            lhs[i, rows:, slot * cols + half : (slot + 1) * cols] = -rows_bf[:, :half]

    for slot in range(n_src):
        for i in range(blocks_here):
            for k in range(NEIGH):
                pltpu.make_async_copy(
                    own[slot].at[pl.ds(0, BLOCK), :],
                    panel.at[i, pl.ds(k * BLOCK, BLOCK), pl.ds(slot * cols, cols)],
                    sems.at[slot],
                ).wait()

    def fold(x):
        total = x[:, :128]
        for c in range(128, x.shape[1], 128):
            total = total + x[:, c : c + 128]
        return jnp.sum(total, axis=0, keepdims=True)

    def adjoint(i):
        return lax.dot_general(lhs[i], panel[i], (((1,), (1,)), ((), ())), preferred_element_type=jnp.float32)

    def forward(i, x_bf, slot):
        prod = jnp.dot(
            x_bf, panel[i, :, slot * cols : (slot + 1) * cols], preferred_element_type=jnp.float32
        )
        return prod[:rows, :half] - prod[rows:, half:], prod[:rows, half:] + prod[rows:, :half]

    zero = jnp.zeros((1, 128), jnp.float32)
    gg, qq, gh, hh, qw, ww = zero, zero, zero, zero, zero, zero
    for i in range(blocks_here):
        mine = slice(i * rows, (i + 1) * rows)
        g0 = adjoint(i)
        grad_out[i] = g0
        gg += fold(g0 * g0)
        g_bf = g0.astype(jnp.bfloat16)
        for slot in range(n_src):
            re, im = forward(i, g_bf, slot)
            qq += fold(re * re + im * im)
            image_out[where[slot], mine, :half] = re
            image_out[where[slot], mine, half:] = im
            re_bf, im_bf = re.astype(jnp.bfloat16), im.astype(jnp.bfloat16)
            lhs[i, :rows, slot * cols : slot * cols + half] = re_bf
            lhs[i, :rows, slot * cols + half : (slot + 1) * cols] = im_bf
            lhs[i, rows:, slot * cols : slot * cols + half] = im_bf
            lhs[i, rows:, slot * cols + half : (slot + 1) * cols] = -re_bf
    for i in range(blocks_here):
        mine = slice(i * rows, (i + 1) * rows)
        h0 = adjoint(i)
        hess_out[i] = h0
        gh += fold(h0 * grad_out[i])
        hh += fold(h0 * h0)
        h_bf = h0.astype(jnp.bfloat16)
        for slot in range(n_src):
            re, im = forward(i, h_bf, slot)
            ww += fold(re * re + im * im)
            qw += fold(re * image_out[where[slot], mine, :half] + im * image_out[where[slot], mine, half:])
            image2_out[where[slot], mine, :half] = re
            image2_out[where[slot], mine, half:] = im
    sums_out[...] = jnp.concatenate([gg, qq, gh, hh, qw, ww, zero, zero], axis=0)


def combine_kernel(everyone, image, image2, steps_out, moved_out):
    total = jnp.sum(jnp.sum(everyone[...], axis=0), axis=1, keepdims=True)
    gg, qq, gh, hh, qw, ww = [total[i : i + 1] for i in range(6)]
    step0 = gg / qq
    grad_next = gg - 2 * step0 * gh + step0 * step0 * hh
    near = 1 + grad_next / gg
    image_sq = near * near * qq - 2 * near * step0 * qw + step0 * step0 * ww
    step1 = grad_next / image_sq
    c1 = step0 + step1 * near
    c2 = -step0 * step1
    steps_out[0:1] = jnp.broadcast_to(c1, (1, 128))
    steps_out[1:2] = jnp.broadcast_to(c2, (1, 128))
    for s in range(image.shape[0]):
        moved_out[s] = (c1 * image[s] + c2 * image2[s]).astype(jnp.bfloat16)


def per_device(n_rcv, n_src, pplus, pminus, band):
    blocks_here = band.shape[0]
    rows = BLOCK // n_src
    cols = 2 * pplus.shape[2]
    order = ring_order(n_src)
    ahead = [(order[p], order[(p + 1) % n_src]) for p in range(n_src)]
    behind = [(d, s) for s, d in ahead]

    def swaps(first):
        pairs = [(r, r + 1) for r in range(first, n_rcv - 1, 2)]
        return pairs + [(d, s) for s, d in pairs]

    own = pplus.reshape(blocks_here * BLOCK, cols)
    chunks, shifts = [own], [0]
    fwd = bwd = own
    for step in range(1, n_src // 2 + 1):
        fwd = lax.ppermute(fwd, "src", ahead)
        chunks.append(fwd)
        shifts.append(-step)
        if len(chunks) < n_src:
            bwd = lax.ppermute(bwd, "src", behind)
            chunks.append(bwd)
            shifts.append(step)
    batches = [list(range(min(3, n_src)))] + [list(range(c, min(c + 2, n_src))) for c in range(3, n_src, 2)]

    me = jnp.stack([lax.axis_index("rcv"), lax.axis_index("src")]).astype(jnp.int32)
    start = lax.optimization_barrier(pminus.reshape(blocks_here * BLOCK, cols))
    start = jnp.transpose(start.reshape(blocks_here, n_src, rows, cols), (1, 0, 2, 3))
    field = lax.all_to_all(start.reshape(n_src, blocks_here * rows, cols), "src", 0, 0, tiled=True)

    joined = [join([chunks[c] for c in batch]) for batch in batches]
    joined[0], field = lax.optimization_barrier((joined[0], field))
    near = [lax.ppermute(c, "rcv", swaps(0)) for c in joined]
    far = [lax.ppermute(c, "rcv", swaps(1)) for c in joined]

    any_spec = pl.BlockSpec(memory_space=pl.ANY)
    smem, vmem = pl.BlockSpec(memory_space=pltpu.SMEM), pl.BlockSpec(memory_space=pltpu.VMEM)
    band_cols = NEIGH * BLOCK
    need = 2 * blocks_here * band_cols * n_src * cols + (24 << 20)
    grad, hess, image, image2, sums = pl.pallas_call(
        functools.partial(maps_kernel, n_src, shifts, batches),
        out_shape=(
            jax.ShapeDtypeStruct((blocks_here, 2 * rows, band_cols), jnp.float32),
            jax.ShapeDtypeStruct((blocks_here, 2 * rows, band_cols), jnp.float32),
            jax.ShapeDtypeStruct((n_src, blocks_here * rows, cols), jnp.float32),
            jax.ShapeDtypeStruct((n_src, blocks_here * rows, cols), jnp.float32),
            jax.ShapeDtypeStruct((8, 128), jnp.float32),
        ),
        in_specs=[smem, smem, vmem] + [any_spec] * (n_src + 2 * len(batches)),
        out_specs=[vmem] * 5,
        scratch_shapes=[
            pltpu.VMEM((blocks_here, band_cols, n_src * cols), jnp.bfloat16),
            pltpu.VMEM((blocks_here, 2 * rows, n_src * cols), jnp.bfloat16),
            pltpu.SemaphoreType.DMA((n_src,)),
        ],
        compiler_params=pltpu.CompilerParams(vmem_limit_bytes=min(need, 56 << 20)),
        name="maps",
    )(me, band, field, *chunks, *near, *far)

    everyone = lax.all_to_all(
        jnp.broadcast_to(sums[None], (n_rcv * n_src,) + sums.shape), ("rcv", "src"), 0, 0, tiled=True
    )
    steps, moved = pl.pallas_call(
        combine_kernel,
        out_shape=(
            jax.ShapeDtypeStruct((2, 128), jnp.float32),
            jax.ShapeDtypeStruct(image.shape, jnp.bfloat16),
        ),
        in_specs=[vmem] * 3,
        out_specs=[vmem] * 2,
        compiler_params=pltpu.CompilerParams(vmem_limit_bytes=32 << 20),
        name="combine",
    )(everyone, image, image2)
    moved = lax.all_to_all(moved, "src", 0, 0, tiled=True)

    def in_place(x):
        return jnp.transpose(x.reshape(blocks_here, 2, rows, NEIGH, BLOCK), (2, 0, 3, 1, 4))

    grad, hess = lax.optimization_barrier((in_place(grad), in_place(hess)))
    refl = steps[0, 0] * grad + steps[1, 0] * hess
    moved = jnp.transpose(moved.reshape(n_src, blocks_here, rows, cols), (1, 0, 2, 3)).astype(jnp.float32)
    misfit = pminus.astype(jnp.float32) - moved.reshape(pminus.shape)
    return refl, misfit


def solution(mesh):
    return jax.shard_map(
        functools.partial(per_device, mesh.shape["rcv"], mesh.shape["src"]),
        mesh=mesh,
        in_specs=(P("rcv", None, "src"), P("rcv", None, "src"), P("rcv", None)),
        out_specs=(P("src", "rcv", None, None, None), P("rcv", None, "src")),
        check_vma=False,
    )
```

```python
import functools

import jax
import jax.numpy as jnp
from jax import lax
from jax.experimental import pallas as pl
from jax.experimental.pallas import tpu as pltpu
from jax.sharding import PartitionSpec as P

BLOCK = 256
NEIGH = 3
HALO_BLK = 2
ROWS_X = 2


def ring_order(count):
    if count % ROWS_X or count < 2 * ROWS_X:
        return list(range(count))
    half = count // ROWS_X
    return [ROWS_X * p for p in range(half)] + [ROWS_X * p + 1 for p in reversed(range(half))]


def ring_place(count, index, shift):
    if count % ROWS_X or count < 2 * ROWS_X:
        return lax.rem(index + shift + count, count)
    half, odd = count // ROWS_X, lax.rem(index, ROWS_X)
    step = (index - odd) // ROWS_X
    place = lax.rem(jnp.where(odd == 1, count - 1 - step, step) + shift + count, count)
    return jnp.where(place < half, ROWS_X * place, ROWS_X * (count - 1 - place) + 1)


def join_kernel(*refs):
    size = refs[0].shape[0]
    for i, part in enumerate(refs[:-1]):
        refs[-1][i * size : (i + 1) * size, :] = part[...]


def join(parts):
    if len(parts) == 1:
        return parts[0]
    rows, cols = parts[0].shape
    return pl.pallas_call(
        join_kernel,
        out_shape=jax.ShapeDtypeStruct((len(parts) * rows, cols), parts[0].dtype),
        in_specs=[pl.BlockSpec(memory_space=pltpu.VMEM)] * len(parts),
        out_specs=pl.BlockSpec(memory_space=pltpu.VMEM),
        name="join",
    )(*parts)


def maps_kernel(n_src, shifts, batches, *refs):
    me, band, field = refs[:3]
    n_bat = len(batches)
    own, near, far = refs[3 : 3 + n_src], refs[3 + n_src : 3 + n_src + n_bat], refs[3 + n_src + n_bat : 3 + n_src + 2 * n_bat]
    grad_out, hess_out, image_out, image2_out, sums_out = refs[3 + n_src + 2 * n_bat : 8 + n_src + 2 * n_bat]
    panel, lhs, sems = refs[8 + n_src + 2 * n_bat :]
    blocks_here = panel.shape[0]
    rows = lhs.shape[1] // 2
    cols = field.shape[2]
    half = cols // 2
    me_rcv, me_src = me[0], me[1]
    odd = lax.rem(me_rcv, 2)
    where = [ring_place(n_src, me_src, shift) for shift in shifts]

    for i in range(blocks_here):
        for k in range(NEIGH):
            offset = band[i, k] - me_rcv * blocks_here
            here = (offset >= 0) & (offset < blocks_here)
            toward = jnp.where(offset < 0, 1, 0)
            inside = jnp.where(offset < 0, offset + HALO_BLK, jnp.where(here, offset, offset - blocks_here))
            start = pl.multiple_of(inside * BLOCK, BLOCK)

            def fetch(arrays, groups, i=i, k=k, start=start):
                for array, group in zip(arrays, groups):
                    for place, slot in enumerate(group):
                        pltpu.make_async_copy(
                            array.at[pl.ds(start + place * blocks_here * BLOCK, BLOCK), :],
                            panel.at[i, pl.ds(k * BLOCK, BLOCK), pl.ds(slot * cols, cols)],
                            sems.at[slot],
                        ).start()

            @pl.when(here)
            def _():
                fetch(own, [[slot] for slot in range(n_src)])

            @pl.when(jnp.logical_not(here) & (toward == odd))
            def _():
                fetch(near, batches)

            @pl.when(jnp.logical_not(here) & (toward != odd))
            def _():
                fetch(far, batches)

    for slot in range(n_src):
        for i in range(blocks_here):
            rows_bf = field[where[slot], i * rows : (i + 1) * rows, :]
            lhs[i, :rows, slot * cols : (slot + 1) * cols] = rows_bf
            lhs[i, rows:, slot * cols : slot * cols + half] = rows_bf[:, half:]
            lhs[i, rows:, slot * cols + half : (slot + 1) * cols] = -rows_bf[:, :half]

    for slot in range(n_src):
        for i in range(blocks_here):
            for k in range(NEIGH):
                pltpu.make_async_copy(
                    own[slot].at[pl.ds(0, BLOCK), :],
                    panel.at[i, pl.ds(k * BLOCK, BLOCK), pl.ds(slot * cols, cols)],
                    sems.at[slot],
                ).wait()

    def fold(x):
        total = x[:, :128]
        for c in range(128, x.shape[1], 128):
            total = total + x[:, c : c + 128]
        return jnp.sum(total, axis=0, keepdims=True)

    def adjoint(i):
        return lax.dot_general(lhs[i], panel[i], (((1,), (1,)), ((), ())), preferred_element_type=jnp.float32)

    def forward(i, x_bf, slot):
        prod = jnp.dot(
            x_bf, panel[i, :, slot * cols : (slot + 1) * cols], preferred_element_type=jnp.float32
        )
        return prod[:rows, :half] - prod[rows:, half:], prod[:rows, half:] + prod[rows:, :half]

    zero = jnp.zeros((1, 128), jnp.float32)
    gg, qq, gh, hh, qw, ww = zero, zero, zero, zero, zero, zero
    for i in range(blocks_here):
        mine = slice(i * rows, (i + 1) * rows)
        g0 = adjoint(i)
        grad_out[i] = g0
        gg += fold(g0 * g0)
        g_bf = g0.astype(jnp.bfloat16)
        for slot in range(n_src):
            re, im = forward(i, g_bf, slot)
            qq += fold(re * re + im * im)
            image_out[where[slot], mine, :half] = re
            image_out[where[slot], mine, half:] = im
            re_bf, im_bf = re.astype(jnp.bfloat16), im.astype(jnp.bfloat16)
            lhs[i, :rows, slot * cols : slot * cols + half] = re_bf
            lhs[i, :rows, slot * cols + half : (slot + 1) * cols] = im_bf
            lhs[i, rows:, slot * cols : slot * cols + half] = im_bf
            lhs[i, rows:, slot * cols + half : (slot + 1) * cols] = -re_bf
    for i in range(blocks_here):
        mine = slice(i * rows, (i + 1) * rows)
        h0 = adjoint(i)
        hess_out[i] = h0
        gh += fold(h0 * grad_out[i])
        hh += fold(h0 * h0)
        h_bf = h0.astype(jnp.bfloat16)
        for slot in range(n_src):
            re, im = forward(i, h_bf, slot)
            ww += fold(re * re + im * im)
            qw += fold(re * image_out[where[slot], mine, :half] + im * image_out[where[slot], mine, half:])
            image2_out[where[slot], mine, :half] = re
            image2_out[where[slot], mine, half:] = im
    sums_out[...] = jnp.concatenate([gg, qq, gh, hh, qw, ww, zero, zero], axis=0)


def combine_kernel(everyone, image, image2, grad, hess, steps_out, moved_out):
    total = jnp.sum(jnp.sum(everyone[...], axis=0), axis=1, keepdims=True)
    gg, qq, gh, hh, qw, ww = [total[i : i + 1] for i in range(6)]
    step0 = gg / qq
    grad_next = gg - 2 * step0 * gh + step0 * step0 * hh
    near = 1 + grad_next / gg
    image_sq = near * near * qq - 2 * near * step0 * qw + step0 * step0 * ww
    step1 = grad_next / image_sq
    c1 = step0 + step1 * near
    c2 = -step0 * step1
    steps_out[0:1] = jnp.broadcast_to(c1, (1, 128))
    steps_out[1:2] = jnp.broadcast_to(c2, (1, 128))
    for s in range(image.shape[0]):
        moved_out[s] = (c1 * image[s] + c2 * image2[s]).astype(jnp.bfloat16)


def per_device(n_rcv, n_src, pplus, pminus, band):
    blocks_here = band.shape[0]
    rows = BLOCK // n_src
    cols = 2 * pplus.shape[2]
    order = ring_order(n_src)
    ahead = [(order[p], order[(p + 1) % n_src]) for p in range(n_src)]
    behind = [(d, s) for s, d in ahead]

    def swaps(first):
        pairs = [(r, r + 1) for r in range(first, n_rcv - 1, 2)]
        return pairs + [(d, s) for s, d in pairs]

    own = pplus.reshape(blocks_here * BLOCK, cols)
    chunks, shifts = [own], [0]
    fwd = bwd = own
    for step in range(1, n_src // 2 + 1):
        fwd = lax.ppermute(fwd, "src", ahead)
        chunks.append(fwd)
        shifts.append(-step)
        if len(chunks) < n_src:
            bwd = lax.ppermute(bwd, "src", behind)
            chunks.append(bwd)
            shifts.append(step)
    batches = [list(range(min(3, n_src)))] + [list(range(c, min(c + 2, n_src))) for c in range(3, n_src, 2)]

    me = jnp.stack([lax.axis_index("rcv"), lax.axis_index("src")]).astype(jnp.int32)
    start = lax.optimization_barrier(pminus.reshape(blocks_here * BLOCK, cols))
    start = jnp.transpose(start.reshape(blocks_here, n_src, rows, cols), (1, 0, 2, 3))
    field = lax.all_to_all(start.reshape(n_src, blocks_here * rows, cols), "src", 0, 0, tiled=True)

    joined = [join([chunks[c] for c in batch]) for batch in batches]
    joined[0], field = lax.optimization_barrier((joined[0], field))
    near = [lax.ppermute(c, "rcv", swaps(0)) for c in joined]
    far = [lax.ppermute(c, "rcv", swaps(1)) for c in joined]

    any_spec = pl.BlockSpec(memory_space=pl.ANY)
    smem, vmem = pl.BlockSpec(memory_space=pltpu.SMEM), pl.BlockSpec(memory_space=pltpu.VMEM)
    band_cols = NEIGH * BLOCK
    need = 2 * blocks_here * band_cols * n_src * cols + (12 << 20)
    grad, hess, image, image2, sums = pl.pallas_call(
        functools.partial(maps_kernel, n_src, shifts, batches),
        out_shape=(
            jax.ShapeDtypeStruct((blocks_here, 2 * rows, band_cols), jnp.float32),
            jax.ShapeDtypeStruct((blocks_here, 2 * rows, band_cols), jnp.float32),
            jax.ShapeDtypeStruct((n_src, blocks_here * rows, cols), jnp.float32),
            jax.ShapeDtypeStruct((n_src, blocks_here * rows, cols), jnp.float32),
            jax.ShapeDtypeStruct((8, 128), jnp.float32),
        ),
        in_specs=[smem, smem, vmem] + [any_spec] * (n_src + 2 * len(batches)),
        out_specs=[vmem] * 5,
        scratch_shapes=[
            pltpu.VMEM((blocks_here, band_cols, n_src * cols), jnp.bfloat16),
            pltpu.VMEM((blocks_here, 2 * rows, n_src * cols), jnp.bfloat16),
            pltpu.SemaphoreType.DMA((n_src,)),
        ],
        compiler_params=pltpu.CompilerParams(vmem_limit_bytes=min(need, 56 << 20)),
        name="maps",
    )(me, band, field, *chunks, *near, *far)

    everyone = lax.all_to_all(
        jnp.broadcast_to(sums[None], (n_rcv * n_src,) + sums.shape), ("rcv", "src"), 0, 0, tiled=True
    )
    def in_place(x):
        return jnp.transpose(x.reshape(blocks_here, 2, rows, NEIGH, BLOCK), (2, 0, 3, 1, 4))

    grad, hess = in_place(grad), in_place(hess)
    steps, moved = pl.pallas_call(
        combine_kernel,
        out_shape=(
            jax.ShapeDtypeStruct((2, 128), jnp.float32),
            jax.ShapeDtypeStruct(image.shape, jnp.bfloat16),
        ),
        in_specs=[vmem] * 3 + [any_spec] * 2,
        out_specs=[vmem] * 2,
        compiler_params=pltpu.CompilerParams(vmem_limit_bytes=16 << 20),
        name="combine",
    )(everyone, image, image2, grad, hess)
    moved = lax.all_to_all(moved, "src", 0, 0, tiled=True)
    refl = steps[0, 0] * grad + steps[1, 0] * hess
    moved = jnp.transpose(moved.reshape(n_src, blocks_here, rows, cols), (1, 0, 2, 3)).astype(jnp.float32)
    misfit = pminus.astype(jnp.float32) - moved.reshape(pminus.shape)
    return refl, misfit


def solution(mesh):
    return jax.shard_map(
        functools.partial(per_device, mesh.shape["rcv"], mesh.shape["src"]),
        mesh=mesh,
        in_specs=(P("rcv", None, "src"), P("rcv", None, "src"), P("rcv", None)),
        out_specs=(P("src", "rcv", None, None, None), P("rcv", None, "src")),
        check_vma=False,
    )
```

```python
import functools

import jax
import jax.numpy as jnp
from jax import lax
from jax.experimental import pallas as pl
from jax.experimental.pallas import tpu as pltpu
from jax.sharding import PartitionSpec as P

BLOCK = 256
NEIGH = 3
HALO_BLK = 2
ROWS_X = 2


def ring_order(count):
    if count % ROWS_X or count < 2 * ROWS_X:
        return list(range(count))
    half = count // ROWS_X
    return [ROWS_X * p for p in range(half)] + [ROWS_X * p + 1 for p in reversed(range(half))]


def ring_place(count, index, shift):
    if count % ROWS_X or count < 2 * ROWS_X:
        return lax.rem(index + shift + count, count)
    half, odd = count // ROWS_X, lax.rem(index, ROWS_X)
    step = (index - odd) // ROWS_X
    place = lax.rem(jnp.where(odd == 1, count - 1 - step, step) + shift + count, count)
    return jnp.where(place < half, ROWS_X * place, ROWS_X * (count - 1 - place) + 1)


def along(sums):
    total = jnp.sum(sums, axis=1, keepdims=True)
    qq, qw = total[1:2], total[4:5]
    return jnp.where(qq > 0, qw / jnp.where(qq > 0, qq, 1.0), 0.0)


def maps_kernel(n_src, shifts, *refs):
    me, band, field = refs[:3]
    own, near, far = refs[3 : 3 + n_src], refs[3 + n_src : 3 + 2 * n_src], refs[3 + 2 * n_src : 3 + 3 * n_src]
    grad_out, hess_out, images_out, sums_out = refs[3 + 3 * n_src : 7 + 3 * n_src]
    panel, lhs, image0, image1, sems = refs[7 + 3 * n_src :]
    blocks_here = panel.shape[0]
    rows = lhs.shape[1] // 2
    cols = field.shape[2]
    half = cols // 2
    me_rcv, me_src = me[0], me[1]
    odd = lax.rem(me_rcv, 2)
    where = [ring_place(n_src, me_src, shift) for shift in shifts]

    for i in range(blocks_here):
        for k in range(NEIGH):
            offset = band[i, k] - me_rcv * blocks_here
            here = (offset >= 0) & (offset < blocks_here)
            toward = jnp.where(offset < 0, 1, 0)
            inside = jnp.where(offset < 0, offset + HALO_BLK, jnp.where(here, offset, offset - blocks_here))
            start = pl.multiple_of(inside * BLOCK, BLOCK)

            def fetch(group, i=i, k=k, start=start):
                for slot in range(n_src):
                    pltpu.make_async_copy(
                        group[slot].at[pl.ds(start, BLOCK), :],
                        panel.at[i, pl.ds(k * BLOCK, BLOCK), pl.ds(slot * cols, cols)],
                        sems.at[slot],
                    ).start()

            @pl.when(here)
            def _():
                fetch(own)

            @pl.when(jnp.logical_not(here) & (toward == odd))
            def _():
                fetch(near)

            @pl.when(jnp.logical_not(here) & (toward != odd))
            def _():
                fetch(far)

    for slot in range(n_src):
        for i in range(blocks_here):
            rows_bf = field[where[slot], i * rows : (i + 1) * rows, :]
            lhs[i, :rows, slot * cols : (slot + 1) * cols] = rows_bf
            lhs[i, rows:, slot * cols : slot * cols + half] = rows_bf[:, half:]
            lhs[i, rows:, slot * cols + half : (slot + 1) * cols] = -rows_bf[:, :half]

    for slot in range(n_src):
        for i in range(blocks_here):
            for k in range(NEIGH):
                pltpu.make_async_copy(
                    own[slot].at[pl.ds(0, BLOCK), :],
                    panel.at[i, pl.ds(k * BLOCK, BLOCK), pl.ds(slot * cols, cols)],
                    sems.at[slot],
                ).wait()

    def fold(x):
        total = x[:, :128]
        for c in range(128, x.shape[1], 128):
            total = total + x[:, c : c + 128]
        return jnp.sum(total, axis=0, keepdims=True)

    def adjoint(i):
        return lax.dot_general(lhs[i], panel[i], (((1,), (1,)), ((), ())), preferred_element_type=jnp.float32)

    def forward(i, x_bf, slot):
        prod = jnp.dot(
            x_bf, panel[i, :, slot * cols : (slot + 1) * cols], preferred_element_type=jnp.float32
        )
        return prod[:rows, :half] - prod[rows:, half:], prod[:rows, half:] + prod[rows:, :half]

    zero = jnp.zeros((1, 128), jnp.float32)
    gg, qq, gh, hh, qw, ww = zero, zero, zero, zero, zero, zero
    for i in range(blocks_here):
        mine = slice(i * rows, (i + 1) * rows)
        g0 = adjoint(i)
        grad_out[i] = g0
        gg += fold(g0 * g0)
        g_bf = g0.astype(jnp.bfloat16)
        for slot in range(n_src):
            re, im = forward(i, g_bf, slot)
            qq += fold(re * re + im * im)
            image0[slot, mine, :half] = re
            image0[slot, mine, half:] = im
            re_bf, im_bf = re.astype(jnp.bfloat16), im.astype(jnp.bfloat16)
            lhs[i, :rows, slot * cols : slot * cols + half] = re_bf
            lhs[i, :rows, slot * cols + half : (slot + 1) * cols] = im_bf
            lhs[i, rows:, slot * cols : slot * cols + half] = im_bf
            lhs[i, rows:, slot * cols + half : (slot + 1) * cols] = -re_bf
    for i in range(blocks_here):
        mine = slice(i * rows, (i + 1) * rows)
        h0 = adjoint(i)
        hess_out[i] = h0
        gh += fold(h0 * grad_out[i])
        hh += fold(h0 * h0)
        h_bf = h0.astype(jnp.bfloat16)
        for slot in range(n_src):
            re, im = forward(i, h_bf, slot)
            ww += fold(re * re + im * im)
            qw += fold(re * image0[slot, mine, :half] + im * image0[slot, mine, half:])
            image1[slot, mine, :half] = re
            image1[slot, mine, half:] = im
    sums = jnp.concatenate([gg, qq, gh, hh, qw, ww, zero, zero], axis=0)
    sums_out[...] = sums
    share = along(sums)
    height = blocks_here * rows
    for slot in range(n_src):
        first = image0[slot]
        images_out[where[slot], :height] = first.astype(jnp.bfloat16)
        images_out[where[slot], height:] = (image1[slot] - share * first).astype(jnp.bfloat16)


def combine_kernel(me, everyone, images, grad, hess, refl_out, moved_out):
    n_src, height = images.shape[0], images.shape[1] // 2
    total = jnp.sum(jnp.sum(everyone[...], axis=0), axis=1, keepdims=True)
    gg, qq, gh, hh, qw, ww = [total[i : i + 1] for i in range(6)]
    step0 = gg / qq
    grad_next = gg - 2 * step0 * gh + step0 * step0 * hh
    near = 1 + grad_next / gg
    image_sq = near * near * qq - 2 * near * step0 * qw + step0 * step0 * ww
    step1 = grad_next / image_sq
    c1 = step0 + step1 * near
    c2 = -step0 * step1
    for i in range(grad.shape[0]):
        refl_out[i] = c1 * grad[i] + c2 * hess[i]
    for s in range(n_src):
        share = along(everyone[me[0] * n_src + s])
        first = images[s, :height].astype(jnp.float32)
        rest = images[s, height:].astype(jnp.float32)
        moved_out[s] = (c1 + c2 * share) * first + c2 * rest


def per_device(n_rcv, n_src, pplus, pminus, band):
    blocks_here = band.shape[0]
    rows = BLOCK // n_src
    cols = 2 * pplus.shape[2]
    order = ring_order(n_src)
    ahead = [(order[p], order[(p + 1) % n_src]) for p in range(n_src)]
    behind = [(d, s) for s, d in ahead]

    def swaps(first):
        pairs = [(r, r + 1) for r in range(first, n_rcv - 1, 2)]
        return pairs + [(d, s) for s, d in pairs]

    own = pplus.reshape(blocks_here * BLOCK, cols)
    chunks, shifts = [own], [0]
    fwd = bwd = own
    for step in range(1, n_src // 2 + 1):
        fwd = lax.ppermute(fwd, "src", ahead)
        chunks.append(fwd)
        shifts.append(-step)
        if len(chunks) < n_src:
            bwd = lax.ppermute(bwd, "src", behind)
            chunks.append(bwd)
            shifts.append(step)
    near = [lax.ppermute(c, "rcv", swaps(0)) for c in chunks]
    far = [lax.ppermute(c, "rcv", swaps(1)) for c in chunks]

    me = jnp.stack([lax.axis_index("rcv"), lax.axis_index("src")]).astype(jnp.int32)
    start = lax.optimization_barrier(pminus.reshape(blocks_here * BLOCK, cols))
    start = jnp.transpose(start.reshape(blocks_here, n_src, rows, cols), (1, 0, 2, 3))
    field = lax.all_to_all(start.reshape(n_src, blocks_here * rows, cols), "src", 0, 0, tiled=True)

    any_spec = pl.BlockSpec(memory_space=pl.ANY)
    smem, vmem = pl.BlockSpec(memory_space=pltpu.SMEM), pl.BlockSpec(memory_space=pltpu.VMEM)
    band_cols = NEIGH * BLOCK
    need = 2 * blocks_here * band_cols * n_src * cols + (16 << 20)
    grad, hess, images, sums = pl.pallas_call(
        functools.partial(maps_kernel, n_src, shifts),
        out_shape=(
            jax.ShapeDtypeStruct((blocks_here, 2 * rows, band_cols), jnp.float32),
            jax.ShapeDtypeStruct((blocks_here, 2 * rows, band_cols), jnp.float32),
            jax.ShapeDtypeStruct((n_src, 2 * blocks_here * rows, cols), jnp.bfloat16),
            jax.ShapeDtypeStruct((8, 128), jnp.float32),
        ),
        in_specs=[smem, smem, vmem] + [any_spec] * (3 * n_src),
        out_specs=[vmem] * 4,
        scratch_shapes=[
            pltpu.VMEM((blocks_here, band_cols, n_src * cols), jnp.bfloat16),
            pltpu.VMEM((blocks_here, 2 * rows, n_src * cols), jnp.bfloat16),
            pltpu.VMEM((n_src, blocks_here * rows, cols), jnp.float32),
            pltpu.VMEM((n_src, blocks_here * rows, cols), jnp.float32),
            pltpu.SemaphoreType.DMA((n_src,)),
        ],
        compiler_params=pltpu.CompilerParams(vmem_limit_bytes=min(need, 56 << 20)),
        name="maps",
    )(me, band, field, *chunks, *near, *far)

    everyone = lax.all_to_all(
        jnp.broadcast_to(sums[None], (n_rcv * n_src,) + sums.shape), ("rcv", "src"), 0, 0, tiled=True
    )
    images = lax.all_to_all(images, "src", 0, 0, tiled=True)
    refl, moved = pl.pallas_call(
        combine_kernel,
        out_shape=(
            jax.ShapeDtypeStruct(grad.shape, jnp.float32),
            jax.ShapeDtypeStruct((n_src, blocks_here * rows, cols), jnp.float32),
        ),
        in_specs=[smem] + [vmem] * 4,
        out_specs=[vmem] * 2,
        compiler_params=pltpu.CompilerParams(vmem_limit_bytes=16 << 20),
        name="combine",
    )(me, everyone, images, grad, hess)

    refl = jnp.transpose(refl.reshape(blocks_here, 2, rows, NEIGH, BLOCK), (2, 0, 3, 1, 4))
    moved = jnp.transpose(moved.reshape(n_src, blocks_here, rows, cols), (1, 0, 2, 3))
    misfit = pminus.astype(jnp.float32) - moved.reshape(pminus.shape)
    return refl, misfit


def solution(mesh):
    return jax.shard_map(
        functools.partial(per_device, mesh.shape["rcv"], mesh.shape["src"]),
        mesh=mesh,
        in_specs=(P("rcv", None, "src"), P("rcv", None, "src"), P("rcv", None)),
        out_specs=(P("src", "rcv", None, None, None), P("rcv", None, "src")),
        check_vma=False,
    )
```

```python
import functools

import jax
import jax.numpy as jnp
from jax import lax
from jax.experimental import pallas as pl
from jax.experimental.pallas import tpu as pltpu
from jax.sharding import PartitionSpec as P

BLOCK = 256
NEIGH = 3
HALO_BLK = 2
ROWS_X = 2
SHARE_ROWS = 16


def ring_order(count):
    if count % ROWS_X or count < 2 * ROWS_X:
        return list(range(count))
    half = count // ROWS_X
    return [ROWS_X * p for p in range(half)] + [ROWS_X * p + 1 for p in reversed(range(half))]


def ring_place(count, index, shift):
    if count % ROWS_X or count < 2 * ROWS_X:
        return lax.rem(index + shift + count, count)
    half, odd = count // ROWS_X, lax.rem(index, ROWS_X)
    step = (index - odd) // ROWS_X
    place = lax.rem(jnp.where(odd == 1, count - 1 - step, step) + shift + count, count)
    return jnp.where(place < half, ROWS_X * place, ROWS_X * (count - 1 - place) + 1)


def along(sums):
    total = jnp.sum(sums, axis=1, keepdims=True)
    qq, qw = total[1:2], total[4:5]
    return jnp.where(qq > 0, qw / jnp.where(qq > 0, qq, 1.0), 0.0)


def maps_kernel(n_src, shifts, *refs):
    me, band, field = refs[:3]
    own, near, far = refs[3 : 3 + n_src], refs[3 + n_src : 3 + 2 * n_src], refs[3 + 2 * n_src : 3 + 3 * n_src]
    grad_out, hess_out, images_out, sums_out = refs[3 + 3 * n_src : 7 + 3 * n_src]
    panel, lhs, image0, image1, grad, hess, images, sems, out_sems = refs[7 + 3 * n_src :]
    blocks_here = panel.shape[0]
    rows = lhs.shape[1] // 2
    cols = field.shape[2]
    half = cols // 2
    me_rcv, me_src = me[0], me[1]
    odd = lax.rem(me_rcv, 2)
    where = [ring_place(n_src, me_src, shift) for shift in shifts]

    for i in range(blocks_here):
        for k in range(NEIGH):
            offset = band[i, k] - me_rcv * blocks_here
            here = (offset >= 0) & (offset < blocks_here)
            toward = jnp.where(offset < 0, 1, 0)
            inside = jnp.where(offset < 0, offset + HALO_BLK, jnp.where(here, offset, offset - blocks_here))
            start = pl.multiple_of(inside * BLOCK, BLOCK)

            def fetch(group, i=i, k=k, start=start):
                for slot in range(n_src):
                    pltpu.make_async_copy(
                        group[slot].at[pl.ds(start, BLOCK), :],
                        panel.at[i, pl.ds(k * BLOCK, BLOCK), pl.ds(slot * cols, cols)],
                        sems.at[slot],
                    ).start()

            @pl.when(here)
            def _():
                fetch(own)

            @pl.when(jnp.logical_not(here) & (toward == odd))
            def _():
                fetch(near)

            @pl.when(jnp.logical_not(here) & (toward != odd))
            def _():
                fetch(far)

    for slot in range(n_src):
        for i in range(blocks_here):
            rows_bf = field[where[slot], i * rows : (i + 1) * rows, :]
            lhs[i, :rows, slot * cols : (slot + 1) * cols] = rows_bf
            lhs[i, rows:, slot * cols : slot * cols + half] = rows_bf[:, half:]
            lhs[i, rows:, slot * cols + half : (slot + 1) * cols] = -rows_bf[:, :half]

    def arrived(slots):
        for slot in slots:
            for i in range(blocks_here):
                for k in range(NEIGH):
                    pltpu.make_async_copy(
                        own[slot].at[pl.ds(0, BLOCK), :],
                        panel.at[i, pl.ds(k * BLOCK, BLOCK), pl.ds(slot * cols, cols)],
                        sems.at[slot],
                    ).wait()

    def fold(x):
        total = x[:, :128]
        for c in range(128, x.shape[1], 128):
            total = total + x[:, c : c + 128]
        return jnp.sum(total, axis=0, keepdims=True)

    def adjoint(i, first=0, last=n_src):
        part = slice(first * cols, last * cols)
        return lax.dot_general(
            lhs[i, :, part], panel[i, :, part], (((1,), (1,)), ((), ())), preferred_element_type=jnp.float32
        )

    def forward(i, x_bf, slot):
        prod = jnp.dot(
            x_bf, panel[i, :, slot * cols : (slot + 1) * cols], preferred_element_type=jnp.float32
        )
        return prod[:rows, :half] - prod[rows:, half:], prod[:rows, half:] + prod[rows:, :half]

    zero = jnp.zeros((1, 128), jnp.float32)
    gg, qq, gh, hh, qw, ww = zero, zero, zero, zero, zero, zero
    middle = (n_src + 1) // 2
    arrived(range(middle))
    for i in range(blocks_here):
        grad[i] = adjoint(i, 0, middle)
    arrived(range(middle, n_src))
    for i in range(blocks_here):
        grad[i] += adjoint(i, middle, n_src)
    grad_copy = pltpu.make_async_copy(grad, grad_out, out_sems.at[0])
    grad_copy.start()
    for i in range(blocks_here):
        mine = slice(i * rows, (i + 1) * rows)
        g0 = grad[i]
        gg += fold(g0 * g0)
        g_bf = g0.astype(jnp.bfloat16)
        for slot in range(n_src):
            re, im = forward(i, g_bf, slot)
            qq += fold(re * re + im * im)
            image0[slot, mine, :half] = re
            image0[slot, mine, half:] = im
            re_bf, im_bf = re.astype(jnp.bfloat16), im.astype(jnp.bfloat16)
            lhs[i, :rows, slot * cols : slot * cols + half] = re_bf
            lhs[i, :rows, slot * cols + half : (slot + 1) * cols] = im_bf
            lhs[i, rows:, slot * cols : slot * cols + half] = im_bf
            lhs[i, rows:, slot * cols + half : (slot + 1) * cols] = -re_bf
    for i in range(blocks_here):
        mine = slice(i * rows, (i + 1) * rows)
        h0 = adjoint(i)
        hess[i] = h0
        gh += fold(h0 * grad[i])
        hh += fold(h0 * h0)
        h_bf = h0.astype(jnp.bfloat16)
        for slot in range(n_src):
            re, im = forward(i, h_bf, slot)
            ww += fold(re * re + im * im)
            qw += fold(re * image0[slot, mine, :half] + im * image0[slot, mine, half:])
            image1[slot, mine, :half] = re
            image1[slot, mine, half:] = im
    sums = jnp.concatenate([gg, qq, gh, hh, qw, ww, zero, zero], axis=0)
    sums_out[...] = sums
    hess_copy = pltpu.make_async_copy(hess, hess_out, out_sems.at[1])
    hess_copy.start()
    share_bf = along(sums).astype(jnp.bfloat16)
    share = share_bf.astype(jnp.float32)
    height = blocks_here * rows
    copies = [grad_copy, hess_copy]
    for slot in range(n_src):
        first = image0[slot]
        images[slot, :height] = first.astype(jnp.bfloat16)
        images[slot, height : 2 * height] = (image1[slot] - share * first).astype(jnp.bfloat16)
        images[slot, 2 * height :] = jnp.broadcast_to(share_bf, (SHARE_ROWS, cols))
        copies.append(pltpu.make_async_copy(images.at[slot], images_out.at[where[slot]], out_sems.at[2 + slot]))
        copies[-1].start()
    for copy in copies:
        copy.wait()


def combine_kernel(sums, images, grad, hess, refl_out, moved_out):
    n_src, height = images.shape[0], (images.shape[1] - SHARE_ROWS) // 2
    total = jnp.sum(sums[...], axis=1, keepdims=True)
    gg, qq, gh, hh, qw, ww = [total[i : i + 1] for i in range(6)]
    step0 = gg / qq
    grad_next = gg - 2 * step0 * gh + step0 * step0 * hh
    near = 1 + grad_next / gg
    image_sq = near * near * qq - 2 * near * step0 * qw + step0 * step0 * ww
    step1 = grad_next / image_sq
    c1 = step0 + step1 * near
    c2 = -step0 * step1
    for i in range(grad.shape[0]):
        refl_out[i] = c1 * grad[i] + c2 * hess[i]
    for s in range(n_src):
        share = images[s, 2 * height :].astype(jnp.float32)[:1, :1]
        first = images[s, :height].astype(jnp.float32)
        rest = images[s, height : 2 * height].astype(jnp.float32)
        moved_out[s] = (c1 + c2 * share) * first + c2 * rest


def summed(x, axes):
    for axis, count in axes:
        if count & (count - 1):
            x = lax.psum(x, axis)
            continue
        bit = 1
        while bit < count:
            x = x + lax.ppermute(x, axis, [(d, d ^ bit) for d in range(count)])
            bit *= 2
    return x


def per_device(n_rcv, n_src, pplus, pminus, band):
    blocks_here = band.shape[0]
    rows = BLOCK // n_src
    cols = 2 * pplus.shape[2]
    order = ring_order(n_src)
    ahead = [(order[p], order[(p + 1) % n_src]) for p in range(n_src)]
    behind = [(d, s) for s, d in ahead]

    def swaps(first):
        pairs = [(r, r + 1) for r in range(first, n_rcv - 1, 2)]
        return pairs + [(d, s) for s, d in pairs]

    own = pplus.reshape(blocks_here * BLOCK, cols)
    chunks, shifts = [own], [0]
    fwd = bwd = own
    for step in range(1, n_src // 2 + 1):
        fwd = lax.ppermute(fwd, "src", ahead)
        chunks.append(fwd)
        shifts.append(-step)
        if len(chunks) < n_src:
            bwd = lax.ppermute(bwd, "src", behind)
            chunks.append(bwd)
            shifts.append(step)
    near = [lax.ppermute(c, "rcv", swaps(0)) for c in chunks]
    far = [lax.ppermute(c, "rcv", swaps(1)) for c in chunks]

    me = jnp.stack([lax.axis_index("rcv"), lax.axis_index("src")]).astype(jnp.int32)
    start = lax.optimization_barrier(pminus.reshape(blocks_here * BLOCK, cols))
    start = jnp.transpose(start.reshape(blocks_here, n_src, rows, cols), (1, 0, 2, 3))
    field = lax.all_to_all(start.reshape(n_src, blocks_here * rows, cols), "src", 0, 0, tiled=True)

    hbm = pl.BlockSpec(memory_space=pltpu.HBM)
    smem, vmem = pl.BlockSpec(memory_space=pltpu.SMEM), pl.BlockSpec(memory_space=pltpu.VMEM)
    band_cols = NEIGH * BLOCK
    need = 2 * blocks_here * band_cols * n_src * cols + (16 << 20)
    grad, hess, images, sums = pl.pallas_call(
        functools.partial(maps_kernel, n_src, shifts),
        out_shape=(
            jax.ShapeDtypeStruct((blocks_here, 2 * rows, band_cols), jnp.float32),
            jax.ShapeDtypeStruct((blocks_here, 2 * rows, band_cols), jnp.float32),
            jax.ShapeDtypeStruct((n_src, 2 * blocks_here * rows + SHARE_ROWS, cols), jnp.bfloat16),
            jax.ShapeDtypeStruct((8, 128), jnp.float32),
        ),
        in_specs=[smem, smem, vmem] + [hbm] * (3 * n_src),
        out_specs=[hbm] * 3 + [vmem],
        scratch_shapes=[
            pltpu.VMEM((blocks_here, band_cols, n_src * cols), jnp.bfloat16),
            pltpu.VMEM((blocks_here, 2 * rows, n_src * cols), jnp.bfloat16),
            pltpu.VMEM((n_src, blocks_here * rows, cols), jnp.float32),
            pltpu.VMEM((n_src, blocks_here * rows, cols), jnp.float32),
            pltpu.VMEM((blocks_here, 2 * rows, band_cols), jnp.float32),
            pltpu.VMEM((blocks_here, 2 * rows, band_cols), jnp.float32),
            pltpu.VMEM((n_src, 2 * blocks_here * rows + SHARE_ROWS, cols), jnp.bfloat16),
            pltpu.SemaphoreType.DMA((n_src,)),
            pltpu.SemaphoreType.DMA((2 + n_src,)),
        ],
        compiler_params=pltpu.CompilerParams(vmem_limit_bytes=min(need, 56 << 20)),
        name="maps",
    )(me, band, field, *chunks, *near, *far)

    images = lax.all_to_all(images, "src", 0, 0, tiled=True)
    sums = summed(sums, (("rcv", n_rcv), ("src", n_src)))
    refl, moved = pl.pallas_call(
        combine_kernel,
        out_shape=(
            jax.ShapeDtypeStruct(grad.shape, jnp.float32),
            jax.ShapeDtypeStruct((n_src, blocks_here * rows, cols), jnp.float32),
        ),
        in_specs=[vmem] * 4,
        out_specs=[vmem] * 2,
        compiler_params=pltpu.CompilerParams(vmem_limit_bytes=16 << 20),
        name="combine",
    )(sums, images, grad, hess)

    refl = jnp.transpose(refl.reshape(blocks_here, 2, rows, NEIGH, BLOCK), (2, 0, 3, 1, 4))
    moved = jnp.transpose(moved.reshape(n_src, blocks_here, rows, cols), (1, 0, 2, 3))
    misfit = pminus.astype(jnp.float32) - moved.reshape(pminus.shape)
    return refl, misfit


def solution(mesh):
    return jax.shard_map(
        functools.partial(per_device, mesh.shape["rcv"], mesh.shape["src"]),
        mesh=mesh,
        in_specs=(P("rcv", None, "src"), P("rcv", None, "src"), P("rcv", None)),
        out_specs=(P("src", "rcv", None, None, None), P("rcv", None, "src")),
        check_vma=False,
    )
```

```python
import functools

import jax
import jax.numpy as jnp
from jax import lax
from jax.experimental import pallas as pl
from jax.experimental.pallas import tpu as pltpu
from jax.sharding import PartitionSpec as P

BLOCK = 256
NEIGH = 3
HALO_BLK = 2
ROWS_X = 2
SHARE_ROWS = 16


def ring_order(count):
    if count % ROWS_X or count < 2 * ROWS_X:
        return list(range(count))
    half = count // ROWS_X
    return [ROWS_X * p for p in range(half)] + [ROWS_X * p + 1 for p in reversed(range(half))]


def ring_place(count, index, shift):
    if count % ROWS_X or count < 2 * ROWS_X:
        return lax.rem(index + shift + count, count)
    half, odd = count // ROWS_X, lax.rem(index, ROWS_X)
    step = (index - odd) // ROWS_X
    place = lax.rem(jnp.where(odd == 1, count - 1 - step, step) + shift + count, count)
    return jnp.where(place < half, ROWS_X * place, ROWS_X * (count - 1 - place) + 1)


def along(sums):
    total = jnp.sum(sums, axis=1, keepdims=True)
    qq, qw = total[1:2], total[4:5]
    return jnp.where(qq > 0, qw / jnp.where(qq > 0, qq, 1.0), 0.0)


def maps_kernel(n_src, shifts, batches, *refs):
    me, band, field = refs[:3]
    ends = [3, 3 + n_src, 3 + n_src + len(batches), 3 + n_src + 2 * len(batches)]
    own, near, far = [refs[a:b] for a, b in zip(ends[:-1], ends[1:])]
    grad_out, hess_out, images_out, sums_out = refs[ends[3] : ends[3] + 4]
    panel, lhs, image0, image1, grad, hess, images, sems, out_sems = refs[ends[3] + 4 :]
    blocks_here = panel.shape[0]
    rows = lhs.shape[0] // (2 * blocks_here)
    cols = field.shape[2]
    half = cols // 2
    me_rcv, me_src = me[0], me[1]
    odd = lax.rem(me_rcv, 2)
    where = [ring_place(n_src, me_src, shift) for shift in shifts]

    for i in range(blocks_here):
        for k in range(NEIGH):
            offset = band[i, k] - me_rcv * blocks_here
            here = (offset >= 0) & (offset < blocks_here)
            toward = jnp.where(offset < 0, 1, 0)
            inside = jnp.where(offset < 0, offset + HALO_BLK, jnp.where(here, offset, offset - blocks_here))
            start = pl.multiple_of(inside * BLOCK, BLOCK)

            def fetch(arrays, groups, i=i, k=k, start=start):
                for array, group in zip(arrays, groups):
                    for place, slot in enumerate(group):
                        pltpu.make_async_copy(
                            array.at[pl.ds(start + place * blocks_here * BLOCK, BLOCK), :],
                            panel.at[i, pl.ds(k * BLOCK, BLOCK), pl.ds(slot * cols, cols)],
                            sems.at[slot],
                        ).start()

            @pl.when(here)
            def _():
                fetch(own, [[slot] for slot in range(n_src)])

            @pl.when(jnp.logical_not(here) & (toward == odd))
            def _():
                fetch(near, batches)

            @pl.when(jnp.logical_not(here) & (toward != odd))
            def _():
                fetch(far, batches)

    def store(i, slot, re_bf, im_bf):
        top, low = slice(2 * i * rows, (2 * i + 1) * rows), slice((2 * i + 1) * rows, (2 * i + 2) * rows)
        left, right = slice(slot * cols, slot * cols + half), slice(slot * cols + half, (slot + 1) * cols)
        lhs[top, left] = re_bf
        lhs[top, right] = im_bf
        lhs[low, left] = im_bf
        lhs[low, right] = -re_bf

    for slot in range(n_src):
        for i in range(blocks_here):
            rows_bf = field[where[slot], i * rows : (i + 1) * rows, :]
            store(i, slot, rows_bf[:, :half], rows_bf[:, half:])

    def arrived(slots):
        for slot in slots:
            for i in range(blocks_here):
                for k in range(NEIGH):
                    pltpu.make_async_copy(
                        own[slot].at[pl.ds(0, BLOCK), :],
                        panel.at[i, pl.ds(k * BLOCK, BLOCK), pl.ds(slot * cols, cols)],
                        sems.at[slot],
                    ).wait()

    def fold(x):
        total = x[:, :128]
        for c in range(128, x.shape[1], 128):
            total = total + x[:, c : c + 128]
        return jnp.sum(total, axis=0, keepdims=True)

    def adjoint(i, first=0, last=n_src):
        part = slice(first * cols, last * cols)
        flipped = lax.dot_general(
            panel[i, :, part], lhs[:, part], (((1,), (1,)), ((), ())), preferred_element_type=jnp.float32
        )
        return jnp.transpose(flipped)[2 * i * rows : 2 * (i + 1) * rows]

    def forward(i, x_bf, slot):
        prod = jnp.dot(
            x_bf, panel[i, :, slot * cols : (slot + 1) * cols], preferred_element_type=jnp.float32
        )
        return prod[:rows, :half] - prod[rows:, half:], prod[:rows, half:] + prod[rows:, :half]

    zero = jnp.zeros((1, 128), jnp.float32)
    gg, qq, gh, hh, qw, ww = zero, zero, zero, zero, zero, zero
    middle = (n_src + 1) // 2
    arrived(range(middle))
    for i in range(blocks_here):
        grad[i] = adjoint(i, 0, middle)
    arrived(range(middle, n_src))
    for i in range(blocks_here):
        grad[i] += adjoint(i, middle, n_src)
    grad_copy = pltpu.make_async_copy(grad, grad_out, out_sems.at[0])
    grad_copy.start()
    for i in range(blocks_here):
        mine = slice(i * rows, (i + 1) * rows)
        g0 = grad[i]
        gg += fold(g0 * g0)
        g_bf = g0.astype(jnp.bfloat16)
        for slot in range(n_src):
            re, im = forward(i, g_bf, slot)
            qq += fold(re * re + im * im)
            image0[slot, mine, :half] = re
            image0[slot, mine, half:] = im
            store(i, slot, re.astype(jnp.bfloat16), im.astype(jnp.bfloat16))
    for i in range(blocks_here):
        mine = slice(i * rows, (i + 1) * rows)
        h0 = adjoint(i)
        hess[i] = h0
        gh += fold(h0 * grad[i])
        hh += fold(h0 * h0)
        h_bf = h0.astype(jnp.bfloat16)
        for slot in range(n_src):
            re, im = forward(i, h_bf, slot)
            ww += fold(re * re + im * im)
            qw += fold(re * image0[slot, mine, :half] + im * image0[slot, mine, half:])
            image1[slot, mine, :half] = re
            image1[slot, mine, half:] = im
    sums = jnp.concatenate([gg, qq, gh, hh, qw, ww, zero, zero], axis=0)
    sums_out[...] = sums
    hess_copy = pltpu.make_async_copy(hess, hess_out, out_sems.at[1])
    hess_copy.start()
    share_bf = along(sums).astype(jnp.bfloat16)
    share = share_bf.astype(jnp.float32)
    height = blocks_here * rows
    copies = [grad_copy, hess_copy]
    for slot in range(n_src):
        first = image0[slot]
        images[slot, :height] = first.astype(jnp.bfloat16)
        images[slot, height : 2 * height] = (image1[slot] - share * first).astype(jnp.bfloat16)
        images[slot, 2 * height :] = jnp.broadcast_to(share_bf, (SHARE_ROWS, cols))
        copies.append(pltpu.make_async_copy(images.at[slot], images_out.at[where[slot]], out_sems.at[2 + slot]))
        copies[-1].start()
    for copy in copies:
        copy.wait()


def combine_kernel(sums, images, grad, hess, refl_out, moved_out):
    n_src, height = images.shape[0], (images.shape[1] - SHARE_ROWS) // 2
    total = jnp.sum(jnp.sum(sums[...], axis=0), axis=1, keepdims=True)
    gg, qq, gh, hh, qw, ww = [total[i : i + 1] for i in range(6)]
    step0 = gg / qq
    grad_next = gg - 2 * step0 * gh + step0 * step0 * hh
    near = 1 + grad_next / gg
    image_sq = near * near * qq - 2 * near * step0 * qw + step0 * step0 * ww
    step1 = grad_next / image_sq
    c1 = step0 + step1 * near
    c2 = -step0 * step1
    for i in range(grad.shape[0]):
        refl_out[i] = c1 * grad[i] + c2 * hess[i]
    for s in range(n_src):
        share = images[s, 2 * height :].astype(jnp.float32)[:1, :1]
        first = images[s, :height].astype(jnp.float32)
        rest = images[s, height : 2 * height].astype(jnp.float32)
        moved_out[s] = (c1 + c2 * share) * first + c2 * rest


def per_device(n_rcv, n_src, pplus, pminus, band):
    blocks_here = band.shape[0]
    rows = BLOCK // n_src
    cols = 2 * pplus.shape[2]
    order = ring_order(n_src)
    ahead = [(order[p], order[(p + 1) % n_src]) for p in range(n_src)]
    behind = [(d, s) for s, d in ahead]

    def swaps(first):
        pairs = [(r, r + 1) for r in range(first, n_rcv - 1, 2)]
        return pairs + [(d, s) for s, d in pairs]

    start = lax.optimization_barrier(pminus.reshape(blocks_here * BLOCK, cols))
    start = jnp.transpose(start.reshape(blocks_here, n_src, rows, cols), (1, 0, 2, 3))
    field = lax.all_to_all(start.reshape(n_src, blocks_here * rows, cols), "src", 0, 0, tiled=True)

    own = pplus.reshape(blocks_here * BLOCK, cols)
    chunks, shifts = [own], [0]
    batches = [[0, 1, 2][:n_src]]
    fwd = bwd = own
    for step in range(1, n_src // 2 + 1):
        if step == 3:
            fwd, bwd, field = lax.optimization_barrier((fwd, bwd, field))
        if step > 1:
            batches.append(list(range(len(chunks), min(len(chunks) + 2, n_src))))
        fwd = lax.ppermute(fwd, "src", ahead)
        chunks.append(fwd)
        shifts.append(-step)
        if len(chunks) < n_src:
            bwd = lax.ppermute(bwd, "src", behind)
            chunks.append(bwd)
            shifts.append(step)
    joined = [jnp.concatenate([chunks[c] for c in batch], axis=0) for batch in batches]
    near = [lax.ppermute(c, "rcv", swaps(0)) for c in joined]
    far = [lax.ppermute(c, "rcv", swaps(1)) for c in joined]
    me = jnp.stack([lax.axis_index("rcv"), lax.axis_index("src")]).astype(jnp.int32)

    any_spec = pl.BlockSpec(memory_space=pl.ANY)
    smem, vmem = pl.BlockSpec(memory_space=pltpu.SMEM), pl.BlockSpec(memory_space=pltpu.VMEM)
    band_cols = NEIGH * BLOCK
    need = 2 * blocks_here * band_cols * n_src * cols + (16 << 20)
    grad, hess, images, sums = pl.pallas_call(
        functools.partial(maps_kernel, n_src, shifts, batches),
        out_shape=(
            jax.ShapeDtypeStruct((blocks_here, 2 * rows, band_cols), jnp.float32),
            jax.ShapeDtypeStruct((blocks_here, 2 * rows, band_cols), jnp.float32),
            jax.ShapeDtypeStruct((n_src, 2 * blocks_here * rows + SHARE_ROWS, cols), jnp.bfloat16),
            jax.ShapeDtypeStruct((8, 128), jnp.float32),
        ),
        in_specs=[smem, smem, vmem] + [any_spec] * (n_src + 2 * len(batches)),
        out_specs=[any_spec] * 3 + [vmem],
        scratch_shapes=[
            pltpu.VMEM((blocks_here, band_cols, n_src * cols), jnp.bfloat16),
            pltpu.VMEM((blocks_here * 2 * rows, n_src * cols), jnp.bfloat16),
            pltpu.VMEM((n_src, blocks_here * rows, cols), jnp.float32),
            pltpu.VMEM((n_src, blocks_here * rows, cols), jnp.float32),
            pltpu.VMEM((blocks_here, 2 * rows, band_cols), jnp.float32),
            pltpu.VMEM((blocks_here, 2 * rows, band_cols), jnp.float32),
            pltpu.VMEM((n_src, 2 * blocks_here * rows + SHARE_ROWS, cols), jnp.bfloat16),
            pltpu.SemaphoreType.DMA((n_src,)),
            pltpu.SemaphoreType.DMA((2 + n_src,)),
        ],
        compiler_params=pltpu.CompilerParams(vmem_limit_bytes=min(need, 56 << 20)),
        name="maps",
    )(me, band, field, *chunks, *near, *far)

    images = lax.all_to_all(images, "src", 0, 0, tiled=True)
    sums = lax.all_gather(sums, ("rcv", "src"))
    refl, moved = pl.pallas_call(
        combine_kernel,
        out_shape=(
            jax.ShapeDtypeStruct(grad.shape, jnp.float32),
            jax.ShapeDtypeStruct((n_src, blocks_here * rows, cols), jnp.float32),
        ),
        in_specs=[vmem] * 4,
        out_specs=[vmem] * 2,
        compiler_params=pltpu.CompilerParams(vmem_limit_bytes=16 << 20),
        name="combine",
    )(sums, images, grad, hess)

    refl = jnp.transpose(refl.reshape(blocks_here, 2, rows, NEIGH, BLOCK), (2, 0, 3, 1, 4))
    moved = jnp.transpose(moved.reshape(n_src, blocks_here, rows, cols), (1, 0, 2, 3))
    misfit = pminus.astype(jnp.float32) - moved.reshape(pminus.shape)
    return refl, misfit


def solution(mesh):
    return jax.shard_map(
        functools.partial(per_device, mesh.shape["rcv"], mesh.shape["src"]),
        mesh=mesh,
        in_specs=(P("rcv", None, "src"), P("rcv", None, "src"), P("rcv", None)),
        out_specs=(P("src", "rcv", None, None, None), P("rcv", None, "src")),
        check_vma=False,
    )
```

```python
import functools

import jax
import jax.numpy as jnp
from jax import lax
from jax.experimental import pallas as pl
from jax.experimental.pallas import tpu as pltpu
from jax.sharding import PartitionSpec as P

BLOCK = 256
NEIGH = 3
HALO_BLK = 2
ROWS_X = 2
SHARE_ROWS = 16


def ring_order(count):
    if count % ROWS_X or count < 2 * ROWS_X:
        return list(range(count))
    half = count // ROWS_X
    return [ROWS_X * p for p in range(half)] + [ROWS_X * p + 1 for p in reversed(range(half))]


def ring_place(count, index, shift):
    if count % ROWS_X or count < 2 * ROWS_X:
        return lax.rem(index + shift + count, count)
    half, odd = count // ROWS_X, lax.rem(index, ROWS_X)
    step = (index - odd) // ROWS_X
    place = lax.rem(jnp.where(odd == 1, count - 1 - step, step) + shift + count, count)
    return jnp.where(place < half, ROWS_X * place, ROWS_X * (count - 1 - place) + 1)


def along(sums):
    total = jnp.sum(sums, axis=1, keepdims=True)
    qq, qw = total[1:2], total[4:5]
    return jnp.where(qq > 0, qw / jnp.where(qq > 0, qq, 1.0), 0.0)


def maps_kernel(n_src, shifts, batches, *refs):
    me, band, field = refs[:3]
    ends = [3, 3 + n_src, 3 + n_src + len(batches), 3 + n_src + 2 * len(batches)]
    own, near, far = [refs[a:b] for a, b in zip(ends[:-1], ends[1:])]
    grad_out, hess_out, images_out, sums_out = refs[ends[3] : ends[3] + 4]
    panel, lhs, image0, image1, grad, hess, images, sems, out_sems = refs[ends[3] + 4 :]
    blocks_here = panel.shape[0]
    rows = lhs.shape[0] // (2 * blocks_here)
    cols = field.shape[2]
    half = cols // 2
    me_rcv, me_src = me[0], me[1]
    odd = lax.rem(me_rcv, 2)
    where = [ring_place(n_src, me_src, shift) for shift in shifts]

    for i in range(blocks_here):
        for k in range(NEIGH):
            offset = band[i, k] - me_rcv * blocks_here
            here = (offset >= 0) & (offset < blocks_here)
            toward = jnp.where(offset < 0, 1, 0)
            inside = jnp.where(offset < 0, offset + HALO_BLK, jnp.where(here, offset, offset - blocks_here))
            start = pl.multiple_of(inside * BLOCK, BLOCK)

            def fetch(arrays, groups, i=i, k=k, start=start):
                for array, group in zip(arrays, groups):
                    for place, slot in enumerate(group):
                        pltpu.make_async_copy(
                            array.at[pl.ds(start + place * blocks_here * BLOCK, BLOCK), :],
                            panel.at[i, pl.ds(k * BLOCK, BLOCK), pl.ds(slot * cols, cols)],
                            sems.at[slot],
                        ).start()

            @pl.when(here)
            def _():
                fetch(own, [[slot] for slot in range(n_src)])

            @pl.when(jnp.logical_not(here) & (toward == odd))
            def _():
                fetch(near, batches)

            @pl.when(jnp.logical_not(here) & (toward != odd))
            def _():
                fetch(far, batches)

    def store(i, slot, re_bf, im_bf):
        top, low = slice(2 * i * rows, (2 * i + 1) * rows), slice((2 * i + 1) * rows, (2 * i + 2) * rows)
        left, right = slice(slot * cols, slot * cols + half), slice(slot * cols + half, (slot + 1) * cols)
        lhs[top, left] = re_bf
        lhs[top, right] = im_bf
        lhs[low, left] = im_bf
        lhs[low, right] = -re_bf

    for slot in range(n_src):
        for i in range(blocks_here):
            rows_bf = field[where[slot], i * rows : (i + 1) * rows, :]
            store(i, slot, rows_bf[:, :half], rows_bf[:, half:])

    def arrived(slots):
        for slot in slots:
            for i in range(blocks_here):
                for k in range(NEIGH):
                    pltpu.make_async_copy(
                        own[slot].at[pl.ds(0, BLOCK), :],
                        panel.at[i, pl.ds(k * BLOCK, BLOCK), pl.ds(slot * cols, cols)],
                        sems.at[slot],
                    ).wait()

    def fold(x):
        total = x[:, :128]
        for c in range(128, x.shape[1], 128):
            total = total + x[:, c : c + 128]
        return jnp.sum(total, axis=0, keepdims=True)

    def adjoint(i, first=0, last=n_src):
        part = slice(first * cols, last * cols)
        mine = slice(2 * i * rows, 2 * (i + 1) * rows)
        return lax.dot_general(
            lhs[mine, part], panel[i, :, part], (((1,), (1,)), ((), ())), preferred_element_type=jnp.float32
        )

    def forward(i, x_bf, slot):
        prod = jnp.dot(
            x_bf, panel[i, :, slot * cols : (slot + 1) * cols], preferred_element_type=jnp.float32
        )
        return prod[:rows, :half] - prod[rows:, half:], prod[:rows, half:] + prod[rows:, :half]

    zero = jnp.zeros((1, 128), jnp.float32)
    gg, qq, gh, hh, qw, ww = zero, zero, zero, zero, zero, zero
    middle = (n_src + 1) // 2
    arrived(range(middle))
    for i in range(blocks_here):
        grad[i] = adjoint(i, 0, middle)
    arrived(range(middle, n_src))
    for i in range(blocks_here):
        grad[i] += adjoint(i, middle, n_src)
    grad_copy = pltpu.make_async_copy(grad, grad_out, out_sems.at[0])
    grad_copy.start()
    for i in range(blocks_here):
        mine = slice(i * rows, (i + 1) * rows)
        g0 = grad[i]
        gg += fold(g0 * g0)
        g_bf = g0.astype(jnp.bfloat16)
        for slot in range(n_src):
            re, im = forward(i, g_bf, slot)
            qq += fold(re * re + im * im)
            image0[slot, mine, :half] = re
            image0[slot, mine, half:] = im
            store(i, slot, re.astype(jnp.bfloat16), im.astype(jnp.bfloat16))
    for i in range(blocks_here):
        mine = slice(i * rows, (i + 1) * rows)
        h0 = adjoint(i)
        hess[i] = h0
        gh += fold(h0 * grad[i])
        hh += fold(h0 * h0)
        h_bf = h0.astype(jnp.bfloat16)
        for slot in range(n_src):
            re, im = forward(i, h_bf, slot)
            ww += fold(re * re + im * im)
            qw += fold(re * image0[slot, mine, :half] + im * image0[slot, mine, half:])
            image1[slot, mine, :half] = re
            image1[slot, mine, half:] = im
    sums = jnp.concatenate([gg, qq, gh, hh, qw, ww, zero, zero], axis=0)
    sums_out[...] = sums
    hess_copy = pltpu.make_async_copy(hess, hess_out, out_sems.at[1])
    hess_copy.start()
    share_bf = along(sums).astype(jnp.bfloat16)
    share = share_bf.astype(jnp.float32)
    height = blocks_here * rows
    copies = [grad_copy, hess_copy]
    for slot in range(n_src):
        first = image0[slot]
        images[slot, :height] = first.astype(jnp.bfloat16)
        images[slot, height : 2 * height] = (image1[slot] - share * first).astype(jnp.bfloat16)
        images[slot, 2 * height :] = jnp.broadcast_to(share_bf, (SHARE_ROWS, cols))
        copies.append(pltpu.make_async_copy(images.at[slot], images_out.at[where[slot]], out_sems.at[2 + slot]))
        copies[-1].start()
    for copy in copies:
        copy.wait()


def combine_kernel(sums, images, grad, hess, refl_out, moved_out):
    n_src, height = images.shape[0], (images.shape[1] - SHARE_ROWS) // 2
    total = jnp.sum(sums[...], axis=1, keepdims=True)
    gg, qq, gh, hh, qw, ww = [total[i : i + 1] for i in range(6)]
    step0 = gg / qq
    grad_next = gg - 2 * step0 * gh + step0 * step0 * hh
    near = 1 + grad_next / gg
    image_sq = near * near * qq - 2 * near * step0 * qw + step0 * step0 * ww
    step1 = grad_next / image_sq
    c1 = step0 + step1 * near
    c2 = -step0 * step1
    for i in range(grad.shape[0]):
        refl_out[i] = c1 * grad[i] + c2 * hess[i]
    for s in range(n_src):
        share = images[s, 2 * height :].astype(jnp.float32)[:1, :1]
        first = images[s, :height].astype(jnp.float32)
        rest = images[s, height : 2 * height].astype(jnp.float32)
        moved_out[s] = (c1 + c2 * share) * first + c2 * rest


def summed(x, axis, count):
    if count & (count - 1):
        return lax.psum(x, axis)
    bit = 1
    while bit < count:
        x = x + lax.ppermute(x, axis, [(d, d ^ bit) for d in range(count)])
        bit *= 2
    return x


def per_device(n_rcv, n_src, pplus, pminus, band):
    blocks_here = band.shape[0]
    rows = BLOCK // n_src
    cols = 2 * pplus.shape[2]
    order = ring_order(n_src)
    ahead = [(order[p], order[(p + 1) % n_src]) for p in range(n_src)]
    behind = [(d, s) for s, d in ahead]

    def swaps(first):
        pairs = [(r, r + 1) for r in range(first, n_rcv - 1, 2)]
        return pairs + [(d, s) for s, d in pairs]

    start = lax.optimization_barrier(pminus.reshape(blocks_here * BLOCK, cols))
    start = jnp.transpose(start.reshape(blocks_here, n_src, rows, cols), (1, 0, 2, 3))
    field = lax.all_to_all(start.reshape(n_src, blocks_here * rows, cols), "src", 0, 0, tiled=True)

    own = pplus.reshape(blocks_here * BLOCK, cols)
    chunks, shifts = [own], [0]
    batches = [[0, 1, 2][:n_src]]
    fwd = bwd = own
    for step in range(1, n_src // 2 + 1):
        if step == 3:
            fwd, bwd, field = lax.optimization_barrier((fwd, bwd, field))
        if step > 1:
            batches.append(list(range(len(chunks), min(len(chunks) + 2, n_src))))
        fwd = lax.ppermute(fwd, "src", ahead)
        chunks.append(fwd)
        shifts.append(-step)
        if len(chunks) < n_src:
            bwd = lax.ppermute(bwd, "src", behind)
            chunks.append(bwd)
            shifts.append(step)
    joined = [jnp.concatenate([chunks[c] for c in batch], axis=0) for batch in batches]
    near, far = [], []
    for batch in joined:
        if far:
            batch, far[-1] = lax.optimization_barrier((batch, far[-1]))
        near.append(lax.ppermute(batch, "rcv", swaps(0)))
        far.append(lax.ppermute(batch, "rcv", swaps(1)))
    me = jnp.stack([lax.axis_index("rcv"), lax.axis_index("src")]).astype(jnp.int32)

    any_spec = pl.BlockSpec(memory_space=pl.ANY)
    smem, vmem = pl.BlockSpec(memory_space=pltpu.SMEM), pl.BlockSpec(memory_space=pltpu.VMEM)
    band_cols = NEIGH * BLOCK
    need = 2 * blocks_here * band_cols * n_src * cols + (16 << 20)
    grad, hess, images, sums = pl.pallas_call(
        functools.partial(maps_kernel, n_src, shifts, batches),
        out_shape=(
            jax.ShapeDtypeStruct((blocks_here, 2 * rows, band_cols), jnp.float32),
            jax.ShapeDtypeStruct((blocks_here, 2 * rows, band_cols), jnp.float32),
            jax.ShapeDtypeStruct((n_src, 2 * blocks_here * rows + SHARE_ROWS, cols), jnp.bfloat16),
            jax.ShapeDtypeStruct((8, 128), jnp.float32),
        ),
        in_specs=[smem, smem, vmem] + [any_spec] * (n_src + 2 * len(batches)),
        out_specs=[any_spec] * 3 + [vmem],
        scratch_shapes=[
            pltpu.VMEM((blocks_here, band_cols, n_src * cols), jnp.bfloat16),
            pltpu.VMEM((blocks_here * 2 * rows, n_src * cols), jnp.bfloat16),
            pltpu.VMEM((n_src, blocks_here * rows, cols), jnp.float32),
            pltpu.VMEM((n_src, blocks_here * rows, cols), jnp.float32),
            pltpu.VMEM((blocks_here, 2 * rows, band_cols), jnp.float32),
            pltpu.VMEM((blocks_here, 2 * rows, band_cols), jnp.float32),
            pltpu.VMEM((n_src, 2 * blocks_here * rows + SHARE_ROWS, cols), jnp.bfloat16),
            pltpu.SemaphoreType.DMA((n_src,)),
            pltpu.SemaphoreType.DMA((2 + n_src,)),
        ],
        compiler_params=pltpu.CompilerParams(vmem_limit_bytes=min(need, 56 << 20)),
        name="maps",
    )(me, band, field, *chunks, *near, *far)

    sums = summed(sums, "rcv", n_rcv)
    images, sums = lax.optimization_barrier((images, sums))
    images = lax.all_to_all(images, "src", 0, 0, tiled=True)
    sums = summed(sums, "src", n_src)
    refl, moved = pl.pallas_call(
        combine_kernel,
        out_shape=(
            jax.ShapeDtypeStruct(grad.shape, jnp.float32),
            jax.ShapeDtypeStruct((n_src, blocks_here * rows, cols), jnp.float32),
        ),
        in_specs=[vmem] * 4,
        out_specs=[vmem] * 2,
        compiler_params=pltpu.CompilerParams(vmem_limit_bytes=16 << 20),
        name="combine",
    )(sums, images, grad, hess)

    refl = jnp.transpose(refl.reshape(blocks_here, 2, rows, NEIGH, BLOCK), (2, 0, 3, 1, 4))
    moved = jnp.transpose(moved.reshape(n_src, blocks_here, rows, cols), (1, 0, 2, 3))
    misfit = pminus.astype(jnp.float32) - moved.reshape(pminus.shape)
    return refl, misfit


def solution(mesh):
    return jax.shard_map(
        functools.partial(per_device, mesh.shape["rcv"], mesh.shape["src"]),
        mesh=mesh,
        in_specs=(P("rcv", None, "src"), P("rcv", None, "src"), P("rcv", None)),
        out_specs=(P("src", "rcv", None, None, None), P("rcv", None, "src")),
        check_vma=False,
    )
```

```python
import functools

import jax
import jax.numpy as jnp
from jax import lax
from jax.experimental import pallas as pl
from jax.experimental.pallas import tpu as pltpu
from jax.sharding import PartitionSpec as P

BLOCK = 256
NEIGH = 3
HALO_BLK = 2
ROWS_X = 2
SHARE_ROWS = 16


def ring_order(count):
    if count % ROWS_X or count < 2 * ROWS_X:
        return list(range(count))
    half = count // ROWS_X
    return [ROWS_X * p for p in range(half)] + [ROWS_X * p + 1 for p in reversed(range(half))]


def ring_place(count, index, shift):
    if count % ROWS_X or count < 2 * ROWS_X:
        return lax.rem(index + shift + count, count)
    half, odd = count // ROWS_X, lax.rem(index, ROWS_X)
    step = (index - odd) // ROWS_X
    place = lax.rem(jnp.where(odd == 1, count - 1 - step, step) + shift + count, count)
    return jnp.where(place < half, ROWS_X * place, ROWS_X * (count - 1 - place) + 1)


def along(sums):
    total = jnp.sum(sums, axis=1, keepdims=True)
    qq, qw = total[1:2], total[4:5]
    return jnp.where(qq > 0, qw / jnp.where(qq > 0, qq, 1.0), 0.0)


def maps_kernel(n_src, shifts, batches, *refs):
    me, band, field = refs[:3]
    ends = [3, 3 + n_src, 3 + n_src + len(batches), 3 + n_src + 2 * len(batches)]
    own, near, far = [refs[a:b] for a, b in zip(ends[:-1], ends[1:])]
    grad_out, hess_out, images_out, sums_out = refs[ends[3] : ends[3] + 4]
    panel, lhs, image0, image1, grad, hess, images, sems, out_sems = refs[ends[3] + 4 :]
    blocks_here = panel.shape[0]
    rows = lhs.shape[0] // (2 * blocks_here)
    cols = field.shape[2]
    half = cols // 2
    me_rcv, me_src = me[0], me[1]
    odd = lax.rem(me_rcv, 2)
    where = [ring_place(n_src, me_src, shift) for shift in shifts]

    for i in range(blocks_here):
        for k in range(NEIGH):
            offset = band[i, k] - me_rcv * blocks_here
            here = (offset >= 0) & (offset < blocks_here)
            toward = jnp.where(offset < 0, 1, 0)
            inside = jnp.where(offset < 0, offset + HALO_BLK, jnp.where(here, offset, offset - blocks_here))
            start = pl.multiple_of(inside * BLOCK, BLOCK)

            def fetch(arrays, groups, i=i, k=k, start=start):
                for array, group in zip(arrays, groups):
                    for place, slot in enumerate(group):
                        pltpu.make_async_copy(
                            array.at[pl.ds(start + place * blocks_here * BLOCK, BLOCK), :],
                            panel.at[i, pl.ds(k * BLOCK, BLOCK), pl.ds(slot * cols, cols)],
                            sems.at[slot],
                        ).start()

            @pl.when(here)
            def _():
                fetch(own, [[slot] for slot in range(n_src)])

            @pl.when(jnp.logical_not(here) & (toward == odd))
            def _():
                fetch(near, batches)

            @pl.when(jnp.logical_not(here) & (toward != odd))
            def _():
                fetch(far, batches)

    def store(i, slot, re_bf, im_bf):
        top, low = slice(2 * i * rows, (2 * i + 1) * rows), slice((2 * i + 1) * rows, (2 * i + 2) * rows)
        left, right = slice(slot * cols, slot * cols + half), slice(slot * cols + half, (slot + 1) * cols)
        lhs[top, left] = re_bf
        lhs[top, right] = im_bf
        lhs[low, left] = im_bf
        lhs[low, right] = -re_bf

    for slot in range(n_src):
        for i in range(blocks_here):
            rows_bf = field[where[slot], i * rows : (i + 1) * rows, :]
            store(i, slot, rows_bf[:, :half], rows_bf[:, half:])

    def arrived(slots):
        for slot in slots:
            for i in range(blocks_here):
                for k in range(NEIGH):
                    pltpu.make_async_copy(
                        own[slot].at[pl.ds(0, BLOCK), :],
                        panel.at[i, pl.ds(k * BLOCK, BLOCK), pl.ds(slot * cols, cols)],
                        sems.at[slot],
                    ).wait()

    def fold(x):
        total = x[:, :128]
        for c in range(128, x.shape[1], 128):
            total = total + x[:, c : c + 128]
        return jnp.sum(total, axis=0, keepdims=True)

    def adjoint(i, first=0, last=n_src):
        part = slice(first * cols, last * cols)
        mine = slice(2 * i * rows, 2 * (i + 1) * rows)
        return lax.dot_general(
            lhs[mine, part], panel[i, :, part], (((1,), (1,)), ((), ())), preferred_element_type=jnp.float32
        )

    def forward(i, x_bf, slot):
        prod = jnp.dot(
            x_bf, panel[i, :, slot * cols : (slot + 1) * cols], preferred_element_type=jnp.float32
        )
        return prod[:rows, :half] - prod[rows:, half:], prod[:rows, half:] + prod[rows:, :half]

    zero = jnp.zeros((1, 128), jnp.float32)
    gg, qq, gh, hh, qw, ww = zero, zero, zero, zero, zero, zero
    middle = (n_src + 1) // 2
    arrived(range(middle))
    for i in range(blocks_here):
        grad[i] = adjoint(i, 0, middle)
    arrived(range(middle, n_src))
    for i in range(blocks_here):
        grad[i] += adjoint(i, middle, n_src)
    grad_copy = pltpu.make_async_copy(grad, grad_out, out_sems.at[0])
    grad_copy.start()
    for i in range(blocks_here):
        mine = slice(i * rows, (i + 1) * rows)
        g0 = grad[i]
        gg += fold(g0 * g0)
        g_bf = g0.astype(jnp.bfloat16)
        for slot in range(n_src):
            re, im = forward(i, g_bf, slot)
            qq += fold(re * re + im * im)
            image0[slot, mine, :half] = re
            image0[slot, mine, half:] = im
            store(i, slot, re.astype(jnp.bfloat16), im.astype(jnp.bfloat16))
    for i in range(blocks_here):
        mine = slice(i * rows, (i + 1) * rows)
        h0 = adjoint(i)
        hess[i] = h0
        gh += fold(h0 * grad[i])
        hh += fold(h0 * h0)
        h_bf = h0.astype(jnp.bfloat16)
        for slot in range(n_src):
            re, im = forward(i, h_bf, slot)
            ww += fold(re * re + im * im)
            qw += fold(re * image0[slot, mine, :half] + im * image0[slot, mine, half:])
            image1[slot, mine, :half] = re
            image1[slot, mine, half:] = im
    sums = jnp.concatenate([gg, qq, gh, hh, qw, ww, zero, zero], axis=0)
    sums_out[...] = sums
    hess_copy = pltpu.make_async_copy(hess, hess_out, out_sems.at[1])
    hess_copy.start()
    share_bf = along(sums).astype(jnp.bfloat16)
    share = share_bf.astype(jnp.float32)
    height = blocks_here * rows
    copies = [grad_copy, hess_copy]
    for slot in range(n_src):
        first = image0[slot]
        images[slot, :height] = first.astype(jnp.bfloat16)
        images[slot, height : 2 * height] = (image1[slot] - share * first).astype(jnp.bfloat16)
        images[slot, 2 * height :] = jnp.broadcast_to(share_bf, (SHARE_ROWS, cols))
        copies.append(pltpu.make_async_copy(images.at[slot], images_out.at[where[slot]], out_sems.at[2 + slot]))
        copies[-1].start()
    for copy in copies:
        copy.wait()


def combine_kernel(sums, images, grad, hess, refl_out, moved_out):
    n_src, height = images.shape[0], (images.shape[1] - SHARE_ROWS) // 2
    total = jnp.sum(sums[...], axis=1, keepdims=True)
    gg, qq, gh, hh, qw, ww = [total[i : i + 1] for i in range(6)]
    step0 = gg / qq
    grad_next = gg - 2 * step0 * gh + step0 * step0 * hh
    near = 1 + grad_next / gg
    image_sq = near * near * qq - 2 * near * step0 * qw + step0 * step0 * ww
    step1 = grad_next / image_sq
    c1 = step0 + step1 * near
    c2 = -step0 * step1
    for i in range(grad.shape[0]):
        refl_out[i] = c1 * grad[i] + c2 * hess[i]
    for s in range(n_src):
        share = images[s, 2 * height :].astype(jnp.float32)[:1, :1]
        first = images[s, :height].astype(jnp.float32)
        rest = images[s, height : 2 * height].astype(jnp.float32)
        moved_out[s] = (c1 + c2 * share) * first + c2 * rest


def summed(x, axis, count):
    if count & (count - 1):
        return lax.psum(x, axis)
    bit = 1
    while bit < count:
        radix = min(4, count // bit)
        others = [lax.ppermute(x, axis, [(d, d ^ (bit * m)) for d in range(count)]) for m in range(1, radix)]
        x = (x + others[0]) + (others[1] + others[2]) if radix == 4 else x + others[0]
        bit *= radix
    return x


def per_device(n_rcv, n_src, pplus, pminus, band):
    blocks_here = band.shape[0]
    rows = BLOCK // n_src
    cols = 2 * pplus.shape[2]
    order = ring_order(n_src)
    ahead = [(order[p], order[(p + 1) % n_src]) for p in range(n_src)]
    behind = [(d, s) for s, d in ahead]

    def swaps(first):
        pairs = [(r, r + 1) for r in range(first, n_rcv - 1, 2)]
        return pairs + [(d, s) for s, d in pairs]

    start = lax.optimization_barrier(pminus.reshape(blocks_here * BLOCK, cols))
    start = jnp.transpose(start.reshape(blocks_here, n_src, rows, cols), (1, 0, 2, 3))
    field = lax.all_to_all(start.reshape(n_src, blocks_here * rows, cols), "src", 0, 0, tiled=True)

    own = pplus.reshape(blocks_here * BLOCK, cols)
    chunks, shifts = [own], [0]
    fwd = bwd = own
    for step in range(1, n_src // 2 + 1):
        if step == 3:
            fwd, bwd, field = lax.optimization_barrier((fwd, bwd, field))
        fwd = lax.ppermute(fwd, "src", ahead)
        chunks.append(fwd)
        shifts.append(-step)
        if len(chunks) < n_src:
            bwd = lax.ppermute(bwd, "src", behind)
            chunks.append(bwd)
            shifts.append(step)
    near = [lax.ppermute(c, "rcv", swaps(0)) for c in chunks]
    far = [lax.ppermute(c, "rcv", swaps(1)) for c in chunks]
    batches = [[c] for c in range(n_src)]
    me = jnp.stack([lax.axis_index("rcv"), lax.axis_index("src")]).astype(jnp.int32)

    any_spec = pl.BlockSpec(memory_space=pl.ANY)
    smem, vmem = pl.BlockSpec(memory_space=pltpu.SMEM), pl.BlockSpec(memory_space=pltpu.VMEM)
    band_cols = NEIGH * BLOCK
    need = 2 * blocks_here * band_cols * n_src * cols + (16 << 20)
    grad, hess, images, sums = pl.pallas_call(
        functools.partial(maps_kernel, n_src, shifts, batches),
        out_shape=(
            jax.ShapeDtypeStruct((blocks_here, 2 * rows, band_cols), jnp.float32),
            jax.ShapeDtypeStruct((blocks_here, 2 * rows, band_cols), jnp.float32),
            jax.ShapeDtypeStruct((n_src, 2 * blocks_here * rows + SHARE_ROWS, cols), jnp.bfloat16),
            jax.ShapeDtypeStruct((8, 128), jnp.float32),
        ),
        in_specs=[smem, smem, vmem] + [any_spec] * (n_src + 2 * len(batches)),
        out_specs=[any_spec] * 3 + [vmem],
        scratch_shapes=[
            pltpu.VMEM((blocks_here, band_cols, n_src * cols), jnp.bfloat16),
            pltpu.VMEM((blocks_here * 2 * rows, n_src * cols), jnp.bfloat16),
            pltpu.VMEM((n_src, blocks_here * rows, cols), jnp.float32),
            pltpu.VMEM((n_src, blocks_here * rows, cols), jnp.float32),
            pltpu.VMEM((blocks_here, 2 * rows, band_cols), jnp.float32),
            pltpu.VMEM((blocks_here, 2 * rows, band_cols), jnp.float32),
            pltpu.VMEM((n_src, 2 * blocks_here * rows + SHARE_ROWS, cols), jnp.bfloat16),
            pltpu.SemaphoreType.DMA((n_src,)),
            pltpu.SemaphoreType.DMA((2 + n_src,)),
        ],
        compiler_params=pltpu.CompilerParams(vmem_limit_bytes=min(need, 56 << 20)),
        name="maps",
    )(me, band, field, *chunks, *near, *far)

    images = lax.all_to_all(images, "src", 0, 0, tiled=True)
    sums = summed(summed(sums, "rcv", n_rcv), "src", n_src)
    refl, moved = pl.pallas_call(
        combine_kernel,
        out_shape=(
            jax.ShapeDtypeStruct(grad.shape, jnp.float32),
            jax.ShapeDtypeStruct((n_src, blocks_here * rows, cols), jnp.float32),
        ),
        in_specs=[vmem] * 4,
        out_specs=[vmem] * 2,
        compiler_params=pltpu.CompilerParams(vmem_limit_bytes=16 << 20),
        name="combine",
    )(sums, images, grad, hess)

    refl = jnp.transpose(refl.reshape(blocks_here, 2, rows, NEIGH, BLOCK), (2, 0, 3, 1, 4))
    moved = jnp.transpose(moved.reshape(n_src, blocks_here, rows, cols), (1, 0, 2, 3))
    misfit = pminus.astype(jnp.float32) - moved.reshape(pminus.shape)
    return refl, misfit


def solution(mesh):
    return jax.shard_map(
        functools.partial(per_device, mesh.shape["rcv"], mesh.shape["src"]),
        mesh=mesh,
        in_specs=(P("rcv", None, "src"), P("rcv", None, "src"), P("rcv", None)),
        out_specs=(P("src", "rcv", None, None, None), P("rcv", None, "src")),
        check_vma=False,
    )
```

```python
import functools

import jax
import jax.numpy as jnp
from jax import lax
from jax.experimental import pallas as pl
from jax.experimental.pallas import tpu as pltpu
from jax.sharding import PartitionSpec as P

BLOCK = 256
NEIGH = 3
HALO_BLK = 2
ROWS_X = 2
SHARE_ROWS = 16


def ring_order(count):
    if count % ROWS_X or count < 2 * ROWS_X:
        return list(range(count))
    half = count // ROWS_X
    return [ROWS_X * p for p in range(half)] + [ROWS_X * p + 1 for p in reversed(range(half))]


def ring_place(count, index, shift):
    if count % ROWS_X or count < 2 * ROWS_X:
        return lax.rem(index + shift + count, count)
    half, odd = count // ROWS_X, lax.rem(index, ROWS_X)
    step = (index - odd) // ROWS_X
    place = lax.rem(jnp.where(odd == 1, count - 1 - step, step) + shift + count, count)
    return jnp.where(place < half, ROWS_X * place, ROWS_X * (count - 1 - place) + 1)


def along(sums):
    total = jnp.sum(sums, axis=1, keepdims=True)
    qq, qw = total[1:2], total[4:5]
    return jnp.where(qq > 0, qw / jnp.where(qq > 0, qq, 1.0), 0.0)


def maps_kernel(n_src, shifts, *refs):
    me, band, field = refs[:3]
    ends = [3, 3 + n_src, 3 + 2 * n_src, 3 + 3 * n_src]
    own, near, far = [refs[a:b] for a, b in zip(ends[:-1], ends[1:])]
    grad, hess, images, sums_out = refs[ends[3] : ends[3] + 4]
    panel, lhs, image0, image1, sems = refs[ends[3] + 4 :]
    blocks_here = panel.shape[0]
    rows = lhs.shape[0] // (2 * blocks_here)
    cols = field.shape[2]
    half = cols // 2
    me_rcv, me_src = me[0], me[1]
    odd = lax.rem(me_rcv, 2)
    where = [ring_place(n_src, me_src, shift) for shift in shifts]

    for i in range(blocks_here):
        for k in range(NEIGH):
            offset = band[i, k] - me_rcv * blocks_here
            here = (offset >= 0) & (offset < blocks_here)
            toward = jnp.where(offset < 0, 1, 0)
            inside = jnp.where(offset < 0, offset + HALO_BLK, jnp.where(here, offset, offset - blocks_here))
            start = pl.multiple_of(inside * BLOCK, BLOCK)

            def fetch(group, i=i, k=k, start=start):
                for slot in range(n_src):
                    pltpu.make_async_copy(
                        group[slot].at[pl.ds(start, BLOCK), :],
                        panel.at[i, pl.ds(k * BLOCK, BLOCK), pl.ds(slot * cols, cols)],
                        sems.at[slot],
                    ).start()

            @pl.when(here)
            def _():
                fetch(own)

            @pl.when(jnp.logical_not(here) & (toward == odd))
            def _():
                fetch(near)

            @pl.when(jnp.logical_not(here) & (toward != odd))
            def _():
                fetch(far)

    def store(i, slot, re_bf, im_bf):
        top, low = slice(2 * i * rows, (2 * i + 1) * rows), slice((2 * i + 1) * rows, (2 * i + 2) * rows)
        left, right = slice(slot * cols, slot * cols + half), slice(slot * cols + half, (slot + 1) * cols)
        lhs[top, left] = re_bf
        lhs[top, right] = im_bf
        lhs[low, left] = im_bf
        lhs[low, right] = -re_bf

    for slot in range(n_src):
        for i in range(blocks_here):
            rows_bf = field[where[slot], i * rows : (i + 1) * rows, :]
            store(i, slot, rows_bf[:, :half], rows_bf[:, half:])

    def arrived(slots):
        for slot in slots:
            for i in range(blocks_here):
                for k in range(NEIGH):
                    pltpu.make_async_copy(
                        own[slot].at[pl.ds(0, BLOCK), :],
                        panel.at[i, pl.ds(k * BLOCK, BLOCK), pl.ds(slot * cols, cols)],
                        sems.at[slot],
                    ).wait()

    def fold(x):
        total = x[:, :128]
        for c in range(128, x.shape[1], 128):
            total = total + x[:, c : c + 128]
        return jnp.sum(total, axis=0, keepdims=True)

    def adjoint(i, first=0, last=n_src):
        part = slice(first * cols, last * cols)
        mine = slice(2 * i * rows, 2 * (i + 1) * rows)
        return lax.dot_general(
            lhs[mine, part], panel[i, :, part], (((1,), (1,)), ((), ())), preferred_element_type=jnp.float32
        )

    def forward(i, x_bf, slot):
        prod = jnp.dot(
            x_bf, panel[i, :, slot * cols : (slot + 1) * cols], preferred_element_type=jnp.float32
        )
        return prod[:rows, :half] - prod[rows:, half:], prod[:rows, half:] + prod[rows:, :half]

    zero = jnp.zeros((1, 128), jnp.float32)
    gg, qq, gh, hh, qw, ww = zero, zero, zero, zero, zero, zero
    middle = (n_src + 1) // 2
    arrived(range(middle))
    for i in range(blocks_here):
        grad[i] = adjoint(i, 0, middle)
    arrived(range(middle, n_src))
    for i in range(blocks_here):
        grad[i] += adjoint(i, middle, n_src)
    for i in range(blocks_here):
        mine = slice(i * rows, (i + 1) * rows)
        g0 = grad[i]
        gg += fold(g0 * g0)
        g_bf = g0.astype(jnp.bfloat16)
        for slot in range(n_src):
            re, im = forward(i, g_bf, slot)
            qq += fold(re * re + im * im)
            image0[slot, mine, :half] = re
            image0[slot, mine, half:] = im
            store(i, slot, re.astype(jnp.bfloat16), im.astype(jnp.bfloat16))
    for i in range(blocks_here):
        mine = slice(i * rows, (i + 1) * rows)
        h0 = adjoint(i)
        hess[i] = h0
        gh += fold(h0 * grad[i])
        hh += fold(h0 * h0)
        h_bf = h0.astype(jnp.bfloat16)
        for slot in range(n_src):
            re, im = forward(i, h_bf, slot)
            ww += fold(re * re + im * im)
            qw += fold(re * image0[slot, mine, :half] + im * image0[slot, mine, half:])
            image1[slot, mine, :half] = re
            image1[slot, mine, half:] = im
    sums = jnp.concatenate([gg, qq, gh, hh, qw, ww, zero, zero], axis=0)
    sums_out[...] = sums
    share_bf = along(sums).astype(jnp.bfloat16)
    share = share_bf.astype(jnp.float32)
    height = blocks_here * rows
    for slot in range(n_src):
        first = image0[slot]
        images[where[slot], :height] = first.astype(jnp.bfloat16)
        images[where[slot], height : 2 * height] = (image1[slot] - share * first).astype(jnp.bfloat16)
        images[where[slot], 2 * height :] = jnp.broadcast_to(share_bf, (SHARE_ROWS, cols))


def combine_kernel(sums, images, grad, hess, refl_out, moved_out):
    n_src, height = images.shape[0], (images.shape[1] - SHARE_ROWS) // 2
    total = jnp.sum(sums[...], axis=1, keepdims=True)
    gg, qq, gh, hh, qw, ww = [total[i : i + 1] for i in range(6)]
    step0 = gg / qq
    grad_next = gg - 2 * step0 * gh + step0 * step0 * hh
    near = 1 + grad_next / gg
    image_sq = near * near * qq - 2 * near * step0 * qw + step0 * step0 * ww
    step1 = grad_next / image_sq
    c1 = step0 + step1 * near
    c2 = -step0 * step1
    for i in range(grad.shape[0]):
        refl_out[i] = c1 * grad[i] + c2 * hess[i]
    for s in range(n_src):
        share = images[s, 2 * height :].astype(jnp.float32)[:1, :1]
        first = images[s, :height].astype(jnp.float32)
        rest = images[s, height : 2 * height].astype(jnp.float32)
        moved_out[s] = (c1 + c2 * share) * first + c2 * rest


def summed(x, axis, count):
    if count & (count - 1):
        return lax.psum(x, axis)
    bit = 1
    while bit < count:
        radix = min(4, count // bit)
        others = [lax.ppermute(x, axis, [(d, d ^ (bit * m)) for d in range(count)]) for m in range(1, radix)]
        x = (x + others[0]) + (others[1] + others[2]) if radix == 4 else x + others[0]
        bit *= radix
    return x


def per_device(n_rcv, n_src, pplus, pminus, band):
    blocks_here = band.shape[0]
    rows = BLOCK // n_src
    cols = 2 * pplus.shape[2]
    order = ring_order(n_src)
    ahead = [(order[p], order[(p + 1) % n_src]) for p in range(n_src)]
    behind = [(d, s) for s, d in ahead]

    def swaps(first):
        pairs = [(r, r + 1) for r in range(first, n_rcv - 1, 2)]
        return pairs + [(d, s) for s, d in pairs]

    start = lax.optimization_barrier(pminus.reshape(blocks_here * BLOCK, cols))
    start = jnp.transpose(start.reshape(blocks_here, n_src, rows, cols), (1, 0, 2, 3))
    field = lax.all_to_all(start.reshape(n_src, blocks_here * rows, cols), "src", 0, 0, tiled=True)

    own = pplus.reshape(blocks_here * BLOCK, cols)
    chunks, shifts = [own], [0]
    fwd = bwd = own
    for step in range(1, n_src // 2 + 1):
        fwd = lax.ppermute(fwd, "src", ahead)
        chunks.append(fwd)
        shifts.append(-step)
        if len(chunks) < n_src:
            bwd = lax.ppermute(bwd, "src", behind)
            chunks.append(bwd)
            shifts.append(step)
    near = [lax.ppermute(c, "rcv", swaps(0)) for c in chunks]
    far = [lax.ppermute(c, "rcv", swaps(1)) for c in chunks]
    me = jnp.stack([lax.axis_index("rcv"), lax.axis_index("src")]).astype(jnp.int32)

    any_spec = pl.BlockSpec(memory_space=pl.ANY)
    smem, vmem = pl.BlockSpec(memory_space=pltpu.SMEM), pl.BlockSpec(memory_space=pltpu.VMEM)
    band_cols = NEIGH * BLOCK
    need = 2 * blocks_here * band_cols * n_src * cols + (16 << 20)
    grad, hess, images, sums = pl.pallas_call(
        functools.partial(maps_kernel, n_src, shifts),
        out_shape=(
            jax.ShapeDtypeStruct((blocks_here, 2 * rows, band_cols), jnp.float32),
            jax.ShapeDtypeStruct((blocks_here, 2 * rows, band_cols), jnp.float32),
            jax.ShapeDtypeStruct((n_src, 2 * blocks_here * rows + SHARE_ROWS, cols), jnp.bfloat16),
            jax.ShapeDtypeStruct((8, 128), jnp.float32),
        ),
        in_specs=[smem, smem, vmem] + [any_spec] * (3 * n_src),
        out_specs=[vmem] * 4,
        scratch_shapes=[
            pltpu.VMEM((blocks_here, band_cols, n_src * cols), jnp.bfloat16),
            pltpu.VMEM((blocks_here * 2 * rows, n_src * cols), jnp.bfloat16),
            pltpu.VMEM((n_src, blocks_here * rows, cols), jnp.float32),
            pltpu.VMEM((n_src, blocks_here * rows, cols), jnp.float32),
            pltpu.SemaphoreType.DMA((n_src,)),
        ],
        compiler_params=pltpu.CompilerParams(vmem_limit_bytes=min(need, 56 << 20)),
        name="maps",
    )(me, band, field, *chunks, *near, *far)

    images = lax.all_to_all(images, "src", 0, 0, tiled=True)
    sums = summed(summed(sums, "rcv", n_rcv), "src", n_src)
    refl, moved = pl.pallas_call(
        combine_kernel,
        out_shape=(
            jax.ShapeDtypeStruct(grad.shape, jnp.float32),
            jax.ShapeDtypeStruct((n_src, blocks_here * rows, cols), jnp.float32),
        ),
        in_specs=[vmem] * 4,
        out_specs=[vmem] * 2,
        compiler_params=pltpu.CompilerParams(vmem_limit_bytes=16 << 20),
        name="combine",
    )(sums, images, grad, hess)

    refl = jnp.transpose(refl.reshape(blocks_here, 2, rows, NEIGH, BLOCK), (2, 0, 3, 1, 4))
    moved = jnp.transpose(moved.reshape(n_src, blocks_here, rows, cols), (1, 0, 2, 3))
    misfit = pminus.astype(jnp.float32) - moved.reshape(pminus.shape)
    return refl, misfit


def solution(mesh):
    return jax.shard_map(
        functools.partial(per_device, mesh.shape["rcv"], mesh.shape["src"]),
        mesh=mesh,
        in_specs=(P("rcv", None, "src"), P("rcv", None, "src"), P("rcv", None)),
        out_specs=(P("src", "rcv", None, None, None), P("rcv", None, "src")),
        check_vma=False,
    )
```

```python
import functools

import jax
import jax.numpy as jnp
from jax import lax
from jax.experimental import pallas as pl
from jax.experimental.pallas import tpu as pltpu
from jax.sharding import PartitionSpec as P

BLOCK = 256
NEIGH = 3
HALO_BLK = 2
ROWS_X = 2
SHARE_ROWS = 16


def ring_order(count):
    if count % ROWS_X or count < 2 * ROWS_X:
        return list(range(count))
    half = count // ROWS_X
    return [ROWS_X * p for p in range(half)] + [ROWS_X * p + 1 for p in reversed(range(half))]


def ring_place(count, index, shift):
    if count % ROWS_X or count < 2 * ROWS_X:
        return lax.rem(index + shift + count, count)
    half, odd = count // ROWS_X, lax.rem(index, ROWS_X)
    step = (index - odd) // ROWS_X
    place = lax.rem(jnp.where(odd == 1, count - 1 - step, step) + shift + count, count)
    return jnp.where(place < half, ROWS_X * place, ROWS_X * (count - 1 - place) + 1)


def along(sums):
    total = jnp.sum(sums, axis=1, keepdims=True)
    qq, qw = total[1:2], total[4:5]
    return jnp.where(qq > 0, qw / jnp.where(qq > 0, qq, 1.0), 0.0)


def maps_kernel(n_src, shifts, *refs):
    me, band, field = refs[:3]
    ends = [3, 3 + n_src, 3 + 2 * n_src, 3 + 3 * n_src]
    groups = [refs[a:b] for a, b in zip(ends[:-1], ends[1:])]
    grad, hess, images, sums_out = refs[ends[3] : ends[3] + 4]
    lhs, every, factors, image0, image1 = refs[ends[3] + 4 :]
    blocks_here = grad.shape[0]
    rows = grad.shape[1] // 2
    cols = field.shape[2]
    half = cols // 2
    window = blocks_here * len(groups)
    me_rcv, me_src = me[0], me[1]
    odd = lax.rem(me_rcv, 2)
    where = [ring_place(n_src, me_src, shift) for shift in shifts]

    places = {}
    for i in range(blocks_here):
        for k in range(NEIGH):
            offset = band[i, k] - me_rcv * blocks_here
            before, here = offset < 0, (offset >= 0) & (offset < blocks_here)
            group = jnp.where(here, 0, jnp.where(jnp.where(before, 1, 0) == odd, 1, 2))
            inside = jnp.where(before, offset + blocks_here, jnp.where(here, offset, offset - blocks_here))
            places[i, k] = group * blocks_here + inside

    def block(place, slot):
        start = place % blocks_here * BLOCK
        return groups[place // blocks_here][slot][start : start + BLOCK, :]

    def store(i, slot, re_bf, im_bf):
        top, low = slice(2 * i * rows, (2 * i + 1) * rows), slice((2 * i + 1) * rows, (2 * i + 2) * rows)
        left, right = slice(slot * cols, slot * cols + half), slice(slot * cols + half, (slot + 1) * cols)
        lhs[top, left] = re_bf
        lhs[top, right] = im_bf
        lhs[low, left] = im_bf
        lhs[low, right] = -re_bf

    def fold(x):
        total = x[:, :128]
        for c in range(128, x.shape[1], 128):
            total = total + x[:, c : c + 128]
        return jnp.sum(total, axis=0, keepdims=True)

    def adjoint(out):
        for place in range(window):
            row = jnp.concatenate([block(place, slot) for slot in range(n_src)], axis=1)
            every[place] = lax.dot_general(
                lhs[...], row, (((1,), (1,)), ((), ())), preferred_element_type=jnp.float32
            )
        for i in range(blocks_here):
            mine = slice(2 * i * rows, 2 * (i + 1) * rows)
            for k in range(NEIGH):
                part = every[places[i, k], mine, :]
                out[i, :, k * BLOCK : (k + 1) * BLOCK] = part
                factors[places[i, k], mine, :] = part.astype(jnp.bfloat16)

    def forward(slot):
        column = jnp.concatenate([block(place, slot) for place in range(window)], axis=0)
        wide = jnp.concatenate([factors[place] for place in range(window)], axis=1)
        prod = jnp.dot(wide, column, preferred_element_type=jnp.float32)
        for i in range(blocks_here):
            top, low = prod[2 * i * rows : (2 * i + 1) * rows], prod[(2 * i + 1) * rows : 2 * (i + 1) * rows]
            yield i, top[:, :half] - low[:, half:], top[:, half:] + low[:, :half]

    factors[...] = jnp.zeros_like(factors)
    for slot in range(n_src):
        for i in range(blocks_here):
            rows_bf = field[where[slot], i * rows : (i + 1) * rows, :]
            store(i, slot, rows_bf[:, :half], rows_bf[:, half:])

    zero = jnp.zeros((1, 128), jnp.float32)
    gg, qq, gh, hh, qw, ww = zero, zero, zero, zero, zero, zero
    adjoint(grad)
    for i in range(blocks_here):
        gg += fold(grad[i] * grad[i])
    for slot in range(n_src):
        for i, re, im in forward(slot):
            mine = slice(i * rows, (i + 1) * rows)
            qq += fold(re * re + im * im)
            image0[slot, mine, :half] = re
            image0[slot, mine, half:] = im
            store(i, slot, re.astype(jnp.bfloat16), im.astype(jnp.bfloat16))
    adjoint(hess)
    for i in range(blocks_here):
        gh += fold(hess[i] * grad[i])
        hh += fold(hess[i] * hess[i])
    for slot in range(n_src):
        for i, re, im in forward(slot):
            mine = slice(i * rows, (i + 1) * rows)
            ww += fold(re * re + im * im)
            qw += fold(re * image0[slot, mine, :half] + im * image0[slot, mine, half:])
            image1[slot, mine, :half] = re
            image1[slot, mine, half:] = im
    sums = jnp.concatenate([gg, qq, gh, hh, qw, ww, zero, zero], axis=0)
    sums_out[...] = sums
    share_bf = along(sums).astype(jnp.bfloat16)
    share = share_bf.astype(jnp.float32)
    height = blocks_here * rows
    for slot in range(n_src):
        first = image0[slot]
        images[where[slot], :height] = first.astype(jnp.bfloat16)
        images[where[slot], height : 2 * height] = (image1[slot] - share * first).astype(jnp.bfloat16)
        images[where[slot], 2 * height :] = jnp.broadcast_to(share_bf, (SHARE_ROWS, cols))


def combine_kernel(sums, images, grad, hess, refl_out, moved_out):
    n_src, height = images.shape[0], (images.shape[1] - SHARE_ROWS) // 2
    total = jnp.sum(sums[...], axis=1, keepdims=True)
    gg, qq, gh, hh, qw, ww = [total[i : i + 1] for i in range(6)]
    step0 = gg / qq
    grad_next = gg - 2 * step0 * gh + step0 * step0 * hh
    near = 1 + grad_next / gg
    image_sq = near * near * qq - 2 * near * step0 * qw + step0 * step0 * ww
    step1 = grad_next / image_sq
    c1 = step0 + step1 * near
    c2 = -step0 * step1
    for i in range(grad.shape[0]):
        refl_out[i] = c1 * grad[i] + c2 * hess[i]
    for s in range(n_src):
        share = images[s, 2 * height :].astype(jnp.float32)[:1, :1]
        first = images[s, :height].astype(jnp.float32)
        rest = images[s, height : 2 * height].astype(jnp.float32)
        moved_out[s] = (c1 + c2 * share) * first + c2 * rest


def summed(x, axis, count):
    if count & (count - 1):
        return lax.psum(x, axis)
    bit = 1
    while bit < count:
        radix = min(4, count // bit)
        others = [lax.ppermute(x, axis, [(d, d ^ (bit * m)) for d in range(count)]) for m in range(1, radix)]
        x = (x + others[0]) + (others[1] + others[2]) if radix == 4 else x + others[0]
        bit *= radix
    return x


def per_device(n_rcv, n_src, pplus, pminus, band):
    blocks_here = band.shape[0]
    rows = BLOCK // n_src
    cols = 2 * pplus.shape[2]
    order = ring_order(n_src)
    ahead = [(order[p], order[(p + 1) % n_src]) for p in range(n_src)]
    behind = [(d, s) for s, d in ahead]

    def swaps(first):
        pairs = [(r, r + 1) for r in range(first, n_rcv - 1, 2)]
        return pairs + [(d, s) for s, d in pairs]

    start = lax.optimization_barrier(pminus.reshape(blocks_here * BLOCK, cols))
    start = jnp.transpose(start.reshape(blocks_here, n_src, rows, cols), (1, 0, 2, 3))
    field = lax.all_to_all(start.reshape(n_src, blocks_here * rows, cols), "src", 0, 0, tiled=True)

    own = pplus.reshape(blocks_here * BLOCK, cols)
    chunks, shifts = [own], [0]
    fwd = bwd = own
    for step in range(1, n_src // 2 + 1):
        fwd = lax.ppermute(fwd, "src", ahead)
        chunks.append(fwd)
        shifts.append(-step)
        if len(chunks) < n_src:
            bwd = lax.ppermute(bwd, "src", behind)
            chunks.append(bwd)
            shifts.append(step)
    near = [lax.ppermute(c, "rcv", swaps(0)) for c in chunks]
    far = [lax.ppermute(c, "rcv", swaps(1)) for c in chunks]
    me = jnp.stack([lax.axis_index("rcv"), lax.axis_index("src")]).astype(jnp.int32)

    smem, vmem = pl.BlockSpec(memory_space=pltpu.SMEM), pl.BlockSpec(memory_space=pltpu.VMEM)
    band_cols = NEIGH * BLOCK
    grad, hess, images, sums = pl.pallas_call(
        functools.partial(maps_kernel, n_src, shifts),
        out_shape=(
            jax.ShapeDtypeStruct((blocks_here, 2 * rows, band_cols), jnp.float32),
            jax.ShapeDtypeStruct((blocks_here, 2 * rows, band_cols), jnp.float32),
            jax.ShapeDtypeStruct((n_src, 2 * blocks_here * rows + SHARE_ROWS, cols), jnp.bfloat16),
            jax.ShapeDtypeStruct((8, 128), jnp.float32),
        ),
        in_specs=[smem, smem] + [vmem] * (1 + 3 * n_src),
        out_specs=[vmem] * 4,
        scratch_shapes=[
            pltpu.VMEM((blocks_here * 2 * rows, n_src * cols), jnp.bfloat16),
            pltpu.VMEM((3 * blocks_here, blocks_here * 2 * rows, BLOCK), jnp.float32),
            pltpu.VMEM((3 * blocks_here, blocks_here * 2 * rows, BLOCK), jnp.bfloat16),
            pltpu.VMEM((n_src, blocks_here * rows, cols), jnp.float32),
            pltpu.VMEM((n_src, blocks_here * rows, cols), jnp.float32),
        ],
        compiler_params=pltpu.CompilerParams(vmem_limit_bytes=16 << 20),
        name="maps",
    )(me, band, *[pltpu.with_memory_space_constraint(x, pltpu.VMEM) for x in (field, *chunks, *near, *far)])

    images = lax.all_to_all(images, "src", 0, 0, tiled=True)
    sums = summed(summed(sums, "rcv", n_rcv), "src", n_src)
    refl, moved = pl.pallas_call(
        combine_kernel,
        out_shape=(
            jax.ShapeDtypeStruct(grad.shape, jnp.float32),
            jax.ShapeDtypeStruct((n_src, blocks_here * rows, cols), jnp.float32),
        ),
        in_specs=[vmem] * 4,
        out_specs=[vmem] * 2,
        compiler_params=pltpu.CompilerParams(vmem_limit_bytes=16 << 20),
        name="combine",
    )(sums, images, grad, hess)

    refl = jnp.transpose(refl.reshape(blocks_here, 2, rows, NEIGH, BLOCK), (2, 0, 3, 1, 4))
    moved = jnp.transpose(moved.reshape(n_src, blocks_here, rows, cols), (1, 0, 2, 3))
    misfit = pminus.astype(jnp.float32) - moved.reshape(pminus.shape)
    return refl, misfit


def solution(mesh):
    return jax.shard_map(
        functools.partial(per_device, mesh.shape["rcv"], mesh.shape["src"]),
        mesh=mesh,
        in_specs=(P("rcv", None, "src"), P("rcv", None, "src"), P("rcv", None)),
        out_specs=(P("src", "rcv", None, None, None), P("rcv", None, "src")),
        check_vma=False,
    )
```

```python
import functools

import jax
import jax.numpy as jnp
from jax import lax
from jax.experimental import pallas as pl
from jax.experimental.pallas import tpu as pltpu
from jax.sharding import PartitionSpec as P

BLOCK = 256
NEIGH = 3
HALO_BLK = 2
ROWS_X = 2
SHARE_ROWS = 16


def ring_order(count):
    if count % ROWS_X or count < 2 * ROWS_X:
        return list(range(count))
    half = count // ROWS_X
    return [ROWS_X * p for p in range(half)] + [ROWS_X * p + 1 for p in reversed(range(half))]


def ring_place(count, index, shift):
    if count % ROWS_X or count < 2 * ROWS_X:
        return lax.rem(index + shift + count, count)
    half, odd = count // ROWS_X, lax.rem(index, ROWS_X)
    step = (index - odd) // ROWS_X
    place = lax.rem(jnp.where(odd == 1, count - 1 - step, step) + shift + count, count)
    return jnp.where(place < half, ROWS_X * place, ROWS_X * (count - 1 - place) + 1)


def along(sums):
    total = jnp.sum(sums, axis=1, keepdims=True)
    qq, qw = total[1:2], total[4:5]
    return jnp.where(qq > 0, qw / jnp.where(qq > 0, qq, 1.0), 0.0)


def maps_kernel(n_src, shifts, *refs):
    me, band, field = refs[:3]
    ends = [3, 3 + n_src, 3 + 2 * n_src, 3 + 3 * n_src]
    groups = [refs[a:b] for a, b in zip(ends[:-1], ends[1:])]
    grad, hess, images, sums_out = refs[ends[3] : ends[3] + 4]
    lhs, every, factors, image0, image1 = refs[ends[3] + 4 :]
    blocks_here = grad.shape[0]
    rows = grad.shape[1] // 2
    cols = field.shape[2]
    half = cols // 2
    window = blocks_here * len(groups)
    me_rcv, me_src = me[0], me[1]
    odd = lax.rem(me_rcv, 2)
    where = [ring_place(n_src, me_src, shift) for shift in shifts]

    places = {}
    for i in range(blocks_here):
        for k in range(NEIGH):
            offset = band[i, k] - me_rcv * blocks_here
            before, here = offset < 0, (offset >= 0) & (offset < blocks_here)
            group = jnp.where(here, 0, jnp.where(jnp.where(before, 1, 0) == odd, 1, 2))
            inside = jnp.where(before, offset + blocks_here, jnp.where(here, offset, offset - blocks_here))
            places[i, k] = group * blocks_here + inside

    def block(place, slot):
        start = place % blocks_here * BLOCK
        return groups[place // blocks_here][slot][start : start + BLOCK, :]

    def store(i, slot, re_bf, im_bf):
        top, low = slice(2 * i * rows, (2 * i + 1) * rows), slice((2 * i + 1) * rows, (2 * i + 2) * rows)
        left, right = slice(slot * cols, slot * cols + half), slice(slot * cols + half, (slot + 1) * cols)
        lhs[top, left] = re_bf
        lhs[top, right] = im_bf
        lhs[low, left] = im_bf
        lhs[low, right] = -re_bf

    def fold(x):
        total = x[:, :128]
        for c in range(128, x.shape[1], 128):
            total = total + x[:, c : c + 128]
        return jnp.sum(total, axis=0, keepdims=True)

    def adjoint(out):
        for place in range(window):
            row = jnp.concatenate([block(place, slot) for slot in range(n_src)], axis=1)
            every[place] = lax.dot_general(
                lhs[...], row, (((1,), (1,)), ((), ())), preferred_element_type=jnp.float32
            )
        for i in range(blocks_here):
            mine = slice(2 * i * rows, 2 * (i + 1) * rows)
            for k in range(NEIGH):
                part = every[places[i, k], mine, :]
                out[i, :, k * BLOCK : (k + 1) * BLOCK] = part
                factors[places[i, k], mine, :] = part.astype(jnp.bfloat16)

    def forward(slot):
        column = jnp.concatenate([block(place, slot) for place in range(window)], axis=0)
        wide = jnp.concatenate([factors[place] for place in range(window)], axis=1)
        prod = jnp.dot(wide, column, preferred_element_type=jnp.float32)
        for i in range(blocks_here):
            top, low = prod[2 * i * rows : (2 * i + 1) * rows], prod[(2 * i + 1) * rows : 2 * (i + 1) * rows]
            yield i, top[:, :half] - low[:, half:], top[:, half:] + low[:, :half]

    factors[...] = jnp.zeros_like(factors)
    for slot in range(n_src):
        for i in range(blocks_here):
            rows_bf = field[where[slot], i * rows : (i + 1) * rows, :]
            store(i, slot, rows_bf[:, :half], rows_bf[:, half:])

    zero = jnp.zeros((1, 128), jnp.float32)
    gg, qq, gh, hh, qw, ww = zero, zero, zero, zero, zero, zero
    adjoint(grad)
    for i in range(blocks_here):
        gg += fold(grad[i] * grad[i])
    for slot in range(n_src):
        for i, re, im in forward(slot):
            mine = slice(i * rows, (i + 1) * rows)
            qq += fold(re * re + im * im)
            image0[slot, mine, :half] = re
            image0[slot, mine, half:] = im
            store(i, slot, re.astype(jnp.bfloat16), im.astype(jnp.bfloat16))
    adjoint(hess)
    for i in range(blocks_here):
        gh += fold(hess[i] * grad[i])
        hh += fold(hess[i] * hess[i])
    for slot in range(n_src):
        for i, re, im in forward(slot):
            mine = slice(i * rows, (i + 1) * rows)
            ww += fold(re * re + im * im)
            qw += fold(re * image0[slot, mine, :half] + im * image0[slot, mine, half:])
            image1[slot, mine, :half] = re
            image1[slot, mine, half:] = im
    sums = jnp.concatenate([gg, qq, gh, hh, qw, ww, zero, zero], axis=0)
    sums_out[...] = sums
    share_bf = along(sums).astype(jnp.bfloat16)
    share = share_bf.astype(jnp.float32)
    height = blocks_here * rows
    for slot in range(n_src):
        first = image0[slot]
        images[where[slot], :height] = first.astype(jnp.bfloat16)
        images[where[slot], height : 2 * height] = (image1[slot] - share * first).astype(jnp.bfloat16)
        images[where[slot], 2 * height :] = jnp.broadcast_to(share_bf, (SHARE_ROWS, cols))


def combine_kernel(sums, images, grad, hess, refl_out, moved_out):
    n_src, height = images.shape[0], (images.shape[1] - SHARE_ROWS) // 2
    total = jnp.sum(sums[...], axis=1, keepdims=True)
    gg, qq, gh, hh, qw, ww = [total[i : i + 1] for i in range(6)]
    step0 = gg / qq
    grad_next = gg - 2 * step0 * gh + step0 * step0 * hh
    near = 1 + grad_next / gg
    image_sq = near * near * qq - 2 * near * step0 * qw + step0 * step0 * ww
    step1 = grad_next / image_sq
    c1 = step0 + step1 * near
    c2 = -step0 * step1
    for i in range(grad.shape[0]):
        refl_out[i] = c1 * grad[i] + c2 * hess[i]
    for s in range(n_src):
        share = images[s, 2 * height :].astype(jnp.float32)[:1, :1]
        first = images[s, :height].astype(jnp.float32)
        rest = images[s, height : 2 * height].astype(jnp.float32)
        moved_out[s] = (c1 + c2 * share) * first + c2 * rest


def summed(x, axis, count):
    if count & (count - 1):
        return lax.psum(x, axis)
    bit = 1
    while bit < count:
        radix = min(4, count // bit)
        others = [lax.ppermute(x, axis, [(d, d ^ (bit * m)) for d in range(count)]) for m in range(1, radix)]
        x = (x + others[0]) + (others[1] + others[2]) if radix == 4 else x + others[0]
        bit *= radix
    return x


def per_device(n_rcv, n_src, pplus, pminus, band):
    blocks_here = band.shape[0]
    rows = BLOCK // n_src
    cols = 2 * pplus.shape[2]
    order = ring_order(n_src)
    ahead = [(order[p], order[(p + 1) % n_src]) for p in range(n_src)]
    behind = [(d, s) for s, d in ahead]

    def swaps(first):
        pairs = [(r, r + 1) for r in range(first, n_rcv - 1, 2)]
        return pairs + [(d, s) for s, d in pairs]

    start = lax.optimization_barrier(pminus.reshape(blocks_here * BLOCK, cols))
    start = jnp.transpose(start.reshape(blocks_here, n_src, rows, cols), (1, 0, 2, 3))
    field = lax.all_to_all(start.reshape(n_src, blocks_here * rows, cols), "src", 0, 0, tiled=True)

    own = pplus.reshape(blocks_here * BLOCK, cols)
    chunks, shifts = [own], [0]
    fwd = bwd = own
    for step in range(1, n_src // 2 + 1):
        fwd = lax.ppermute(fwd, "src", ahead)
        chunks.append(fwd)
        shifts.append(-step)
        if len(chunks) < n_src:
            bwd = lax.ppermute(bwd, "src", behind)
            chunks.append(bwd)
            shifts.append(step)
    near = [lax.ppermute(c, "rcv", swaps(0)) for c in chunks]
    far = [lax.ppermute(c, "rcv", swaps(1)) for c in chunks]
    me = jnp.stack([lax.axis_index("rcv"), lax.axis_index("src")]).astype(jnp.int32)

    smem, vmem = pl.BlockSpec(memory_space=pltpu.SMEM), pl.BlockSpec(memory_space=pltpu.VMEM)
    band_cols = NEIGH * BLOCK
    grad, hess, images, sums = pl.pallas_call(
        functools.partial(maps_kernel, n_src, shifts),
        out_shape=(
            jax.ShapeDtypeStruct((blocks_here, 2 * rows, band_cols), jnp.float32),
            jax.ShapeDtypeStruct((blocks_here, 2 * rows, band_cols), jnp.float32),
            jax.ShapeDtypeStruct((n_src, 2 * blocks_here * rows + SHARE_ROWS, cols), jnp.bfloat16),
            jax.ShapeDtypeStruct((8, 128), jnp.float32),
        ),
        in_specs=[smem, smem] + [vmem] * (1 + 3 * n_src),
        out_specs=[vmem] * 4,
        scratch_shapes=[
            pltpu.VMEM((blocks_here * 2 * rows, n_src * cols), jnp.bfloat16),
            pltpu.VMEM((3 * blocks_here, blocks_here * 2 * rows, BLOCK), jnp.float32),
            pltpu.VMEM((3 * blocks_here, blocks_here * 2 * rows, BLOCK), jnp.bfloat16),
            pltpu.VMEM((n_src, blocks_here * rows, cols), jnp.float32),
            pltpu.VMEM((n_src, blocks_here * rows, cols), jnp.float32),
        ],
        compiler_params=pltpu.CompilerParams(vmem_limit_bytes=8 << 20),
        name="maps",
    )(me, band, *[pltpu.with_memory_space_constraint(x, pltpu.VMEM) for x in (field, *chunks, *near, *far)])

    images = lax.all_to_all(images, "src", 0, 0, tiled=True)
    sums = summed(summed(sums, "rcv", n_rcv), "src", n_src)
    refl, moved = pl.pallas_call(
        combine_kernel,
        out_shape=(
            jax.ShapeDtypeStruct(grad.shape, jnp.float32),
            jax.ShapeDtypeStruct((n_src, blocks_here * rows, cols), jnp.float32),
        ),
        in_specs=[vmem] * 4,
        out_specs=[vmem] * 2,
        compiler_params=pltpu.CompilerParams(vmem_limit_bytes=8 << 20),
        name="combine",
    )(sums, images, grad, hess)

    refl = jnp.transpose(refl.reshape(blocks_here, 2, rows, NEIGH, BLOCK), (2, 0, 3, 1, 4))
    moved = jnp.transpose(moved.reshape(n_src, blocks_here, rows, cols), (1, 0, 2, 3))
    misfit = pminus.astype(jnp.float32) - moved.reshape(pminus.shape)
    return refl, misfit


def solution(mesh):
    return jax.shard_map(
        functools.partial(per_device, mesh.shape["rcv"], mesh.shape["src"]),
        mesh=mesh,
        in_specs=(P("rcv", None, "src"), P("rcv", None, "src"), P("rcv", None)),
        out_specs=(P("src", "rcv", None, None, None), P("rcv", None, "src")),
        check_vma=False,
    )
```

```python
import functools

import jax
import jax.numpy as jnp
from jax import lax
from jax.experimental import pallas as pl
from jax.experimental.pallas import tpu as pltpu
from jax.sharding import PartitionSpec as P

BLOCK = 256
NEIGH = 3
HALO_BLK = 2
ROWS_X = 2
SHARE_ROWS = 16


def ring_order(count):
    if count % ROWS_X or count < 2 * ROWS_X:
        return list(range(count))
    half = count // ROWS_X
    return [ROWS_X * p for p in range(half)] + [ROWS_X * p + 1 for p in reversed(range(half))]


def ring_place(count, index, shift):
    if count % ROWS_X or count < 2 * ROWS_X:
        return lax.rem(index + shift + count, count)
    half, odd = count // ROWS_X, lax.rem(index, ROWS_X)
    step = (index - odd) // ROWS_X
    place = lax.rem(jnp.where(odd == 1, count - 1 - step, step) + shift + count, count)
    return jnp.where(place < half, ROWS_X * place, ROWS_X * (count - 1 - place) + 1)


def along(sums):
    total = jnp.sum(sums, axis=1, keepdims=True)
    qq, qw = total[1:2], total[4:5]
    return jnp.where(qq > 0, qw / jnp.where(qq > 0, qq, 1.0), 0.0)


def maps_kernel(n_src, shifts, *refs):
    me, band, field = refs[:3]
    ends = [3, 3 + n_src, 3 + 2 * n_src, 3 + 3 * n_src]
    sources = [refs[a:b] for a, b in zip(ends[:-1], ends[1:])]
    grad, hess, images, sums_out = refs[ends[3] : ends[3] + 4]
    held, lhs, every, factors, image0, image1, sems = refs[ends[3] + 4 :]
    blocks_here = grad.shape[0]
    rows = grad.shape[1] // 2
    cols = field.shape[2]
    half = cols // 2
    window = blocks_here * len(sources)
    me_rcv, me_src = me[0], me[1]
    odd = lax.rem(me_rcv, 2)
    where = [ring_place(n_src, me_src, shift) for shift in shifts]

    fetches = [
        [pltpu.make_async_copy(chunk, held.at[g, slot], sems.at[g, slot]) for slot, chunk in enumerate(group)]
        for g, group in enumerate(sources)
    ]
    for fetch in sum(fetches, []):
        fetch.start()

    places = {}
    for i in range(blocks_here):
        for k in range(NEIGH):
            offset = band[i, k] - me_rcv * blocks_here
            before, here = offset < 0, (offset >= 0) & (offset < blocks_here)
            group = jnp.where(here, 0, jnp.where(jnp.where(before, 1, 0) == odd, 1, 2))
            inside = jnp.where(before, offset + blocks_here, jnp.where(here, offset, offset - blocks_here))
            places[i, k] = group * blocks_here + inside

    def block(place, slot):
        start = place % blocks_here * BLOCK
        return held[place // blocks_here, slot, start : start + BLOCK, :]

    def store(i, slot, re_bf, im_bf):
        top, low = slice(2 * i * rows, (2 * i + 1) * rows), slice((2 * i + 1) * rows, (2 * i + 2) * rows)
        left, right = slice(slot * cols, slot * cols + half), slice(slot * cols + half, (slot + 1) * cols)
        lhs[top, left] = re_bf
        lhs[top, right] = im_bf
        lhs[low, left] = im_bf
        lhs[low, right] = -re_bf

    def fold(x):
        total = x[:, :128]
        for c in range(128, x.shape[1], 128):
            total = total + x[:, c : c + 128]
        return jnp.sum(total, axis=0, keepdims=True)

    def adjoint(out, first):
        for place in range(window):
            if first and place % blocks_here == 0:
                for fetch in fetches[place // blocks_here]:
                    fetch.wait()
            row = jnp.concatenate([block(place, slot) for slot in range(n_src)], axis=1)
            every[place] = lax.dot_general(
                lhs[...], row, (((1,), (1,)), ((), ())), preferred_element_type=jnp.float32
            )
        for i in range(blocks_here):
            mine = slice(2 * i * rows, 2 * (i + 1) * rows)
            for k in range(NEIGH):
                part = every[places[i, k], mine, :]
                out[i, :, k * BLOCK : (k + 1) * BLOCK] = part
                factors[places[i, k], mine, :] = part.astype(jnp.bfloat16)

    def forward(slot):
        column = jnp.concatenate([block(place, slot) for place in range(window)], axis=0)
        wide = jnp.concatenate([factors[place] for place in range(window)], axis=1)
        prod = jnp.dot(wide, column, preferred_element_type=jnp.float32)
        for i in range(blocks_here):
            top, low = prod[2 * i * rows : (2 * i + 1) * rows], prod[(2 * i + 1) * rows : 2 * (i + 1) * rows]
            yield i, top[:, :half] - low[:, half:], top[:, half:] + low[:, :half]

    factors[...] = jnp.zeros_like(factors)
    for slot in range(n_src):
        for i in range(blocks_here):
            rows_bf = field[where[slot], i * rows : (i + 1) * rows, :]
            store(i, slot, rows_bf[:, :half], rows_bf[:, half:])

    zero = jnp.zeros((1, 128), jnp.float32)
    gg, qq, gh, hh, qw, ww = zero, zero, zero, zero, zero, zero
    adjoint(grad, True)
    for i in range(blocks_here):
        gg += fold(grad[i] * grad[i])
    for slot in range(n_src):
        for i, re, im in forward(slot):
            mine = slice(i * rows, (i + 1) * rows)
            qq += fold(re * re + im * im)
            image0[slot, mine, :half] = re
            image0[slot, mine, half:] = im
            store(i, slot, re.astype(jnp.bfloat16), im.astype(jnp.bfloat16))
    adjoint(hess, False)
    for i in range(blocks_here):
        gh += fold(hess[i] * grad[i])
        hh += fold(hess[i] * hess[i])
    for slot in range(n_src):
        for i, re, im in forward(slot):
            mine = slice(i * rows, (i + 1) * rows)
            ww += fold(re * re + im * im)
            qw += fold(re * image0[slot, mine, :half] + im * image0[slot, mine, half:])
            image1[slot, mine, :half] = re
            image1[slot, mine, half:] = im
    sums = jnp.concatenate([gg, qq, gh, hh, qw, ww, zero, zero], axis=0)
    sums_out[...] = sums
    share_bf = along(sums).astype(jnp.bfloat16)
    share = share_bf.astype(jnp.float32)
    height = blocks_here * rows
    for slot in range(n_src):
        first = image0[slot]
        images[where[slot], :height] = first.astype(jnp.bfloat16)
        images[where[slot], height : 2 * height] = (image1[slot] - share * first).astype(jnp.bfloat16)
        images[where[slot], 2 * height :] = jnp.broadcast_to(share_bf, (SHARE_ROWS, cols))


def combine_kernel(sums, images, grad, hess, refl_out, moved_out):
    n_src, height = images.shape[0], (images.shape[1] - SHARE_ROWS) // 2
    total = jnp.sum(sums[...], axis=1, keepdims=True)
    gg, qq, gh, hh, qw, ww = [total[i : i + 1] for i in range(6)]
    step0 = gg / qq
    grad_next = gg - 2 * step0 * gh + step0 * step0 * hh
    near = 1 + grad_next / gg
    image_sq = near * near * qq - 2 * near * step0 * qw + step0 * step0 * ww
    step1 = grad_next / image_sq
    c1 = step0 + step1 * near
    c2 = -step0 * step1
    for i in range(grad.shape[0]):
        refl_out[i] = c1 * grad[i] + c2 * hess[i]
    for s in range(n_src):
        share = images[s, 2 * height :].astype(jnp.float32)[:1, :1]
        first = images[s, :height].astype(jnp.float32)
        rest = images[s, height : 2 * height].astype(jnp.float32)
        moved_out[s] = (c1 + c2 * share) * first + c2 * rest


def summed(x, axis, count):
    if count & (count - 1):
        return lax.psum(x, axis)
    bit = 1
    while bit < count:
        radix = min(4, count // bit)
        others = [lax.ppermute(x, axis, [(d, d ^ (bit * m)) for d in range(count)]) for m in range(1, radix)]
        x = (x + others[0]) + (others[1] + others[2]) if radix == 4 else x + others[0]
        bit *= radix
    return x


def per_device(n_rcv, n_src, pplus, pminus, band):
    blocks_here = band.shape[0]
    rows = BLOCK // n_src
    cols = 2 * pplus.shape[2]
    order = ring_order(n_src)
    ahead = [(order[p], order[(p + 1) % n_src]) for p in range(n_src)]
    behind = [(d, s) for s, d in ahead]

    def swaps(first):
        pairs = [(r, r + 1) for r in range(first, n_rcv - 1, 2)]
        return pairs + [(d, s) for s, d in pairs]

    start = lax.optimization_barrier(pminus.reshape(blocks_here * BLOCK, cols))
    start = jnp.transpose(start.reshape(blocks_here, n_src, rows, cols), (1, 0, 2, 3))
    field = lax.all_to_all(start.reshape(n_src, blocks_here * rows, cols), "src", 0, 0, tiled=True)

    own = pplus.reshape(blocks_here * BLOCK, cols)
    chunks, shifts = [own], [0]
    fwd = bwd = own
    for step in range(1, n_src // 2 + 1):
        fwd = lax.ppermute(fwd, "src", ahead)
        chunks.append(fwd)
        shifts.append(-step)
        if len(chunks) < n_src:
            bwd = lax.ppermute(bwd, "src", behind)
            chunks.append(bwd)
            shifts.append(step)
    near = [lax.ppermute(c, "rcv", swaps(0)) for c in chunks]
    far = [lax.ppermute(c, "rcv", swaps(1)) for c in chunks]
    me = jnp.stack([lax.axis_index("rcv"), lax.axis_index("src")]).astype(jnp.int32)

    any_spec = pl.BlockSpec(memory_space=pl.ANY)
    smem, vmem = pl.BlockSpec(memory_space=pltpu.SMEM), pl.BlockSpec(memory_space=pltpu.VMEM)
    band_cols = NEIGH * BLOCK
    grad, hess, images, sums = pl.pallas_call(
        functools.partial(maps_kernel, n_src, shifts),
        out_shape=(
            jax.ShapeDtypeStruct((blocks_here, 2 * rows, band_cols), jnp.float32),
            jax.ShapeDtypeStruct((blocks_here, 2 * rows, band_cols), jnp.float32),
            jax.ShapeDtypeStruct((n_src, 2 * blocks_here * rows + SHARE_ROWS, cols), jnp.bfloat16),
            jax.ShapeDtypeStruct((8, 128), jnp.float32),
        ),
        in_specs=[smem, smem, vmem] + [any_spec] * (3 * n_src),
        out_specs=[vmem] * 4,
        scratch_shapes=[
            pltpu.VMEM((3, n_src, blocks_here * BLOCK, cols), jnp.bfloat16),
            pltpu.VMEM((blocks_here * 2 * rows, n_src * cols), jnp.bfloat16),
            pltpu.VMEM((3 * blocks_here, blocks_here * 2 * rows, BLOCK), jnp.float32),
            pltpu.VMEM((3 * blocks_here, blocks_here * 2 * rows, BLOCK), jnp.bfloat16),
            pltpu.VMEM((n_src, blocks_here * rows, cols), jnp.float32),
            pltpu.VMEM((n_src, blocks_here * rows, cols), jnp.float32),
            pltpu.SemaphoreType.DMA((3, n_src)),
        ],
        compiler_params=pltpu.CompilerParams(vmem_limit_bytes=60 << 20),
        name="maps",
    )(me, band, field, *chunks, *near, *far)

    images = lax.all_to_all(images, "src", 0, 0, tiled=True)
    sums = summed(summed(sums, "rcv", n_rcv), "src", n_src)
    refl, moved = pl.pallas_call(
        combine_kernel,
        out_shape=(
            jax.ShapeDtypeStruct(grad.shape, jnp.float32),
            jax.ShapeDtypeStruct((n_src, blocks_here * rows, cols), jnp.float32),
        ),
        in_specs=[vmem] * 4,
        out_specs=[vmem] * 2,
        compiler_params=pltpu.CompilerParams(vmem_limit_bytes=8 << 20),
        name="combine",
    )(sums, images, grad, hess)

    refl = jnp.transpose(refl.reshape(blocks_here, 2, rows, NEIGH, BLOCK), (2, 0, 3, 1, 4))
    moved = jnp.transpose(moved.reshape(n_src, blocks_here, rows, cols), (1, 0, 2, 3))
    misfit = pminus.astype(jnp.float32) - moved.reshape(pminus.shape)
    return refl, misfit


def solution(mesh):
    return jax.shard_map(
        functools.partial(per_device, mesh.shape["rcv"], mesh.shape["src"]),
        mesh=mesh,
        in_specs=(P("rcv", None, "src"), P("rcv", None, "src"), P("rcv", None)),
        out_specs=(P("src", "rcv", None, None, None), P("rcv", None, "src")),
        check_vma=False,
    )
```

```python
import functools

import jax
import jax.numpy as jnp
from jax import lax
from jax.experimental import pallas as pl
from jax.experimental.pallas import tpu as pltpu
from jax.sharding import PartitionSpec as P

BLOCK = 256
NEIGH = 3
HALO_BLK = 2
ROWS_X = 2
SHARE_ROWS = 16


def ring_order(count):
    if count % ROWS_X or count < 2 * ROWS_X:
        return list(range(count))
    half = count // ROWS_X
    return [ROWS_X * p for p in range(half)] + [ROWS_X * p + 1 for p in reversed(range(half))]


def ring_place(count, index, shift):
    if count % ROWS_X or count < 2 * ROWS_X:
        return lax.rem(index + shift + count, count)
    half, odd = count // ROWS_X, lax.rem(index, ROWS_X)
    step = (index - odd) // ROWS_X
    place = lax.rem(jnp.where(odd == 1, count - 1 - step, step) + shift + count, count)
    return jnp.where(place < half, ROWS_X * place, ROWS_X * (count - 1 - place) + 1)


def along(sums):
    total = jnp.sum(sums, axis=1, keepdims=True)
    qq, qw = total[1:2], total[4:5]
    return jnp.where(qq > 0, qw / jnp.where(qq > 0, qq, 1.0), 0.0)


def maps_kernel(n_src, shifts, *refs):
    band_in, field = refs[:2]
    ends = [2, 2 + n_src, 2 + 2 * n_src, 2 + 3 * n_src]
    sources = [refs[a:b] for a, b in zip(ends[:-1], ends[1:])]
    grad, hess, images, sums_out = refs[ends[3] : ends[3] + 4]
    band, held, lhs, every, factors, image0, image1, sems, band_sem = refs[ends[3] + 4 :]
    blocks_here = grad.shape[0]
    rows = grad.shape[1] // 2
    cols = field.shape[2]
    half = cols // 2
    window = blocks_here * len(sources)
    me_rcv, me_src = lax.axis_index("rcv"), lax.axis_index("src")
    odd = lax.rem(me_rcv, 2)
    where = [ring_place(n_src, me_src, shift) for shift in shifts]

    fetches = [
        [pltpu.make_async_copy(chunk, held.at[g, slot], sems.at[g, slot]) for slot, chunk in enumerate(group)]
        for g, group in enumerate(sources)
    ]
    band_fetch = pltpu.make_async_copy(band_in, band, band_sem)
    band_fetch.start()
    for fetch in sum(fetches, []):
        fetch.start()
    band_fetch.wait()

    places = {}
    for i in range(blocks_here):
        for k in range(NEIGH):
            offset = band[i, k] - me_rcv * blocks_here
            before, here = offset < 0, (offset >= 0) & (offset < blocks_here)
            group = jnp.where(here, 0, jnp.where(jnp.where(before, 1, 0) == odd, 1, 2))
            inside = jnp.where(before, offset + blocks_here, jnp.where(here, offset, offset - blocks_here))
            places[i, k] = group * blocks_here + inside

    def block(place, slot):
        start = place % blocks_here * BLOCK
        return held[place // blocks_here, slot, start : start + BLOCK, :]

    def store(i, slot, re_bf, im_bf):
        top, low = slice(2 * i * rows, (2 * i + 1) * rows), slice((2 * i + 1) * rows, (2 * i + 2) * rows)
        left, right = slice(slot * cols, slot * cols + half), slice(slot * cols + half, (slot + 1) * cols)
        lhs[top, left] = re_bf
        lhs[top, right] = im_bf
        lhs[low, left] = im_bf
        lhs[low, right] = -re_bf

    def fold(x):
        total = x[:, :128]
        for c in range(128, x.shape[1], 128):
            total = total + x[:, c : c + 128]
        return jnp.sum(total, axis=0, keepdims=True)

    def adjoint(out, first):
        for place in range(window):
            if first and place % blocks_here == 0:
                for fetch in fetches[place // blocks_here]:
                    fetch.wait()
            row = jnp.concatenate([block(place, slot) for slot in range(n_src)], axis=1)
            every[place] = lax.dot_general(
                lhs[...], row, (((1,), (1,)), ((), ())), preferred_element_type=jnp.float32
            )
        for i in range(blocks_here):
            mine = slice(2 * i * rows, 2 * (i + 1) * rows)
            for k in range(NEIGH):
                part = every[places[i, k], mine, :]
                out[i, :, k * BLOCK : (k + 1) * BLOCK] = part
                factors[places[i, k], mine, :] = part.astype(jnp.bfloat16)

    def forward(slot):
        column = jnp.concatenate([block(place, slot) for place in range(window)], axis=0)
        wide = jnp.concatenate([factors[place] for place in range(window)], axis=1)
        prod = jnp.dot(wide, column, preferred_element_type=jnp.float32)
        for i in range(blocks_here):
            top, low = prod[2 * i * rows : (2 * i + 1) * rows], prod[(2 * i + 1) * rows : 2 * (i + 1) * rows]
            yield i, top[:, :half] - low[:, half:], top[:, half:] + low[:, :half]

    factors[...] = jnp.zeros_like(factors)
    for slot in range(n_src):
        for i in range(blocks_here):
            rows_bf = field[where[slot], i * rows : (i + 1) * rows, :]
            store(i, slot, rows_bf[:, :half], rows_bf[:, half:])

    zero = jnp.zeros((1, 128), jnp.float32)
    gg, qq, gh, hh, qw, ww = zero, zero, zero, zero, zero, zero
    adjoint(grad, True)
    for i in range(blocks_here):
        gg += fold(grad[i] * grad[i])
    for slot in range(n_src):
        for i, re, im in forward(slot):
            mine = slice(i * rows, (i + 1) * rows)
            qq += fold(re * re + im * im)
            image0[slot, mine, :half] = re
            image0[slot, mine, half:] = im
            store(i, slot, re.astype(jnp.bfloat16), im.astype(jnp.bfloat16))
    adjoint(hess, False)
    for i in range(blocks_here):
        gh += fold(hess[i] * grad[i])
        hh += fold(hess[i] * hess[i])
    for slot in range(n_src):
        for i, re, im in forward(slot):
            mine = slice(i * rows, (i + 1) * rows)
            ww += fold(re * re + im * im)
            qw += fold(re * image0[slot, mine, :half] + im * image0[slot, mine, half:])
            image1[slot, mine, :half] = re
            image1[slot, mine, half:] = im
    sums = jnp.concatenate([gg, qq, gh, hh, qw, ww, zero, zero], axis=0)
    sums_out[...] = sums
    share_bf = along(sums).astype(jnp.bfloat16)
    share = share_bf.astype(jnp.float32)
    height = blocks_here * rows
    for slot in range(n_src):
        first = image0[slot]
        images[where[slot], :height] = first.astype(jnp.bfloat16)
        images[where[slot], height : 2 * height] = (image1[slot] - share * first).astype(jnp.bfloat16)
        images[where[slot], 2 * height :] = jnp.broadcast_to(share_bf, (SHARE_ROWS, cols))


def combine_kernel(sums, images, grad, hess, refl_out, moved_out):
    n_src, height = images.shape[0], (images.shape[1] - SHARE_ROWS) // 2
    total = jnp.sum(sums[...], axis=1, keepdims=True)
    gg, qq, gh, hh, qw, ww = [total[i : i + 1] for i in range(6)]
    step0 = gg / qq
    grad_next = gg - 2 * step0 * gh + step0 * step0 * hh
    near = 1 + grad_next / gg
    image_sq = near * near * qq - 2 * near * step0 * qw + step0 * step0 * ww
    step1 = grad_next / image_sq
    c1 = step0 + step1 * near
    c2 = -step0 * step1
    for i in range(grad.shape[0]):
        refl_out[i] = c1 * grad[i] + c2 * hess[i]
    for s in range(n_src):
        share = images[s, 2 * height :].astype(jnp.float32)[:1, :1]
        first = images[s, :height].astype(jnp.float32)
        rest = images[s, height : 2 * height].astype(jnp.float32)
        moved_out[s] = (c1 + c2 * share) * first + c2 * rest


def summed(x, axis, count):
    if count & (count - 1):
        return lax.psum(x, axis)
    bit = 1
    while bit < count:
        radix = min(4, count // bit)
        others = [lax.ppermute(x, axis, [(d, d ^ (bit * m)) for d in range(count)]) for m in range(1, radix)]
        x = (x + others[0]) + (others[1] + others[2]) if radix == 4 else x + others[0]
        bit *= radix
    return x


def per_device(n_rcv, n_src, pplus, pminus, band):
    blocks_here = band.shape[0]
    rows = BLOCK // n_src
    cols = 2 * pplus.shape[2]
    order = ring_order(n_src)
    ahead = [(order[p], order[(p + 1) % n_src]) for p in range(n_src)]
    behind = [(d, s) for s, d in ahead]

    def swaps(first):
        pairs = [(r, r + 1) for r in range(first, n_rcv - 1, 2)]
        return pairs + [(d, s) for s, d in pairs]

    start = lax.optimization_barrier(pminus.reshape(blocks_here * BLOCK, cols))
    start = jnp.transpose(start.reshape(blocks_here, n_src, rows, cols), (1, 0, 2, 3))
    field = lax.all_to_all(start.reshape(n_src, blocks_here * rows, cols), "src", 0, 0, tiled=True)

    own = pplus.reshape(blocks_here * BLOCK, cols)
    chunks, shifts = [own], [0]
    fwd = bwd = own
    for step in range(1, n_src // 2 + 1):
        fwd = lax.ppermute(fwd, "src", ahead)
        chunks.append(fwd)
        shifts.append(-step)
        if len(chunks) < n_src:
            bwd = lax.ppermute(bwd, "src", behind)
            chunks.append(bwd)
            shifts.append(step)
    near = [lax.ppermute(c, "rcv", swaps(0)) for c in chunks]
    far = [lax.ppermute(c, "rcv", swaps(1)) for c in chunks]
    any_spec = pl.BlockSpec(memory_space=pl.ANY)
    vmem = pl.BlockSpec(memory_space=pltpu.VMEM)
    band_cols = NEIGH * BLOCK
    grad, hess, images, sums = pl.pallas_call(
        functools.partial(maps_kernel, n_src, shifts),
        out_shape=(
            jax.ShapeDtypeStruct((blocks_here, 2 * rows, band_cols), jnp.float32),
            jax.ShapeDtypeStruct((blocks_here, 2 * rows, band_cols), jnp.float32),
            jax.ShapeDtypeStruct((n_src, 2 * blocks_here * rows + SHARE_ROWS, cols), jnp.bfloat16),
            jax.ShapeDtypeStruct((8, 128), jnp.float32),
        ),
        in_specs=[any_spec, vmem] + [any_spec] * (3 * n_src),
        out_specs=[vmem] * 4,
        scratch_shapes=[
            pltpu.SMEM(band.shape, jnp.int32),
            pltpu.VMEM((3, n_src, blocks_here * BLOCK, cols), jnp.bfloat16),
            pltpu.VMEM((blocks_here * 2 * rows, n_src * cols), jnp.bfloat16),
            pltpu.VMEM((3 * blocks_here, blocks_here * 2 * rows, BLOCK), jnp.float32),
            pltpu.VMEM((3 * blocks_here, blocks_here * 2 * rows, BLOCK), jnp.bfloat16),
            pltpu.VMEM((n_src, blocks_here * rows, cols), jnp.float32),
            pltpu.VMEM((n_src, blocks_here * rows, cols), jnp.float32),
            pltpu.SemaphoreType.DMA((3, n_src)),
            pltpu.SemaphoreType.DMA,
        ],
        compiler_params=pltpu.CompilerParams(vmem_limit_bytes=60 << 20),
        name="maps",
    )(band, field, *chunks, *near, *far)

    images = lax.all_to_all(images, "src", 0, 0, tiled=True)
    sums = summed(summed(sums, "rcv", n_rcv), "src", n_src)
    refl, moved = pl.pallas_call(
        combine_kernel,
        out_shape=(
            jax.ShapeDtypeStruct(grad.shape, jnp.float32),
            jax.ShapeDtypeStruct((n_src, blocks_here * rows, cols), jnp.float32),
        ),
        in_specs=[vmem] * 4,
        out_specs=[vmem] * 2,
        compiler_params=pltpu.CompilerParams(vmem_limit_bytes=8 << 20),
        name="combine",
    )(sums, images, grad, hess)

    refl = jnp.transpose(refl.reshape(blocks_here, 2, rows, NEIGH, BLOCK), (2, 0, 3, 1, 4))
    moved = jnp.transpose(moved.reshape(n_src, blocks_here, rows, cols), (1, 0, 2, 3))
    misfit = pminus.astype(jnp.float32) - moved.reshape(pminus.shape)
    return refl, misfit


def solution(mesh):
    return jax.shard_map(
        functools.partial(per_device, mesh.shape["rcv"], mesh.shape["src"]),
        mesh=mesh,
        in_specs=(P("rcv", None, "src"), P("rcv", None, "src"), P("rcv", None)),
        out_specs=(P("src", "rcv", None, None, None), P("rcv", None, "src")),
        check_vma=False,
    )
```

```python
import functools

import jax
import jax.numpy as jnp
from jax import lax
from jax.experimental import pallas as pl
from jax.experimental.pallas import tpu as pltpu
from jax.sharding import PartitionSpec as P

BLOCK = 256
NEIGH = 3
HALO_BLK = 2
ROWS_X = 2
SHARE_ROWS = 16
PAIR = 2


def ring_order(count):
    if count % ROWS_X or count < 2 * ROWS_X:
        return list(range(count))
    half = count // ROWS_X
    return [ROWS_X * p for p in range(half)] + [ROWS_X * p + 1 for p in reversed(range(half))]


def ring_place(count, index, shift):
    if count % ROWS_X or count < 2 * ROWS_X:
        return lax.rem(index + shift + count, count)
    half, odd = count // ROWS_X, lax.rem(index, ROWS_X)
    step = (index - odd) // ROWS_X
    place = lax.rem(jnp.where(odd == 1, count - 1 - step, step) + shift + count, count)
    return jnp.where(place < half, ROWS_X * place, ROWS_X * (count - 1 - place) + 1)


def along(sums):
    total = jnp.sum(sums, axis=1, keepdims=True)
    qq, qw = total[1:2], total[4:5]
    return jnp.where(qq > 0, qw / jnp.where(qq > 0, qq, 1.0), 0.0)


def maps_kernel(n_src, shifts, *refs):
    band_in, field = refs[:2]
    ends = [2, 2 + n_src, 2 + 2 * n_src, 2 + 3 * n_src]
    sources = [refs[a:b] for a, b in zip(ends[:-1], ends[1:])]
    grad, hess, images, sums_out = refs[ends[3] : ends[3] + 4]
    band, held, lhs, every, factors, image0, image1, sems, band_sem = refs[ends[3] + 4 :]
    blocks_here = grad.shape[0]
    rows = grad.shape[1] // 2
    cols = field.shape[2]
    half = cols // 2
    window = blocks_here * len(sources)
    me_rcv, me_src = lax.axis_index("rcv"), lax.axis_index("src")
    odd = lax.rem(me_rcv, 2)
    where = [ring_place(n_src, me_src, shift) for shift in shifts]

    fetches = [
        [pltpu.make_async_copy(chunk, held.at[g, slot], sems.at[g, slot]) for slot, chunk in enumerate(group)]
        for g, group in enumerate(sources)
    ]
    band_fetch = pltpu.make_async_copy(band_in, band, band_sem)
    band_fetch.start()
    for fetch in sum(fetches, []):
        fetch.start()
    band_fetch.wait()

    places = {}
    for i in range(blocks_here):
        for k in range(NEIGH):
            offset = band[i, k] - me_rcv * blocks_here
            before, here = offset < 0, (offset >= 0) & (offset < blocks_here)
            group = jnp.where(here, 0, jnp.where(jnp.where(before, 1, 0) == odd, 1, 2))
            inside = jnp.where(before, offset + blocks_here, jnp.where(here, offset, offset - blocks_here))
            places[i, k] = group * blocks_here + inside

    def store(i, slot, re_bf, im_bf):
        top, low = slice(2 * i * rows, (2 * i + 1) * rows), slice((2 * i + 1) * rows, (2 * i + 2) * rows)
        left, right = slice(slot * cols, slot * cols + half), slice(slot * cols + half, (slot + 1) * cols)
        lhs[top, left] = re_bf
        lhs[top, right] = im_bf
        lhs[low, left] = im_bf
        lhs[low, right] = -re_bf

    def fold(x):
        total = x[:, :128]
        for c in range(128, x.shape[1], 128):
            total = total + x[:, c : c + 128]
        return jnp.sum(total, axis=0, keepdims=True)

    def adjoint(out, first):
        for g in range(len(sources)):
            if first:
                for fetch in fetches[g]:
                    fetch.wait()
            chunks = jnp.concatenate([held[g, slot] for slot in range(n_src)], axis=1)
            both = lax.dot_general(lhs[...], chunks, (((1,), (1,)), ((), ())), preferred_element_type=jnp.float32)
            for inside in range(blocks_here):
                every[g * blocks_here + inside] = both[:, inside * BLOCK : (inside + 1) * BLOCK]
        for i in range(blocks_here):
            mine = slice(2 * i * rows, 2 * (i + 1) * rows)
            for k in range(NEIGH):
                part = every[places[i, k], mine, :]
                out[i, :, k * BLOCK : (k + 1) * BLOCK] = part
                factors[places[i, k], mine, :] = part.astype(jnp.bfloat16)

    def forward():
        wide = jnp.concatenate([factors[place] for place in range(window)], axis=1)
        for base in range(0, n_src, PAIR):
            slots = range(base, min(base + PAIR, n_src))
            columns = [
                jnp.concatenate([held[g, slot] for g in range(len(sources))], axis=0) for slot in slots
            ]
            prod = jnp.dot(wide, jnp.concatenate(columns, axis=1), preferred_element_type=jnp.float32)
            for slot in slots:
                left = (slot - base) * cols
                for i in range(blocks_here):
                    top = prod[2 * i * rows : (2 * i + 1) * rows, left : left + cols]
                    low = prod[(2 * i + 1) * rows : 2 * (i + 1) * rows, left : left + cols]
                    yield slot, i, top[:, :half] - low[:, half:], top[:, half:] + low[:, :half]

    factors[...] = jnp.zeros_like(factors)
    for slot in range(n_src):
        for i in range(blocks_here):
            rows_bf = field[where[slot], i * rows : (i + 1) * rows, :]
            store(i, slot, rows_bf[:, :half], rows_bf[:, half:])

    zero = jnp.zeros((1, 128), jnp.float32)
    gg, qq, gh, hh, qw, ww = zero, zero, zero, zero, zero, zero
    adjoint(grad, True)
    for i in range(blocks_here):
        gg += fold(grad[i] * grad[i])
    for slot, i, re, im in forward():
        mine = slice(i * rows, (i + 1) * rows)
        qq += fold(re * re + im * im)
        image0[slot, mine, :half] = re
        image0[slot, mine, half:] = im
        store(i, slot, re.astype(jnp.bfloat16), im.astype(jnp.bfloat16))
    adjoint(hess, False)
    for i in range(blocks_here):
        gh += fold(hess[i] * grad[i])
        hh += fold(hess[i] * hess[i])
    for slot, i, re, im in forward():
        mine = slice(i * rows, (i + 1) * rows)
        ww += fold(re * re + im * im)
        qw += fold(re * image0[slot, mine, :half] + im * image0[slot, mine, half:])
        image1[slot, mine, :half] = re
        image1[slot, mine, half:] = im
    sums = jnp.concatenate([gg, qq, gh, hh, qw, ww, zero, zero], axis=0)
    sums_out[...] = sums
    share_bf = along(sums).astype(jnp.bfloat16)
    share = share_bf.astype(jnp.float32)
    height = blocks_here * rows
    for slot in range(n_src):
        first = image0[slot]
        images[where[slot], :height] = first.astype(jnp.bfloat16)
        images[where[slot], height : 2 * height] = (image1[slot] - share * first).astype(jnp.bfloat16)
        images[where[slot], 2 * height :] = jnp.broadcast_to(share_bf, (SHARE_ROWS, cols))


def combine_kernel(sums, images, grad, hess, refl_out, moved_out):
    n_src, height = images.shape[0], (images.shape[1] - SHARE_ROWS) // 2
    total = jnp.sum(sums[...], axis=1, keepdims=True)
    gg, qq, gh, hh, qw, ww = [total[i : i + 1] for i in range(6)]
    step0 = gg / qq
    grad_next = gg - 2 * step0 * gh + step0 * step0 * hh
    near = 1 + grad_next / gg
    image_sq = near * near * qq - 2 * near * step0 * qw + step0 * step0 * ww
    step1 = grad_next / image_sq
    c1 = step0 + step1 * near
    c2 = -step0 * step1
    for i in range(grad.shape[0]):
        refl_out[i] = c1 * grad[i] + c2 * hess[i]
    for s in range(n_src):
        share = images[s, 2 * height :].astype(jnp.float32)[:1, :1]
        first = images[s, :height].astype(jnp.float32)
        rest = images[s, height : 2 * height].astype(jnp.float32)
        moved_out[s] = (c1 + c2 * share) * first + c2 * rest


def summed(x, axis, count):
    if count & (count - 1):
        return lax.psum(x, axis)
    bit = 1
    while bit < count:
        radix = min(4, count // bit)
        others = [lax.ppermute(x, axis, [(d, d ^ (bit * m)) for d in range(count)]) for m in range(1, radix)]
        x = (x + others[0]) + (others[1] + others[2]) if radix == 4 else x + others[0]
        bit *= radix
    return x


def per_device(n_rcv, n_src, pplus, pminus, band):
    blocks_here = band.shape[0]
    rows = BLOCK // n_src
    cols = 2 * pplus.shape[2]
    order = ring_order(n_src)
    ahead = [(order[p], order[(p + 1) % n_src]) for p in range(n_src)]
    behind = [(d, s) for s, d in ahead]

    def swaps(first):
        pairs = [(r, r + 1) for r in range(first, n_rcv - 1, 2)]
        return pairs + [(d, s) for s, d in pairs]

    start = lax.optimization_barrier(pminus.reshape(blocks_here * BLOCK, cols))
    start = jnp.transpose(start.reshape(blocks_here, n_src, rows, cols), (1, 0, 2, 3))
    field = lax.all_to_all(start.reshape(n_src, blocks_here * rows, cols), "src", 0, 0, tiled=True)

    own = pplus.reshape(blocks_here * BLOCK, cols)
    chunks, shifts = [own], [0]
    fwd = bwd = own
    for step in range(1, n_src // 2 + 1):
        fwd = lax.ppermute(fwd, "src", ahead)
        chunks.append(fwd)
        shifts.append(-step)
        if len(chunks) < n_src:
            bwd = lax.ppermute(bwd, "src", behind)
            chunks.append(bwd)
            shifts.append(step)
    near = [lax.ppermute(c, "rcv", swaps(0)) for c in chunks]
    far = [lax.ppermute(c, "rcv", swaps(1)) for c in chunks]
    any_spec = pl.BlockSpec(memory_space=pl.ANY)
    vmem = pl.BlockSpec(memory_space=pltpu.VMEM)
    band_cols = NEIGH * BLOCK
    grad, hess, images, sums = pl.pallas_call(
        functools.partial(maps_kernel, n_src, shifts),
        out_shape=(
            jax.ShapeDtypeStruct((blocks_here, 2 * rows, band_cols), jnp.float32),
            jax.ShapeDtypeStruct((blocks_here, 2 * rows, band_cols), jnp.float32),
            jax.ShapeDtypeStruct((n_src, 2 * blocks_here * rows + SHARE_ROWS, cols), jnp.bfloat16),
            jax.ShapeDtypeStruct((8, 128), jnp.float32),
        ),
        in_specs=[any_spec, vmem] + [any_spec] * (3 * n_src),
        out_specs=[vmem] * 4,
        scratch_shapes=[
            pltpu.SMEM(band.shape, jnp.int32),
            pltpu.VMEM((3, n_src, blocks_here * BLOCK, cols), jnp.bfloat16),
            pltpu.VMEM((blocks_here * 2 * rows, n_src * cols), jnp.bfloat16),
            pltpu.VMEM((3 * blocks_here, blocks_here * 2 * rows, BLOCK), jnp.float32),
            pltpu.VMEM((3 * blocks_here, blocks_here * 2 * rows, BLOCK), jnp.bfloat16),
            pltpu.VMEM((n_src, blocks_here * rows, cols), jnp.float32),
            pltpu.VMEM((n_src, blocks_here * rows, cols), jnp.float32),
            pltpu.SemaphoreType.DMA((3, n_src)),
            pltpu.SemaphoreType.DMA,
        ],
        compiler_params=pltpu.CompilerParams(vmem_limit_bytes=60 << 20),
        name="maps",
    )(band, field, *chunks, *near, *far)

    images = lax.all_to_all(images, "src", 0, 0, tiled=True)
    sums = summed(summed(sums, "rcv", n_rcv), "src", n_src)
    refl, moved = pl.pallas_call(
        combine_kernel,
        out_shape=(
            jax.ShapeDtypeStruct(grad.shape, jnp.float32),
            jax.ShapeDtypeStruct((n_src, blocks_here * rows, cols), jnp.float32),
        ),
        in_specs=[vmem] * 4,
        out_specs=[vmem] * 2,
        compiler_params=pltpu.CompilerParams(vmem_limit_bytes=8 << 20),
        name="combine",
    )(sums, images, grad, hess)

    refl = jnp.transpose(refl.reshape(blocks_here, 2, rows, NEIGH, BLOCK), (2, 0, 3, 1, 4))
    moved = jnp.transpose(moved.reshape(n_src, blocks_here, rows, cols), (1, 0, 2, 3))
    misfit = pminus.astype(jnp.float32) - moved.reshape(pminus.shape)
    return refl, misfit


def solution(mesh):
    return jax.shard_map(
        functools.partial(per_device, mesh.shape["rcv"], mesh.shape["src"]),
        mesh=mesh,
        in_specs=(P("rcv", None, "src"), P("rcv", None, "src"), P("rcv", None)),
        out_specs=(P("src", "rcv", None, None, None), P("rcv", None, "src")),
        check_vma=False,
    )
```

```python
import functools

import jax
import jax.numpy as jnp
from jax import lax
from jax.experimental import pallas as pl
from jax.experimental.pallas import tpu as pltpu
from jax.sharding import PartitionSpec as P

BLOCK = 256
NEIGH = 3
HALO_BLK = 2
ROWS_X = 2
SHARE_ROWS = 16
PAIR = 2


def ring_order(count):
    if count % ROWS_X or count < 2 * ROWS_X:
        return list(range(count))
    half = count // ROWS_X
    return [ROWS_X * p for p in range(half)] + [ROWS_X * p + 1 for p in reversed(range(half))]


def ring_place(count, index, shift):
    if count % ROWS_X or count < 2 * ROWS_X:
        return lax.rem(index + shift + count, count)
    half, odd = count // ROWS_X, lax.rem(index, ROWS_X)
    step = (index - odd) // ROWS_X
    place = lax.rem(jnp.where(odd == 1, count - 1 - step, step) + shift + count, count)
    return jnp.where(place < half, ROWS_X * place, ROWS_X * (count - 1 - place) + 1)


def along(sums):
    total = jnp.sum(sums, axis=1, keepdims=True)
    qq, qw = total[1:2], total[4:5]
    return jnp.where(qq > 0, qw / jnp.where(qq > 0, qq, 1.0), 0.0)


def turned(lhs, i, slot, re_bf, im_bf):
    rows, half = re_bf.shape
    top, low = slice(2 * i * rows, (2 * i + 1) * rows), slice((2 * i + 1) * rows, (2 * i + 2) * rows)
    left, right = slice(2 * slot * half, (2 * slot + 1) * half), slice((2 * slot + 1) * half, 2 * (slot + 1) * half)
    lhs[top, left] = re_bf
    lhs[top, right] = im_bf
    lhs[low, left] = im_bf
    lhs[low, right] = -re_bf


def turn_field(lhs, field, shifts):
    n_src, half = field.shape[0], field.shape[2] // 2
    me_src = lax.axis_index("src")
    rows = BLOCK // n_src
    for slot, shift in enumerate(shifts):
        place = ring_place(n_src, me_src, shift)
        for i in range(field.shape[1] // rows):
            rows_bf = field[place, i * rows : (i + 1) * rows, :]
            turned(lhs, i, slot, rows_bf[:, :half], rows_bf[:, half:])


def project(lhs, held, g, every, base):
    chunks = jnp.concatenate([held[g, slot] for slot in range(held.shape[1])], axis=1)
    both = lax.dot_general(lhs[...], chunks, (((1,), (1,)), ((), ())), preferred_element_type=jnp.float32)
    for inside in range(both.shape[1] // BLOCK):
        every[base + inside] = both[:, inside * BLOCK : (inside + 1) * BLOCK]


def fetching(groups, held, sems):
    return [
        [pltpu.make_async_copy(chunk, held.at[g, slot], sems.at[g, slot]) for slot, chunk in enumerate(group)]
        for g, group in enumerate(groups)
    ]


def begin_kernel(n_src, shifts, field, *refs):
    every, held, lhs, sems = refs[2 * n_src :]
    blocks_here = held.shape[2] // BLOCK
    fetches = fetching([refs[:n_src], refs[n_src : 2 * n_src]], held, sems)
    for fetch in sum(fetches, []):
        fetch.start()
    turn_field(lhs, field, shifts)
    for g, group in enumerate(fetches):
        for fetch in group:
            fetch.wait()
        project(lhs, held, g, every, g * blocks_here)


def maps_kernel(n_src, shifts, *refs):
    band_in, field, begun = refs[:3]
    ends = [3, 3 + n_src, 3 + 2 * n_src, 3 + 3 * n_src]
    sources = [refs[a:b] for a, b in zip(ends[:-1], ends[1:])]
    grad, hess, images, sums_out = refs[ends[3] : ends[3] + 4]
    band, held, lhs, every, factors, image0, image1, sems, band_sem = refs[ends[3] + 4 :]
    blocks_here = grad.shape[0]
    rows = grad.shape[1] // 2
    cols = field.shape[2]
    half = cols // 2
    window = blocks_here * len(sources)
    me_rcv, me_src = lax.axis_index("rcv"), lax.axis_index("src")
    odd = lax.rem(me_rcv, 2)
    where = [ring_place(n_src, me_src, shift) for shift in shifts]

    fetches = fetching(sources, held, sems)
    band_fetch = pltpu.make_async_copy(band_in, band, band_sem)
    band_fetch.start()
    for fetch in fetches[2] + fetches[0] + fetches[1]:
        fetch.start()
    band_fetch.wait()

    places = {}
    for i in range(blocks_here):
        for k in range(NEIGH):
            offset = band[i, k] - me_rcv * blocks_here
            before, here = offset < 0, (offset >= 0) & (offset < blocks_here)
            group = jnp.where(here, 0, jnp.where(jnp.where(before, 1, 0) == odd, 1, 2))
            inside = jnp.where(before, offset + blocks_here, jnp.where(here, offset, offset - blocks_here))
            places[i, k] = group * blocks_here + inside

    def fold(x):
        total = x[:, :128]
        for c in range(128, x.shape[1], 128):
            total = total + x[:, c : c + 128]
        return jnp.sum(total, axis=0, keepdims=True)

    def wait(group):
        for fetch in group:
            fetch.wait()

    def adjoint(out, first):
        if first:
            for place in range(2 * blocks_here):
                every[place] = begun[place]
            wait(fetches[2])
        for g in [2] if first else range(len(sources)):
            project(lhs, held, g, every, g * blocks_here)
        for i in range(blocks_here):
            mine = slice(2 * i * rows, 2 * (i + 1) * rows)
            for k in range(NEIGH):
                part = every[places[i, k], mine, :]
                out[i, :, k * BLOCK : (k + 1) * BLOCK] = part
                factors[places[i, k], mine, :] = part.astype(jnp.bfloat16)

    def forward():
        wide = jnp.concatenate([factors[place] for place in range(window)], axis=1)
        for base in range(0, n_src, PAIR):
            slots = range(base, min(base + PAIR, n_src))
            columns = [
                jnp.concatenate([held[g, slot] for g in range(len(sources))], axis=0) for slot in slots
            ]
            prod = jnp.dot(wide, jnp.concatenate(columns, axis=1), preferred_element_type=jnp.float32)
            for slot in slots:
                left = (slot - base) * cols
                for i in range(blocks_here):
                    top = prod[2 * i * rows : (2 * i + 1) * rows, left : left + cols]
                    low = prod[(2 * i + 1) * rows : 2 * (i + 1) * rows, left : left + cols]
                    yield slot, i, top[:, :half] - low[:, half:], top[:, half:] + low[:, :half]

    factors[...] = jnp.zeros_like(factors)
    turn_field(lhs, field, shifts)

    zero = jnp.zeros((1, 128), jnp.float32)
    gg, qq, gh, hh, qw, ww = zero, zero, zero, zero, zero, zero
    adjoint(grad, True)
    for i in range(blocks_here):
        gg += fold(grad[i] * grad[i])
    wait(fetches[0] + fetches[1])
    for slot, i, re, im in forward():
        mine = slice(i * rows, (i + 1) * rows)
        qq += fold(re * re + im * im)
        image0[slot, mine, :half] = re
        image0[slot, mine, half:] = im
        turned(lhs, i, slot, re.astype(jnp.bfloat16), im.astype(jnp.bfloat16))
    adjoint(hess, False)
    for i in range(blocks_here):
        gh += fold(hess[i] * grad[i])
        hh += fold(hess[i] * hess[i])
    for slot, i, re, im in forward():
        mine = slice(i * rows, (i + 1) * rows)
        ww += fold(re * re + im * im)
        qw += fold(re * image0[slot, mine, :half] + im * image0[slot, mine, half:])
        image1[slot, mine, :half] = re
        image1[slot, mine, half:] = im
    sums = jnp.concatenate([gg, qq, gh, hh, qw, ww, zero, zero], axis=0)
    sums_out[...] = sums
    share_bf = along(sums).astype(jnp.bfloat16)
    share = share_bf.astype(jnp.float32)
    height = blocks_here * rows
    for slot in range(n_src):
        first = image0[slot]
        images[where[slot], :height] = first.astype(jnp.bfloat16)
        images[where[slot], height : 2 * height] = (image1[slot] - share * first).astype(jnp.bfloat16)
        images[where[slot], 2 * height :] = jnp.broadcast_to(share_bf, (SHARE_ROWS, cols))


def combine_kernel(sums, images, grad, hess, refl_out, moved_out):
    n_src, height = images.shape[0], (images.shape[1] - SHARE_ROWS) // 2
    total = jnp.sum(sums[...], axis=1, keepdims=True)
    gg, qq, gh, hh, qw, ww = [total[i : i + 1] for i in range(6)]
    step0 = gg / qq
    grad_next = gg - 2 * step0 * gh + step0 * step0 * hh
    near = 1 + grad_next / gg
    image_sq = near * near * qq - 2 * near * step0 * qw + step0 * step0 * ww
    step1 = grad_next / image_sq
    c1 = step0 + step1 * near
    c2 = -step0 * step1
    for i in range(grad.shape[0]):
        refl_out[i] = c1 * grad[i] + c2 * hess[i]
    for s in range(n_src):
        share = images[s, 2 * height :].astype(jnp.float32)[:1, :1]
        first = images[s, :height].astype(jnp.float32)
        rest = images[s, height : 2 * height].astype(jnp.float32)
        moved_out[s] = (c1 + c2 * share) * first + c2 * rest


def summed(x, axis, count):
    if count & (count - 1):
        return lax.psum(x, axis)
    bit = 1
    while bit < count:
        radix = min(8, count // bit)
        terms = [x] + [lax.ppermute(x, axis, [(d, d ^ (bit * m)) for d in range(count)]) for m in range(1, radix)]
        while len(terms) > 1:
            terms = [a + b for a, b in zip(terms[::2], terms[1::2])]
        x = terms[0]
        bit *= radix
    return x


def per_device(n_rcv, n_src, pplus, pminus, band):
    blocks_here = band.shape[0]
    rows = BLOCK // n_src
    cols = 2 * pplus.shape[2]
    order = ring_order(n_src)
    ahead = [(order[p], order[(p + 1) % n_src]) for p in range(n_src)]
    behind = [(d, s) for s, d in ahead]

    def swaps(first):
        pairs = [(r, r + 1) for r in range(first, n_rcv - 1, 2)]
        return pairs + [(d, s) for s, d in pairs]

    start = lax.optimization_barrier(pminus.reshape(blocks_here * BLOCK, cols))
    start = jnp.transpose(start.reshape(blocks_here, n_src, rows, cols), (1, 0, 2, 3))
    field = lax.all_to_all(start.reshape(n_src, blocks_here * rows, cols), "src", 0, 0, tiled=True)

    own = pplus.reshape(blocks_here * BLOCK, cols)
    chunks, shifts = [own], [0]
    fwd = bwd = own
    for step in range(1, n_src // 2 + 1):
        fwd = lax.ppermute(fwd, "src", ahead)
        chunks.append(fwd)
        shifts.append(-step)
        if len(chunks) < n_src:
            bwd = lax.ppermute(bwd, "src", behind)
            chunks.append(bwd)
            shifts.append(step)
    near = [lax.ppermute(c, "rcv", swaps(0)) for c in chunks]
    far = [lax.ppermute(c, "rcv", swaps(1)) for c in chunks]
    any_spec = pl.BlockSpec(memory_space=pl.ANY)
    vmem = pl.BlockSpec(memory_space=pltpu.VMEM)
    band_cols = NEIGH * BLOCK
    tall = blocks_here * 2 * rows
    begun = pl.pallas_call(
        functools.partial(begin_kernel, n_src, shifts),
        out_shape=jax.ShapeDtypeStruct((2 * blocks_here, tall, BLOCK), jnp.float32),
        in_specs=[vmem] + [any_spec] * (2 * n_src),
        out_specs=vmem,
        scratch_shapes=[
            pltpu.VMEM((2, n_src, blocks_here * BLOCK, cols), jnp.bfloat16),
            pltpu.VMEM((tall, n_src * cols), jnp.bfloat16),
            pltpu.SemaphoreType.DMA((2, n_src)),
        ],
        compiler_params=pltpu.CompilerParams(vmem_limit_bytes=60 << 20),
        cost_estimate=pl.CostEstimate(
            flops=4 * tall * n_src * cols * blocks_here * BLOCK,
            bytes_accessed=4 * n_src * blocks_here * BLOCK * cols,
            transcendentals=0,
        ),
        name="begin",
    )(field, *chunks, *near)
    grad, hess, images, sums = pl.pallas_call(
        functools.partial(maps_kernel, n_src, shifts),
        out_shape=(
            jax.ShapeDtypeStruct((blocks_here, 2 * rows, band_cols), jnp.float32),
            jax.ShapeDtypeStruct((blocks_here, 2 * rows, band_cols), jnp.float32),
            jax.ShapeDtypeStruct((n_src, 2 * blocks_here * rows + SHARE_ROWS, cols), jnp.bfloat16),
            jax.ShapeDtypeStruct((8, 128), jnp.float32),
        ),
        in_specs=[any_spec, vmem, vmem] + [any_spec] * (3 * n_src),
        out_specs=[vmem] * 4,
        scratch_shapes=[
            pltpu.SMEM(band.shape, jnp.int32),
            pltpu.VMEM((3, n_src, blocks_here * BLOCK, cols), jnp.bfloat16),
            pltpu.VMEM((blocks_here * 2 * rows, n_src * cols), jnp.bfloat16),
            pltpu.VMEM((3 * blocks_here, blocks_here * 2 * rows, BLOCK), jnp.float32),
            pltpu.VMEM((3 * blocks_here, blocks_here * 2 * rows, BLOCK), jnp.bfloat16),
            pltpu.VMEM((n_src, blocks_here * rows, cols), jnp.float32),
            pltpu.VMEM((n_src, blocks_here * rows, cols), jnp.float32),
            pltpu.SemaphoreType.DMA((3, n_src)),
            pltpu.SemaphoreType.DMA,
        ],
        compiler_params=pltpu.CompilerParams(vmem_limit_bytes=60 << 20),
        name="maps",
    )(band, field, begun, *chunks, *near, *far)

    images = lax.all_to_all(images, "src", 0, 0, tiled=True)
    sums = summed(summed(sums, "rcv", n_rcv), "src", n_src)
    refl, moved = pl.pallas_call(
        combine_kernel,
        out_shape=(
            jax.ShapeDtypeStruct(grad.shape, jnp.float32),
            jax.ShapeDtypeStruct((n_src, blocks_here * rows, cols), jnp.float32),
        ),
        in_specs=[vmem] * 4,
        out_specs=[vmem] * 2,
        compiler_params=pltpu.CompilerParams(vmem_limit_bytes=8 << 20),
        name="combine",
    )(sums, images, grad, hess)

    refl = jnp.transpose(refl.reshape(blocks_here, 2, rows, NEIGH, BLOCK), (2, 0, 3, 1, 4))
    moved = jnp.transpose(moved.reshape(n_src, blocks_here, rows, cols), (1, 0, 2, 3))
    misfit = pminus.astype(jnp.float32) - moved.reshape(pminus.shape)
    return refl, misfit


def solution(mesh):
    return jax.shard_map(
        functools.partial(per_device, mesh.shape["rcv"], mesh.shape["src"]),
        mesh=mesh,
        in_specs=(P("rcv", None, "src"), P("rcv", None, "src"), P("rcv", None)),
        out_specs=(P("src", "rcv", None, None, None), P("rcv", None, "src")),
        check_vma=False,
    )
```

```python
import functools

import jax
import jax.numpy as jnp
from jax import lax
from jax.experimental import pallas as pl
from jax.experimental.pallas import tpu as pltpu
from jax.sharding import PartitionSpec as P

BLOCK = 256
NEIGH = 3
HALO_BLK = 2
ROWS_X = 2
SHARE_ROWS = 16
PAIR = 2


def ring_order(count):
    if count % ROWS_X or count < 2 * ROWS_X:
        return list(range(count))
    half = count // ROWS_X
    return [ROWS_X * p for p in range(half)] + [ROWS_X * p + 1 for p in reversed(range(half))]


def ring_place(count, index, shift):
    if count % ROWS_X or count < 2 * ROWS_X:
        return lax.rem(index + shift + count, count)
    half, odd = count // ROWS_X, lax.rem(index, ROWS_X)
    step = (index - odd) // ROWS_X
    place = lax.rem(jnp.where(odd == 1, count - 1 - step, step) + shift + count, count)
    return jnp.where(place < half, ROWS_X * place, ROWS_X * (count - 1 - place) + 1)


def along(sums):
    total = jnp.sum(sums, axis=1, keepdims=True)
    qq, qw = total[1:2], total[4:5]
    return jnp.where(qq > 0, qw / jnp.where(qq > 0, qq, 1.0), 0.0)


def maps_kernel(n_src, shifts, *refs):
    band_in, field = refs[:2]
    ends = [2, 2 + n_src, 2 + 2 * n_src, 2 + 3 * n_src]
    sources = [refs[a:b] for a, b in zip(ends[:-1], ends[1:])]
    grad, hess, images, sums_out = refs[ends[3] : ends[3] + 4]
    band, held, lhs, every, factors, image0, image1, sems, band_sem = refs[ends[3] + 4 :]
    blocks_here = grad.shape[0]
    rows = grad.shape[1] // 2
    cols = field.shape[2]
    half = cols // 2
    window = blocks_here * len(sources)
    me_rcv, me_src = lax.axis_index("rcv"), lax.axis_index("src")
    odd = lax.rem(me_rcv, 2)
    where = [ring_place(n_src, me_src, shift) for shift in shifts]

    fetches = [
        [pltpu.make_async_copy(chunk, held.at[g, slot], sems.at[g, slot]) for slot, chunk in enumerate(group)]
        for g, group in enumerate(sources)
    ]
    band_fetch = pltpu.make_async_copy(band_in, band, band_sem)
    band_fetch.start()
    for fetch in sum(fetches, []):
        fetch.start()
    band_fetch.wait()

    places = {}
    for i in range(blocks_here):
        for k in range(NEIGH):
            offset = band[i, k] - me_rcv * blocks_here
            before, here = offset < 0, (offset >= 0) & (offset < blocks_here)
            group = jnp.where(here, 0, jnp.where(jnp.where(before, 1, 0) == odd, 1, 2))
            inside = jnp.where(before, offset + blocks_here, jnp.where(here, offset, offset - blocks_here))
            places[i, k] = group * blocks_here + inside

    def store(i, slot, re_bf, im_bf):
        top, low = slice(2 * i * rows, (2 * i + 1) * rows), slice((2 * i + 1) * rows, (2 * i + 2) * rows)
        left, right = slice(slot * cols, slot * cols + half), slice(slot * cols + half, (slot + 1) * cols)
        lhs[top, left] = re_bf
        lhs[top, right] = im_bf
        lhs[low, left] = im_bf
        lhs[low, right] = -re_bf

    def fold(x):
        total = x[:, :128]
        for c in range(128, x.shape[1], 128):
            total = total + x[:, c : c + 128]
        return jnp.sum(total, axis=0, keepdims=True)

    def adjoint(out, first):
        for g in range(len(sources)):
            if first:
                for fetch in fetches[g]:
                    fetch.wait()
            chunks = jnp.concatenate([held[g, slot] for slot in range(n_src)], axis=1)
            both = lax.dot_general(lhs[...], chunks, (((1,), (1,)), ((), ())), preferred_element_type=jnp.float32)
            for inside in range(blocks_here):
                every[g * blocks_here + inside] = both[:, inside * BLOCK : (inside + 1) * BLOCK]
        for i in range(blocks_here):
            mine = slice(2 * i * rows, 2 * (i + 1) * rows)
            for k in range(NEIGH):
                part = every[places[i, k], mine, :]
                out[i, :, k * BLOCK : (k + 1) * BLOCK] = part
                factors[places[i, k], mine, :] = part.astype(jnp.bfloat16)

    def forward():
        wide = jnp.concatenate([factors[place] for place in range(window)], axis=1)
        for base in range(0, n_src, PAIR):
            slots = range(base, min(base + PAIR, n_src))
            columns = [
                jnp.concatenate([held[g, slot] for g in range(len(sources))], axis=0) for slot in slots
            ]
            prod = jnp.dot(wide, jnp.concatenate(columns, axis=1), preferred_element_type=jnp.float32)
            for slot in slots:
                left = (slot - base) * cols
                for i in range(blocks_here):
                    top = prod[2 * i * rows : (2 * i + 1) * rows, left : left + cols]
                    low = prod[(2 * i + 1) * rows : 2 * (i + 1) * rows, left : left + cols]
                    yield slot, i, top[:, :half] - low[:, half:], top[:, half:] + low[:, :half]

    factors[...] = jnp.zeros_like(factors)
    for slot in range(n_src):
        for i in range(blocks_here):
            rows_bf = field[where[slot], i * rows : (i + 1) * rows, :]
            store(i, slot, rows_bf[:, :half], rows_bf[:, half:])

    zero = jnp.zeros((1, 128), jnp.float32)
    gg, qq, gh, hh, qw, ww = zero, zero, zero, zero, zero, zero
    adjoint(grad, True)
    for i in range(blocks_here):
        gg += fold(grad[i] * grad[i])
    for slot, i, re, im in forward():
        mine = slice(i * rows, (i + 1) * rows)
        qq += fold(re * re + im * im)
        image0[slot, mine, :half] = re
        image0[slot, mine, half:] = im
        store(i, slot, re.astype(jnp.bfloat16), im.astype(jnp.bfloat16))
    adjoint(hess, False)
    for i in range(blocks_here):
        gh += fold(hess[i] * grad[i])
        hh += fold(hess[i] * hess[i])
    for slot, i, re, im in forward():
        mine = slice(i * rows, (i + 1) * rows)
        ww += fold(re * re + im * im)
        qw += fold(re * image0[slot, mine, :half] + im * image0[slot, mine, half:])
        image1[slot, mine, :half] = re
        image1[slot, mine, half:] = im
    sums = jnp.concatenate([gg, qq, gh, hh, qw, ww, zero, zero], axis=0)
    sums_out[...] = sums
    share_bf = along(sums).astype(jnp.bfloat16)
    share = share_bf.astype(jnp.float32)
    height = blocks_here * rows
    for slot in range(n_src):
        first = image0[slot]
        images[where[slot], :height] = first.astype(jnp.bfloat16)
        images[where[slot], height : 2 * height] = (image1[slot] - share * first).astype(jnp.bfloat16)
        images[where[slot], 2 * height :] = jnp.broadcast_to(share_bf, (SHARE_ROWS, cols))


def combine_kernel(sums, images, grad, hess, refl_out, moved_out):
    n_src, height = images.shape[0], (images.shape[1] - SHARE_ROWS) // 2
    total = jnp.sum(sums[...], axis=1, keepdims=True)
    gg, qq, gh, hh, qw, ww = [total[i : i + 1] for i in range(6)]
    step0 = gg / qq
    grad_next = gg - 2 * step0 * gh + step0 * step0 * hh
    near = 1 + grad_next / gg
    image_sq = near * near * qq - 2 * near * step0 * qw + step0 * step0 * ww
    step1 = grad_next / image_sq
    c1 = step0 + step1 * near
    c2 = -step0 * step1
    for i in range(grad.shape[0]):
        refl_out[i] = c1 * grad[i] + c2 * hess[i]
    for s in range(n_src):
        share = images[s, 2 * height :].astype(jnp.float32)[:1, :1]
        first = images[s, :height].astype(jnp.float32)
        rest = images[s, height : 2 * height].astype(jnp.float32)
        moved_out[s] = (c1 + c2 * share) * first + c2 * rest


def summed(x, axis, count):
    if count & (count - 1):
        return lax.psum(x, axis)
    bit = 1
    while bit < count:
        radix = min(4, count // bit)
        others = [lax.ppermute(x, axis, [(d, d ^ (bit * m)) for d in range(count)]) for m in range(1, radix)]
        x = (x + others[0]) + (others[1] + others[2]) if radix == 4 else x + others[0]
        bit *= radix
    return x


def per_device(n_rcv, n_src, pplus, pminus, band):
    blocks_here = band.shape[0]
    rows = BLOCK // n_src
    cols = 2 * pplus.shape[2]
    order = ring_order(n_src)
    ahead = [(order[p], order[(p + 1) % n_src]) for p in range(n_src)]
    behind = [(d, s) for s, d in ahead]

    def swaps(first):
        pairs = [(r, r + 1) for r in range(first, n_rcv - 1, 2)]
        return pairs + [(d, s) for s, d in pairs]

    start = lax.optimization_barrier(pminus.reshape(blocks_here * BLOCK, cols))
    start = jnp.transpose(start.reshape(blocks_here, n_src, rows, cols), (1, 0, 2, 3))
    field = lax.all_to_all(start.reshape(n_src, blocks_here * rows, cols), "src", 0, 0, tiled=True)

    own = pplus.reshape(blocks_here * BLOCK, cols)
    chunks, shifts, settled = [own], [0], [own]
    fwd = bwd = own
    for step in range(1, n_src // 2 + 1):
        fwd = lax.ppermute(fwd, "src", ahead)
        chunks.append(fwd)
        shifts.append(-step)
        if len(chunks) < n_src:
            bwd = lax.ppermute(bwd, "src", behind)
            chunks.append(bwd)
            shifts.append(step)
            settled.extend(lax.optimization_barrier((fwd, bwd)))
        else:
            settled.append(fwd)
    near = [lax.ppermute(c, "rcv", swaps(0)) for c in settled]
    far = [lax.ppermute(c, "rcv", swaps(1)) for c in settled]

    any_spec = pl.BlockSpec(memory_space=pl.ANY)
    vmem = pl.BlockSpec(memory_space=pltpu.VMEM)
    band_cols = NEIGH * BLOCK
    grad, hess, images, sums = pl.pallas_call(
        functools.partial(maps_kernel, n_src, shifts),
        out_shape=(
            jax.ShapeDtypeStruct((blocks_here, 2 * rows, band_cols), jnp.float32),
            jax.ShapeDtypeStruct((blocks_here, 2 * rows, band_cols), jnp.float32),
            jax.ShapeDtypeStruct((n_src, 2 * blocks_here * rows + SHARE_ROWS, cols), jnp.bfloat16),
            jax.ShapeDtypeStruct((8, 128), jnp.float32),
        ),
        in_specs=[any_spec, vmem] + [any_spec] * (3 * n_src),
        out_specs=[vmem] * 4,
        scratch_shapes=[
            pltpu.SMEM(band.shape, jnp.int32),
            pltpu.VMEM((3, n_src, blocks_here * BLOCK, cols), jnp.bfloat16),
            pltpu.VMEM((blocks_here * 2 * rows, n_src * cols), jnp.bfloat16),
            pltpu.VMEM((3 * blocks_here, blocks_here * 2 * rows, BLOCK), jnp.float32),
            pltpu.VMEM((3 * blocks_here, blocks_here * 2 * rows, BLOCK), jnp.bfloat16),
            pltpu.VMEM((n_src, blocks_here * rows, cols), jnp.float32),
            pltpu.VMEM((n_src, blocks_here * rows, cols), jnp.float32),
            pltpu.SemaphoreType.DMA((3, n_src)),
            pltpu.SemaphoreType.DMA,
        ],
        compiler_params=pltpu.CompilerParams(vmem_limit_bytes=60 << 20),
        name="maps",
    )(band, field, *chunks, *near, *far)

    images = lax.all_to_all(images, "src", 0, 0, tiled=True)
    sums = summed(summed(sums, "rcv", n_rcv), "src", n_src)
    refl, moved = pl.pallas_call(
        combine_kernel,
        out_shape=(
            jax.ShapeDtypeStruct(grad.shape, jnp.float32),
            jax.ShapeDtypeStruct((n_src, blocks_here * rows, cols), jnp.float32),
        ),
        in_specs=[vmem] * 4,
        out_specs=[vmem] * 2,
        compiler_params=pltpu.CompilerParams(vmem_limit_bytes=8 << 20),
        name="combine",
    )(sums, images, grad, hess)

    refl = jnp.transpose(refl.reshape(blocks_here, 2, rows, NEIGH, BLOCK), (2, 0, 3, 1, 4))
    moved = jnp.transpose(moved.reshape(n_src, blocks_here, rows, cols), (1, 0, 2, 3))
    misfit = pminus.astype(jnp.float32) - moved.reshape(pminus.shape)
    return refl, misfit


def solution(mesh):
    return jax.shard_map(
        functools.partial(per_device, mesh.shape["rcv"], mesh.shape["src"]),
        mesh=mesh,
        in_specs=(P("rcv", None, "src"), P("rcv", None, "src"), P("rcv", None)),
        out_specs=(P("src", "rcv", None, None, None), P("rcv", None, "src")),
        check_vma=False,
    )
```

```python
import functools

import jax
import jax.numpy as jnp
from jax import lax
from jax.experimental import pallas as pl
from jax.experimental.pallas import tpu as pltpu
from jax.sharding import PartitionSpec as P

BLOCK = 256
NEIGH = 3
HALO_BLK = 2
ROWS_X = 2
SHARE_ROWS = 16
PAIR = 2


def ring_order(count):
    if count % ROWS_X or count < 2 * ROWS_X:
        return list(range(count))
    half = count // ROWS_X
    return [ROWS_X * p for p in range(half)] + [ROWS_X * p + 1 for p in reversed(range(half))]


def ring_place(count, index, shift):
    if count % ROWS_X or count < 2 * ROWS_X:
        return lax.rem(index + shift + count, count)
    half, odd = count // ROWS_X, lax.rem(index, ROWS_X)
    step = (index - odd) // ROWS_X
    place = lax.rem(jnp.where(odd == 1, count - 1 - step, step) + shift + count, count)
    return jnp.where(place < half, ROWS_X * place, ROWS_X * (count - 1 - place) + 1)


def along(sums):
    total = jnp.sum(sums, axis=1, keepdims=True)
    qq, qw = total[1:2], total[4:5]
    return jnp.where(qq > 0, qw / jnp.where(qq > 0, qq, 1.0), 0.0)


def maps_kernel(n_src, shifts, *refs):
    band_in, field = refs[:2]
    ends = [2, 2 + n_src, 2 + 2 * n_src, 2 + 3 * n_src]
    sources = [refs[a:b] for a, b in zip(ends[:-1], ends[1:])]
    grad, hess, images, sums_out = refs[ends[3] : ends[3] + 4]
    band, held, lhs, every, factors, image0, image1, sems, band_sem = refs[ends[3] + 4 :]
    blocks_here = grad.shape[0]
    rows = grad.shape[1] // 2
    cols = field.shape[2]
    half = cols // 2
    window = blocks_here * len(sources)
    me_rcv, me_src = lax.axis_index("rcv"), lax.axis_index("src")
    odd = lax.rem(me_rcv, 2)
    where = [ring_place(n_src, me_src, shift) for shift in shifts]

    fetches = [
        [pltpu.make_async_copy(chunk, held.at[g, slot], sems.at[g, slot]) for slot, chunk in enumerate(group)]
        for g, group in enumerate(sources)
    ]
    band_fetch = pltpu.make_async_copy(band_in, band, band_sem)
    band_fetch.start()
    for fetch in sum(fetches, []):
        fetch.start()
    band_fetch.wait()

    places = {}
    for i in range(blocks_here):
        for k in range(NEIGH):
            offset = band[i, k] - me_rcv * blocks_here
            before, here = offset < 0, (offset >= 0) & (offset < blocks_here)
            group = jnp.where(here, 0, jnp.where(jnp.where(before, 1, 0) == odd, 1, 2))
            inside = jnp.where(before, offset + blocks_here, jnp.where(here, offset, offset - blocks_here))
            places[i, k] = group * blocks_here + inside

    def store(i, slot, re_bf, im_bf):
        top, low = slice(2 * i * rows, (2 * i + 1) * rows), slice((2 * i + 1) * rows, (2 * i + 2) * rows)
        left, right = slice(slot * cols, slot * cols + half), slice(slot * cols + half, (slot + 1) * cols)
        lhs[top, left] = re_bf
        lhs[top, right] = im_bf
        lhs[low, left] = im_bf
        lhs[low, right] = -re_bf

    def fold(x):
        total = x[:, :128]
        for c in range(128, x.shape[1], 128):
            total = total + x[:, c : c + 128]
        return jnp.sum(total, axis=0, keepdims=True)

    def adjoint(out, first):
        for g in range(len(sources)):
            if first:
                for fetch in fetches[g]:
                    fetch.wait()
            chunks = jnp.concatenate([held[g, slot] for slot in range(n_src)], axis=1)
            both = lax.dot_general(lhs[...], chunks, (((1,), (1,)), ((), ())), preferred_element_type=jnp.float32)
            for inside in range(blocks_here):
                every[g * blocks_here + inside] = both[:, inside * BLOCK : (inside + 1) * BLOCK]
        for i in range(blocks_here):
            mine = slice(2 * i * rows, 2 * (i + 1) * rows)
            for k in range(NEIGH):
                part = every[places[i, k], mine, :]
                out[i, :, k * BLOCK : (k + 1) * BLOCK] = part
                factors[places[i, k], mine, :] = part.astype(jnp.bfloat16)

    def forward():
        wide = jnp.concatenate([factors[place] for place in range(window)], axis=1)
        for base in range(0, n_src, PAIR):
            slots = range(base, min(base + PAIR, n_src))
            columns = [
                jnp.concatenate([held[g, slot] for g in range(len(sources))], axis=0) for slot in slots
            ]
            prod = jnp.dot(wide, jnp.concatenate(columns, axis=1), preferred_element_type=jnp.float32)
            for slot in slots:
                left = (slot - base) * cols
                for i in range(blocks_here):
                    top = prod[2 * i * rows : (2 * i + 1) * rows, left : left + cols]
                    low = prod[(2 * i + 1) * rows : 2 * (i + 1) * rows, left : left + cols]
                    yield slot, i, top[:, :half] - low[:, half:], top[:, half:] + low[:, :half]

    factors[...] = jnp.zeros_like(factors)
    for slot in range(n_src):
        for i in range(blocks_here):
            rows_bf = field[where[slot], i * rows : (i + 1) * rows, :]
            store(i, slot, rows_bf[:, :half], rows_bf[:, half:])

    zero = jnp.zeros((1, 128), jnp.float32)
    gg, qq, gh, hh, qw, ww = zero, zero, zero, zero, zero, zero
    adjoint(grad, True)
    for i in range(blocks_here):
        gg += fold(grad[i] * grad[i])
    for slot, i, re, im in forward():
        mine = slice(i * rows, (i + 1) * rows)
        qq += fold(re * re + im * im)
        image0[slot, mine, :half] = re
        image0[slot, mine, half:] = im
        store(i, slot, re.astype(jnp.bfloat16), im.astype(jnp.bfloat16))
    adjoint(hess, False)
    for i in range(blocks_here):
        gh += fold(hess[i] * grad[i])
        hh += fold(hess[i] * hess[i])
    for slot, i, re, im in forward():
        mine = slice(i * rows, (i + 1) * rows)
        ww += fold(re * re + im * im)
        qw += fold(re * image0[slot, mine, :half] + im * image0[slot, mine, half:])
        image1[slot, mine, :half] = re
        image1[slot, mine, half:] = im
    sums = jnp.concatenate([gg, qq, gh, hh, qw, ww, zero, zero], axis=0)
    sums_out[...] = sums
    share_bf = along(sums).astype(jnp.bfloat16)
    share = share_bf.astype(jnp.float32)
    height = blocks_here * rows
    for slot in range(n_src):
        first = image0[slot]
        images[where[slot], :height] = first.astype(jnp.bfloat16)
        images[where[slot], height : 2 * height] = (image1[slot] - share * first).astype(jnp.bfloat16)
        images[where[slot], 2 * height :] = jnp.broadcast_to(share_bf, (SHARE_ROWS, cols))


def combine_kernel(sums, images, grad, hess, refl_out, moved_out):
    n_src, height = images.shape[0], (images.shape[1] - SHARE_ROWS) // 2
    total = jnp.sum(sums[...], axis=1, keepdims=True)
    gg, qq, gh, hh, qw, ww = [total[i : i + 1] for i in range(6)]
    step0 = gg / qq
    grad_next = gg - 2 * step0 * gh + step0 * step0 * hh
    near = 1 + grad_next / gg
    image_sq = near * near * qq - 2 * near * step0 * qw + step0 * step0 * ww
    step1 = grad_next / image_sq
    c1 = step0 + step1 * near
    c2 = -step0 * step1
    for i in range(grad.shape[0]):
        refl_out[i] = c1 * grad[i] + c2 * hess[i]
    for s in range(n_src):
        share = images[s, 2 * height :].astype(jnp.float32)[:1, :1]
        first = images[s, :height].astype(jnp.float32)
        rest = images[s, height : 2 * height].astype(jnp.float32)
        moved_out[s] = (c1 + c2 * share) * first + c2 * rest


def summed(x, axis, count):
    if count & (count - 1):
        return lax.psum(x, axis)
    bit = 1
    while bit < count:
        radix = min(4, count // bit)
        others = [lax.ppermute(x, axis, [(d, d ^ (bit * m)) for d in range(count)]) for m in range(1, radix)]
        x = (x + others[0]) + (others[1] + others[2]) if radix == 4 else x + others[0]
        bit *= radix
    return x


def per_device(n_rcv, n_src, pplus, pminus, band):
    blocks_here = band.shape[0]
    rows = BLOCK // n_src
    cols = 2 * pplus.shape[2]
    order = ring_order(n_src)
    ahead = [(order[p], order[(p + 1) % n_src]) for p in range(n_src)]
    behind = [(d, s) for s, d in ahead]

    def swaps(first):
        pairs = [(r, r + 1) for r in range(first, n_rcv - 1, 2)]
        return pairs + [(d, s) for s, d in pairs]

    start = lax.optimization_barrier(pminus.reshape(blocks_here * BLOCK, cols))
    start = jnp.transpose(start.reshape(blocks_here, n_src, rows, cols), (1, 0, 2, 3))
    field = lax.all_to_all(start.reshape(n_src, blocks_here * rows, cols), "src", 0, 0, tiled=True)

    own = pplus.reshape(blocks_here * BLOCK, cols)
    outer = sorted(r for r, _ in swaps(1))

    def on_outer(pairs):
        return [(r * n_src + d, r * n_src + e) for r in outer for d, e in pairs]

    beyond = lax.ppermute(own, "rcv", swaps(1))
    chunks, far, shifts = [own], [beyond], [0]
    fwd = bwd = own
    far_fwd = far_bwd = beyond
    for step in range(1, n_src // 2 + 1):
        fwd = lax.ppermute(fwd, "src", ahead)
        far_fwd = lax.ppermute(far_fwd, ("rcv", "src"), on_outer(ahead))
        chunks.append(fwd)
        far.append(far_fwd)
        shifts.append(-step)
        if len(chunks) < n_src:
            bwd = lax.ppermute(bwd, "src", behind)
            far_bwd = lax.ppermute(far_bwd, ("rcv", "src"), on_outer(behind))
            chunks.append(bwd)
            far.append(far_bwd)
            shifts.append(step)
    near = [lax.ppermute(c, "rcv", swaps(0)) for c in chunks]

    any_spec = pl.BlockSpec(memory_space=pl.ANY)
    vmem = pl.BlockSpec(memory_space=pltpu.VMEM)
    band_cols = NEIGH * BLOCK
    grad, hess, images, sums = pl.pallas_call(
        functools.partial(maps_kernel, n_src, shifts),
        out_shape=(
            jax.ShapeDtypeStruct((blocks_here, 2 * rows, band_cols), jnp.float32),
            jax.ShapeDtypeStruct((blocks_here, 2 * rows, band_cols), jnp.float32),
            jax.ShapeDtypeStruct((n_src, 2 * blocks_here * rows + SHARE_ROWS, cols), jnp.bfloat16),
            jax.ShapeDtypeStruct((8, 128), jnp.float32),
        ),
        in_specs=[any_spec, vmem] + [any_spec] * (3 * n_src),
        out_specs=[vmem] * 4,
        scratch_shapes=[
            pltpu.SMEM(band.shape, jnp.int32),
            pltpu.VMEM((3, n_src, blocks_here * BLOCK, cols), jnp.bfloat16),
            pltpu.VMEM((blocks_here * 2 * rows, n_src * cols), jnp.bfloat16),
            pltpu.VMEM((3 * blocks_here, blocks_here * 2 * rows, BLOCK), jnp.float32),
            pltpu.VMEM((3 * blocks_here, blocks_here * 2 * rows, BLOCK), jnp.bfloat16),
            pltpu.VMEM((n_src, blocks_here * rows, cols), jnp.float32),
            pltpu.VMEM((n_src, blocks_here * rows, cols), jnp.float32),
            pltpu.SemaphoreType.DMA((3, n_src)),
            pltpu.SemaphoreType.DMA,
        ],
        compiler_params=pltpu.CompilerParams(vmem_limit_bytes=60 << 20),
        name="maps",
    )(band, field, *chunks, *near, *far)

    images = lax.all_to_all(images, "src", 0, 0, tiled=True)
    sums = summed(summed(sums, "rcv", n_rcv), "src", n_src)
    refl, moved = pl.pallas_call(
        combine_kernel,
        out_shape=(
            jax.ShapeDtypeStruct(grad.shape, jnp.float32),
            jax.ShapeDtypeStruct((n_src, blocks_here * rows, cols), jnp.float32),
        ),
        in_specs=[vmem] * 4,
        out_specs=[vmem] * 2,
        compiler_params=pltpu.CompilerParams(vmem_limit_bytes=8 << 20),
        name="combine",
    )(sums, images, grad, hess)

    refl = jnp.transpose(refl.reshape(blocks_here, 2, rows, NEIGH, BLOCK), (2, 0, 3, 1, 4))
    moved = jnp.transpose(moved.reshape(n_src, blocks_here, rows, cols), (1, 0, 2, 3))
    misfit = pminus.astype(jnp.float32) - moved.reshape(pminus.shape)
    return refl, misfit


def solution(mesh):
    return jax.shard_map(
        functools.partial(per_device, mesh.shape["rcv"], mesh.shape["src"]),
        mesh=mesh,
        in_specs=(P("rcv", None, "src"), P("rcv", None, "src"), P("rcv", None)),
        out_specs=(P("src", "rcv", None, None, None), P("rcv", None, "src")),
        check_vma=False,
    )
```

```python
import functools

import jax
import jax.numpy as jnp
from jax import lax
from jax.experimental import pallas as pl
from jax.experimental.pallas import tpu as pltpu
from jax.sharding import PartitionSpec as P

BLOCK = 256
NEIGH = 3
HALO_BLK = 2
ROWS_X = 2
SHARE_ROWS = 16
PAIR = 2


def ring_order(count):
    if count % ROWS_X or count < 2 * ROWS_X:
        return list(range(count))
    half = count // ROWS_X
    return [ROWS_X * p for p in range(half)] + [ROWS_X * p + 1 for p in reversed(range(half))]


def ring_place(count, index, shift):
    if count % ROWS_X or count < 2 * ROWS_X:
        return lax.rem(index + shift + count, count)
    half, odd = count // ROWS_X, lax.rem(index, ROWS_X)
    step = (index - odd) // ROWS_X
    place = lax.rem(jnp.where(odd == 1, count - 1 - step, step) + shift + count, count)
    return jnp.where(place < half, ROWS_X * place, ROWS_X * (count - 1 - place) + 1)


def along(sums):
    total = jnp.sum(sums, axis=1, keepdims=True)
    qq, qw = total[1:2], total[4:5]
    return jnp.where(qq > 0, qw / jnp.where(qq > 0, qq, 1.0), 0.0)


def maps_kernel(n_src, shifts, *refs):
    band_in, field = refs[:2]
    ends = [2, 2 + n_src, 2 + 2 * n_src, 2 + 3 * n_src]
    sources = [refs[a:b] for a, b in zip(ends[:-1], ends[1:])]
    grad, hess, images, sums_out = refs[ends[3] : ends[3] + 4]
    band, held, lhs, every, factors, image0, image1, sems, band_sem = refs[ends[3] + 4 :]
    blocks_here = grad.shape[0]
    rows = grad.shape[1] // 2
    cols = field.shape[2]
    half = cols // 2
    window = blocks_here * len(sources)
    me_rcv, me_src = lax.axis_index("rcv"), lax.axis_index("src")
    odd = lax.rem(me_rcv, 2)
    where = [ring_place(n_src, me_src, shift) for shift in shifts]

    fetches = [
        [pltpu.make_async_copy(chunk, held.at[g, slot], sems.at[g, slot]) for slot, chunk in enumerate(group)]
        for g, group in enumerate(sources)
    ]
    band_fetch = pltpu.make_async_copy(band_in, band, band_sem)
    band_fetch.start()
    for fetch in sum(fetches, []):
        fetch.start()
    band_fetch.wait()

    places = {}
    for i in range(blocks_here):
        for k in range(NEIGH):
            offset = band[i, k] - me_rcv * blocks_here
            before, here = offset < 0, (offset >= 0) & (offset < blocks_here)
            group = jnp.where(here, 0, jnp.where(jnp.where(before, 1, 0) == odd, 1, 2))
            inside = jnp.where(before, offset + blocks_here, jnp.where(here, offset, offset - blocks_here))
            places[i, k] = group * blocks_here + inside

    def store(i, slot, re_bf, im_bf):
        top, low = slice(2 * i * rows, (2 * i + 1) * rows), slice((2 * i + 1) * rows, (2 * i + 2) * rows)
        left, right = slice(slot * cols, slot * cols + half), slice(slot * cols + half, (slot + 1) * cols)
        lhs[top, left] = re_bf
        lhs[top, right] = im_bf
        lhs[low, left] = im_bf
        lhs[low, right] = -re_bf

    def fold(x):
        total = x[:, :128]
        for c in range(128, x.shape[1], 128):
            total = total + x[:, c : c + 128]
        return jnp.sum(total, axis=0, keepdims=True)

    def adjoint(out, first):
        for g in range(len(sources)):
            if first:
                for fetch in fetches[g]:
                    fetch.wait()
            chunks = jnp.concatenate([held[g, slot] for slot in range(n_src)], axis=1)
            both = lax.dot_general(lhs[...], chunks, (((1,), (1,)), ((), ())), preferred_element_type=jnp.float32)
            for inside in range(blocks_here):
                every[g * blocks_here + inside] = both[:, inside * BLOCK : (inside + 1) * BLOCK]
        for i in range(blocks_here):
            mine = slice(2 * i * rows, 2 * (i + 1) * rows)
            for k in range(NEIGH):
                part = every[places[i, k], mine, :]
                out[i, :, k * BLOCK : (k + 1) * BLOCK] = part
                factors[places[i, k], mine, :] = part.astype(jnp.bfloat16)

    def forward():
        wide = jnp.concatenate([factors[place] for place in range(window)], axis=1)
        for base in range(0, n_src, PAIR):
            slots = range(base, min(base + PAIR, n_src))
            columns = [
                jnp.concatenate([held[g, slot] for g in range(len(sources))], axis=0) for slot in slots
            ]
            prod = jnp.dot(wide, jnp.concatenate(columns, axis=1), preferred_element_type=jnp.float32)
            for slot in slots:
                left = (slot - base) * cols
                for i in range(blocks_here):
                    top = prod[2 * i * rows : (2 * i + 1) * rows, left : left + cols]
                    low = prod[(2 * i + 1) * rows : 2 * (i + 1) * rows, left : left + cols]
                    yield slot, i, top[:, :half] - low[:, half:], top[:, half:] + low[:, :half]

    factors[...] = jnp.zeros_like(factors)
    for slot in range(n_src):
        for i in range(blocks_here):
            rows_bf = field[where[slot], i * rows : (i + 1) * rows, :]
            store(i, slot, rows_bf[:, :half], rows_bf[:, half:])

    zero = jnp.zeros((1, 128), jnp.float32)
    gg, qq, gh, hh, qw, ww = zero, zero, zero, zero, zero, zero
    adjoint(grad, True)
    for i in range(blocks_here):
        gg += fold(grad[i] * grad[i])
    for slot, i, re, im in forward():
        mine = slice(i * rows, (i + 1) * rows)
        qq += fold(re * re + im * im)
        image0[slot, mine, :half] = re
        image0[slot, mine, half:] = im
        store(i, slot, re.astype(jnp.bfloat16), im.astype(jnp.bfloat16))
    adjoint(hess, False)
    for i in range(blocks_here):
        gh += fold(hess[i] * grad[i])
        hh += fold(hess[i] * hess[i])
    for slot, i, re, im in forward():
        mine = slice(i * rows, (i + 1) * rows)
        ww += fold(re * re + im * im)
        qw += fold(re * image0[slot, mine, :half] + im * image0[slot, mine, half:])
        image1[slot, mine, :half] = re
        image1[slot, mine, half:] = im
    sums = jnp.concatenate([gg, qq, gh, hh, qw, ww, zero, zero], axis=0)
    sums_out[...] = sums
    share_bf = along(sums).astype(jnp.bfloat16)
    share = share_bf.astype(jnp.float32)
    height = blocks_here * rows
    for slot in range(n_src):
        first = image0[slot]
        images[where[slot], :height] = first.astype(jnp.bfloat16)
        images[where[slot], height : 2 * height] = (image1[slot] - share * first).astype(jnp.bfloat16)
        images[where[slot], 2 * height :] = jnp.broadcast_to(share_bf, (SHARE_ROWS, cols))


def combine_kernel(sums, images, grad, hess, start, refl_out, misfit_out):
    n_src, height = images.shape[0], (images.shape[1] - SHARE_ROWS) // 2
    total = jnp.sum(sums[...], axis=1, keepdims=True)
    gg, qq, gh, hh, qw, ww = [total[i : i + 1] for i in range(6)]
    step0 = gg / qq
    grad_next = gg - 2 * step0 * gh + step0 * step0 * hh
    near = 1 + grad_next / gg
    image_sq = near * near * qq - 2 * near * step0 * qw + step0 * step0 * ww
    step1 = grad_next / image_sq
    c1 = step0 + step1 * near
    c2 = -step0 * step1
    blocks_here, rows = grad.shape[0], grad.shape[1] // 2
    half = start.shape[2] // 2
    for i in range(blocks_here):
        for k in range(NEIGH):
            for t in range(2):
                part = (i, slice(t * rows, (t + 1) * rows), slice(k * BLOCK, (k + 1) * BLOCK))
                refl_out[:, i, k, t, :] = c1 * grad[part] + c2 * hess[part]
    for s in range(n_src):
        share = images[s, 2 * height :].astype(jnp.float32)[:1, :1]
        first = images[s, :height].astype(jnp.float32)
        rest = images[s, height : 2 * height].astype(jnp.float32)
        left = start[s].astype(jnp.float32) - ((c1 + c2 * share) * first + c2 * rest)
        for i in range(blocks_here):
            place = slice(i * BLOCK + s * rows, i * BLOCK + (s + 1) * rows)
            mine = left[i * rows : (i + 1) * rows]
            misfit_out[place, 0, :] = mine[:, :half]
            misfit_out[place, 1, :] = mine[:, half:]


def summed(x, axis, count):
    if count & (count - 1):
        return lax.psum(x, axis)
    bit = 1
    while bit < count:
        radix = min(4, count // bit)
        others = [lax.ppermute(x, axis, [(d, d ^ (bit * m)) for d in range(count)]) for m in range(1, radix)]
        x = (x + others[0]) + (others[1] + others[2]) if radix == 4 else x + others[0]
        bit *= radix
    return x


def per_device(n_rcv, n_src, pplus, pminus, band):
    blocks_here = band.shape[0]
    rows = BLOCK // n_src
    cols = 2 * pplus.shape[2]
    order = ring_order(n_src)
    ahead = [(order[p], order[(p + 1) % n_src]) for p in range(n_src)]
    behind = [(d, s) for s, d in ahead]

    def swaps(first):
        pairs = [(r, r + 1) for r in range(first, n_rcv - 1, 2)]
        return pairs + [(d, s) for s, d in pairs]

    start = lax.optimization_barrier(pminus.reshape(blocks_here * BLOCK, cols))
    start = jnp.transpose(start.reshape(blocks_here, n_src, rows, cols), (1, 0, 2, 3))
    start = start.reshape(n_src, blocks_here * rows, cols)
    field = lax.all_to_all(start, "src", 0, 0, tiled=True)

    own = pplus.reshape(blocks_here * BLOCK, cols)
    chunks, shifts = [own], [0]
    fwd = bwd = own
    for step in range(1, n_src // 2 + 1):
        fwd = lax.ppermute(fwd, "src", ahead)
        chunks.append(fwd)
        shifts.append(-step)
        if len(chunks) < n_src:
            bwd = lax.ppermute(bwd, "src", behind)
            chunks.append(bwd)
            shifts.append(step)
    near = [lax.ppermute(c, "rcv", swaps(0)) for c in chunks]
    far = [lax.ppermute(c, "rcv", swaps(1)) for c in chunks]
    any_spec = pl.BlockSpec(memory_space=pl.ANY)
    vmem = pl.BlockSpec(memory_space=pltpu.VMEM)
    band_cols = NEIGH * BLOCK
    grad, hess, images, sums = pl.pallas_call(
        functools.partial(maps_kernel, n_src, shifts),
        out_shape=(
            jax.ShapeDtypeStruct((blocks_here, 2 * rows, band_cols), jnp.float32),
            jax.ShapeDtypeStruct((blocks_here, 2 * rows, band_cols), jnp.float32),
            jax.ShapeDtypeStruct((n_src, 2 * blocks_here * rows + SHARE_ROWS, cols), jnp.bfloat16),
            jax.ShapeDtypeStruct((8, 128), jnp.float32),
        ),
        in_specs=[any_spec, vmem] + [any_spec] * (3 * n_src),
        out_specs=[vmem] * 4,
        scratch_shapes=[
            pltpu.SMEM(band.shape, jnp.int32),
            pltpu.VMEM((3, n_src, blocks_here * BLOCK, cols), jnp.bfloat16),
            pltpu.VMEM((blocks_here * 2 * rows, n_src * cols), jnp.bfloat16),
            pltpu.VMEM((3 * blocks_here, blocks_here * 2 * rows, BLOCK), jnp.float32),
            pltpu.VMEM((3 * blocks_here, blocks_here * 2 * rows, BLOCK), jnp.bfloat16),
            pltpu.VMEM((n_src, blocks_here * rows, cols), jnp.float32),
            pltpu.VMEM((n_src, blocks_here * rows, cols), jnp.float32),
            pltpu.SemaphoreType.DMA((3, n_src)),
            pltpu.SemaphoreType.DMA,
        ],
        compiler_params=pltpu.CompilerParams(vmem_limit_bytes=60 << 20),
        name="maps",
    )(band, field, *chunks, *near, *far)

    images = lax.all_to_all(images, "src", 0, 0, tiled=True)
    sums = summed(summed(sums, "rcv", n_rcv), "src", n_src)
    return tuple(
        pl.pallas_call(
            combine_kernel,
            out_shape=(
                jax.ShapeDtypeStruct((rows, blocks_here, NEIGH, 2, BLOCK), jnp.float32),
                jax.ShapeDtypeStruct(pminus.shape, jnp.float32),
            ),
            in_specs=[vmem] * 5,
            out_specs=[vmem] * 2,
            compiler_params=pltpu.CompilerParams(vmem_limit_bytes=16 << 20),
            name="combine",
        )(sums, images, grad, hess, start)
    )


def solution(mesh):
    return jax.shard_map(
        functools.partial(per_device, mesh.shape["rcv"], mesh.shape["src"]),
        mesh=mesh,
        in_specs=(P("rcv", None, "src"), P("rcv", None, "src"), P("rcv", None)),
        out_specs=(P("src", "rcv", None, None, None), P("rcv", None, "src")),
        check_vma=False,
    )
```

```python
import functools

import jax
import jax.numpy as jnp
from jax import lax
from jax.experimental import pallas as pl
from jax.experimental.pallas import tpu as pltpu
from jax.sharding import PartitionSpec as P

BLOCK = 256
NEIGH = 3
HALO_BLK = 2
ROWS_X = 2
SHARE_ROWS = 16
PAIR = 2


def ring_order(count):
    if count % ROWS_X or count < 2 * ROWS_X:
        return list(range(count))
    half = count // ROWS_X
    return [ROWS_X * p for p in range(half)] + [ROWS_X * p + 1 for p in reversed(range(half))]


def ring_place(count, index, shift):
    if count % ROWS_X or count < 2 * ROWS_X:
        return lax.rem(index + shift + count, count)
    half, odd = count // ROWS_X, lax.rem(index, ROWS_X)
    step = (index - odd) // ROWS_X
    place = lax.rem(jnp.where(odd == 1, count - 1 - step, step) + shift + count, count)
    return jnp.where(place < half, ROWS_X * place, ROWS_X * (count - 1 - place) + 1)


def along(sums):
    total = jnp.sum(sums, axis=1, keepdims=True)
    qq, qw = total[1:2], total[4:5]
    return jnp.where(qq > 0, qw / jnp.where(qq > 0, qq, 1.0), 0.0)


def maps_kernel(n_src, shifts, *refs):
    band_in, field = refs[:2]
    ends = [2, 2 + n_src, 2 + 2 * n_src, 2 + 3 * n_src]
    sources = [refs[a:b] for a, b in zip(ends[:-1], ends[1:])]
    grad, hess, images, sums_out = refs[ends[3] : ends[3] + 4]
    band, held, lhs, every, factors, image0, image1, sems, band_sem = refs[ends[3] + 4 :]
    blocks_here = grad.shape[0]
    rows = grad.shape[1] // 2
    cols = field.shape[2]
    half = cols // 2
    window = blocks_here * len(sources)
    me_rcv, me_src = lax.axis_index("rcv"), lax.axis_index("src")
    odd = lax.rem(me_rcv, 2)
    where = [ring_place(n_src, me_src, shift) for shift in shifts]

    fetches = [
        [pltpu.make_async_copy(chunk, held.at[g, slot], sems.at[g, slot]) for slot, chunk in enumerate(group)]
        for g, group in enumerate(sources)
    ]
    band_fetch = pltpu.make_async_copy(band_in, band, band_sem)
    band_fetch.start()
    for fetch in sum(fetches, []):
        fetch.start()
    band_fetch.wait()

    places = {}
    for i in range(blocks_here):
        for k in range(NEIGH):
            offset = band[i, k] - me_rcv * blocks_here
            before, here = offset < 0, (offset >= 0) & (offset < blocks_here)
            group = jnp.where(here, 0, jnp.where(jnp.where(before, 1, 0) == odd, 1, 2))
            inside = jnp.where(before, offset + blocks_here, jnp.where(here, offset, offset - blocks_here))
            places[i, k] = group * blocks_here + inside

    def store(i, slot, re_bf, im_bf):
        top, low = slice(2 * i * rows, (2 * i + 1) * rows), slice((2 * i + 1) * rows, (2 * i + 2) * rows)
        left, right = slice(slot * cols, slot * cols + half), slice(slot * cols + half, (slot + 1) * cols)
        lhs[top, left] = re_bf
        lhs[top, right] = im_bf
        lhs[low, left] = im_bf
        lhs[low, right] = -re_bf

    def fold(x):
        total = x[:, :128]
        for c in range(128, x.shape[1], 128):
            total = total + x[:, c : c + 128]
        return jnp.sum(total, axis=0, keepdims=True)

    def adjoint(out, first):
        for g in range(len(sources)):
            if first:
                for fetch in fetches[g]:
                    fetch.wait()
            chunks = jnp.concatenate([held[g, slot] for slot in range(n_src)], axis=1)
            both = lax.dot_general(lhs[...], chunks, (((1,), (1,)), ((), ())), preferred_element_type=jnp.float32)
            for inside in range(blocks_here):
                every[g * blocks_here + inside] = both[:, inside * BLOCK : (inside + 1) * BLOCK]
        for i in range(blocks_here):
            mine = slice(2 * i * rows, 2 * (i + 1) * rows)
            for k in range(NEIGH):
                part = every[places[i, k], mine, :]
                out[i, :, k * BLOCK : (k + 1) * BLOCK] = part
                factors[places[i, k], mine, :] = part.astype(jnp.bfloat16)

    def forward():
        wide = jnp.concatenate([factors[place] for place in range(window)], axis=1)
        for base in range(0, n_src, PAIR):
            slots = range(base, min(base + PAIR, n_src))
            columns = [
                jnp.concatenate([held[g, slot] for g in range(len(sources))], axis=0) for slot in slots
            ]
            prod = jnp.dot(wide, jnp.concatenate(columns, axis=1), preferred_element_type=jnp.float32)
            for slot in slots:
                left = (slot - base) * cols
                for i in range(blocks_here):
                    top = prod[2 * i * rows : (2 * i + 1) * rows, left : left + cols]
                    low = prod[(2 * i + 1) * rows : 2 * (i + 1) * rows, left : left + cols]
                    yield slot, i, top[:, :half] - low[:, half:], top[:, half:] + low[:, :half]

    factors[...] = jnp.zeros_like(factors)
    for slot in range(n_src):
        for i in range(blocks_here):
            rows_bf = field[where[slot], i * rows : (i + 1) * rows, :]
            store(i, slot, rows_bf[:, :half], rows_bf[:, half:])

    zero = jnp.zeros((1, 128), jnp.float32)
    gg, qq, gh, hh, qw, ww = zero, zero, zero, zero, zero, zero
    adjoint(grad, True)
    for i in range(blocks_here):
        gg += fold(grad[i] * grad[i])
    for slot, i, re, im in forward():
        mine = slice(i * rows, (i + 1) * rows)
        qq += fold(re * re + im * im)
        image0[slot, mine, :half] = re
        image0[slot, mine, half:] = im
        store(i, slot, re.astype(jnp.bfloat16), im.astype(jnp.bfloat16))
    adjoint(hess, False)
    for i in range(blocks_here):
        gh += fold(hess[i] * grad[i])
        hh += fold(hess[i] * hess[i])
    for slot, i, re, im in forward():
        mine = slice(i * rows, (i + 1) * rows)
        ww += fold(re * re + im * im)
        qw += fold(re * image0[slot, mine, :half] + im * image0[slot, mine, half:])
        image1[slot, mine, :half] = re
        image1[slot, mine, half:] = im
    sums = jnp.concatenate([gg, qq, gh, hh, qw, ww, zero, zero], axis=0)
    sums_out[...] = sums
    share_bf = along(sums).astype(jnp.bfloat16)
    share = share_bf.astype(jnp.float32)
    height = blocks_here * rows
    for slot in range(n_src):
        first = image0[slot]
        images[where[slot], :height] = first.astype(jnp.bfloat16)
        images[where[slot], height : 2 * height] = (image1[slot] - share * first).astype(jnp.bfloat16)
        images[where[slot], 2 * height :] = jnp.broadcast_to(share_bf, (SHARE_ROWS, cols))


def combine_kernel(sums, images, grad, hess, start, refl_out, misfit_out):
    n_src, height = images.shape[0], (images.shape[1] - SHARE_ROWS) // 2
    total = jnp.sum(sums[...], axis=1, keepdims=True)
    gg, qq, gh, hh, qw, ww = [total[i : i + 1] for i in range(6)]
    step0 = gg / qq
    grad_next = gg - 2 * step0 * gh + step0 * step0 * hh
    near = 1 + grad_next / gg
    image_sq = near * near * qq - 2 * near * step0 * qw + step0 * step0 * ww
    step1 = grad_next / image_sq
    c1 = step0 + step1 * near
    c2 = -step0 * step1
    blocks_here, rows = grad.shape[0], grad.shape[1] // 2
    half = start.shape[2] // 2
    for i in range(blocks_here):
        for k in range(NEIGH):
            for t in range(2):
                part = (i, slice(t * rows, (t + 1) * rows), slice(k * BLOCK, (k + 1) * BLOCK))
                refl_out[:, i, k, t, :] = c1 * grad[part] + c2 * hess[part]
    for s in range(n_src):
        share = images[s, 2 * height :].astype(jnp.float32)[:1, :1]
        first = images[s, :height].astype(jnp.float32)
        rest = images[s, height : 2 * height].astype(jnp.float32)
        left = start[s].astype(jnp.float32) - ((c1 + c2 * share) * first + c2 * rest)
        for i in range(blocks_here):
            place = slice(i * BLOCK + s * rows, i * BLOCK + (s + 1) * rows)
            mine = left[i * rows : (i + 1) * rows]
            misfit_out[place, 0, :] = mine[:, :half]
            misfit_out[place, 1, :] = mine[:, half:]


def summed(x, axis, count):
    if count & (count - 1):
        return lax.psum(x, axis)
    bit = 1
    while bit < count:
        radix = min(4, count // bit)
        others = [lax.ppermute(x, axis, [(d, d ^ (bit * m)) for d in range(count)]) for m in range(1, radix)]
        x = (x + others[0]) + (others[1] + others[2]) if radix == 4 else x + others[0]
        bit *= radix
    return x


def per_device(n_rcv, n_src, pplus, pminus, band):
    blocks_here = band.shape[0]
    rows = BLOCK // n_src
    cols = 2 * pplus.shape[2]
    order = ring_order(n_src)
    ahead = [(order[p], order[(p + 1) % n_src]) for p in range(n_src)]
    behind = [(d, s) for s, d in ahead]

    def swaps(first):
        pairs = [(r, r + 1) for r in range(first, n_rcv - 1, 2)]
        return pairs + [(d, s) for s, d in pairs]

    start = lax.optimization_barrier(pminus.reshape(blocks_here * BLOCK, cols))
    start = jnp.transpose(start.reshape(blocks_here, n_src, rows, cols), (1, 0, 2, 3))
    start = start.reshape(n_src, blocks_here * rows, cols)
    field = lax.all_to_all(start, "src", 0, 0, tiled=True)

    own = pplus.reshape(blocks_here * BLOCK, cols)
    chunks, shifts = [own], [0]
    fwd = bwd = own
    for step in range(1, n_src // 2 + 1):
        fwd = lax.ppermute(fwd, "src", ahead)
        chunks.append(fwd)
        shifts.append(-step)
        if len(chunks) < n_src:
            bwd = lax.ppermute(bwd, "src", behind)
            chunks.append(bwd)
            shifts.append(step)
    far = [lax.ppermute(c, "rcv", swaps(1)) for c in chunks]
    near = [lax.ppermute(c, "rcv", swaps(0)) for c in chunks]
    any_spec = pl.BlockSpec(memory_space=pl.ANY)
    vmem = pl.BlockSpec(memory_space=pltpu.VMEM)
    band_cols = NEIGH * BLOCK
    grad, hess, images, sums = pl.pallas_call(
        functools.partial(maps_kernel, n_src, shifts),
        out_shape=(
            jax.ShapeDtypeStruct((blocks_here, 2 * rows, band_cols), jnp.float32),
            jax.ShapeDtypeStruct((blocks_here, 2 * rows, band_cols), jnp.float32),
            jax.ShapeDtypeStruct((n_src, 2 * blocks_here * rows + SHARE_ROWS, cols), jnp.bfloat16),
            jax.ShapeDtypeStruct((8, 128), jnp.float32),
        ),
        in_specs=[any_spec, vmem] + [any_spec] * (3 * n_src),
        out_specs=[vmem] * 4,
        scratch_shapes=[
            pltpu.SMEM(band.shape, jnp.int32),
            pltpu.VMEM((3, n_src, blocks_here * BLOCK, cols), jnp.bfloat16),
            pltpu.VMEM((blocks_here * 2 * rows, n_src * cols), jnp.bfloat16),
            pltpu.VMEM((3 * blocks_here, blocks_here * 2 * rows, BLOCK), jnp.float32),
            pltpu.VMEM((3 * blocks_here, blocks_here * 2 * rows, BLOCK), jnp.bfloat16),
            pltpu.VMEM((n_src, blocks_here * rows, cols), jnp.float32),
            pltpu.VMEM((n_src, blocks_here * rows, cols), jnp.float32),
            pltpu.SemaphoreType.DMA((3, n_src)),
            pltpu.SemaphoreType.DMA,
        ],
        compiler_params=pltpu.CompilerParams(vmem_limit_bytes=60 << 20),
        name="maps",
    )(band, field, *chunks, *near, *far)

    images = lax.all_to_all(images, "src", 0, 0, tiled=True)
    sums = summed(summed(sums, "rcv", n_rcv), "src", n_src)
    return tuple(
        pl.pallas_call(
            combine_kernel,
            out_shape=(
                jax.ShapeDtypeStruct((rows, blocks_here, NEIGH, 2, BLOCK), jnp.float32),
                jax.ShapeDtypeStruct(pminus.shape, jnp.float32),
            ),
            in_specs=[vmem] * 5,
            out_specs=[vmem] * 2,
            compiler_params=pltpu.CompilerParams(vmem_limit_bytes=16 << 20),
            name="combine",
        )(sums, images, grad, hess, start)
    )


def solution(mesh):
    return jax.shard_map(
        functools.partial(per_device, mesh.shape["rcv"], mesh.shape["src"]),
        mesh=mesh,
        in_specs=(P("rcv", None, "src"), P("rcv", None, "src"), P("rcv", None)),
        out_specs=(P("src", "rcv", None, None, None), P("rcv", None, "src")),
        check_vma=False,
    )
```

```python
import functools

import jax
import jax.numpy as jnp
from jax import lax
from jax.experimental import pallas as pl
from jax.experimental.pallas import tpu as pltpu
from jax.sharding import PartitionSpec as P

BLOCK = 256
NEIGH = 3
HALO_BLK = 2
ROWS_X = 2
SHARE_ROWS = 16
PAIR = 2


def ring_order(count):
    if count % ROWS_X or count < 2 * ROWS_X:
        return list(range(count))
    half = count // ROWS_X
    return [ROWS_X * p for p in range(half)] + [ROWS_X * p + 1 for p in reversed(range(half))]


def ring_place(count, index, shift):
    if count % ROWS_X or count < 2 * ROWS_X:
        return lax.rem(index + shift + count, count)
    half, odd = count // ROWS_X, lax.rem(index, ROWS_X)
    step = (index - odd) // ROWS_X
    place = lax.rem(jnp.where(odd == 1, count - 1 - step, step) + shift + count, count)
    return jnp.where(place < half, ROWS_X * place, ROWS_X * (count - 1 - place) + 1)


def along(sums):
    total = jnp.sum(sums, axis=1, keepdims=True)
    qq, qw = total[1:2], total[4:5]
    return jnp.where(qq > 0, qw / jnp.where(qq > 0, qq, 1.0), 0.0)


def maps_kernel(n_src, shifts, *refs):
    band_in, field = refs[:2]
    ends = [2, 2 + n_src, 2 + 2 * n_src, 2 + 3 * n_src]
    sources = [refs[a:b] for a, b in zip(ends[:-1], ends[1:])]
    grad, hess, images, sums_out = refs[ends[3] : ends[3] + 4]
    band, held, lhs, every, factors, image0, image1, sems, band_sem = refs[ends[3] + 4 :]
    blocks_here = grad.shape[0]
    rows = grad.shape[1] // 2
    cols = field.shape[2]
    half = cols // 2
    window = blocks_here * len(sources)
    me_rcv, me_src = lax.axis_index("rcv"), lax.axis_index("src")
    odd = lax.rem(me_rcv, 2)
    where = [ring_place(n_src, me_src, shift) for shift in shifts]

    fetches = [
        [pltpu.make_async_copy(chunk, held.at[g, slot], sems.at[g, slot]) for slot, chunk in enumerate(group)]
        for g, group in enumerate(sources)
    ]
    band_fetch = pltpu.make_async_copy(band_in, band, band_sem)
    band_fetch.start()
    for fetch in sum(fetches, []):
        fetch.start()
    band_fetch.wait()

    places = {}
    for i in range(blocks_here):
        for k in range(NEIGH):
            offset = band[i, k] - me_rcv * blocks_here
            before, here = offset < 0, (offset >= 0) & (offset < blocks_here)
            group = jnp.where(here, 0, jnp.where(jnp.where(before, 1, 0) == odd, 1, 2))
            inside = jnp.where(before, offset + blocks_here, jnp.where(here, offset, offset - blocks_here))
            places[i, k] = group * blocks_here + inside

    def store(i, slot, re_bf, im_bf):
        top, low = slice(2 * i * rows, (2 * i + 1) * rows), slice((2 * i + 1) * rows, (2 * i + 2) * rows)
        left, right = slice(slot * cols, slot * cols + half), slice(slot * cols + half, (slot + 1) * cols)
        lhs[top, left] = re_bf
        lhs[top, right] = im_bf
        lhs[low, left] = im_bf
        lhs[low, right] = -re_bf

    def fold(x):
        total = x[:, :128]
        for c in range(128, x.shape[1], 128):
            total = total + x[:, c : c + 128]
        return jnp.sum(total, axis=0, keepdims=True)

    def adjoint(out, first):
        for g in range(len(sources)):
            if first:
                for fetch in fetches[g]:
                    fetch.wait()
            chunks = jnp.concatenate([held[g, slot] for slot in range(n_src)], axis=1)
            both = lax.dot_general(lhs[...], chunks, (((1,), (1,)), ((), ())), preferred_element_type=jnp.float32)
            for inside in range(blocks_here):
                every[g * blocks_here + inside] = both[:, inside * BLOCK : (inside + 1) * BLOCK]
        for i in range(blocks_here):
            mine = slice(2 * i * rows, 2 * (i + 1) * rows)
            for k in range(NEIGH):
                part = every[places[i, k], mine, :]
                out[i, :, k * BLOCK : (k + 1) * BLOCK] = part
                factors[places[i, k], mine, :] = part.astype(jnp.bfloat16)

    def forward():
        wide = jnp.concatenate([factors[place] for place in range(window)], axis=1)
        for base in range(0, n_src, PAIR):
            slots = range(base, min(base + PAIR, n_src))
            columns = [
                jnp.concatenate([held[g, slot] for g in range(len(sources))], axis=0) for slot in slots
            ]
            prod = jnp.dot(wide, jnp.concatenate(columns, axis=1), preferred_element_type=jnp.float32)
            for slot in slots:
                left = (slot - base) * cols
                for i in range(blocks_here):
                    top = prod[2 * i * rows : (2 * i + 1) * rows, left : left + cols]
                    low = prod[(2 * i + 1) * rows : 2 * (i + 1) * rows, left : left + cols]
                    yield slot, i, top[:, :half] - low[:, half:], top[:, half:] + low[:, :half]

    factors[...] = jnp.zeros_like(factors)
    for slot in range(n_src):
        for i in range(blocks_here):
            rows_bf = field[where[slot], i * rows : (i + 1) * rows, :]
            store(i, slot, rows_bf[:, :half], rows_bf[:, half:])

    zero = jnp.zeros((1, 128), jnp.float32)
    gg, qq, gh, hh, qw, ww = zero, zero, zero, zero, zero, zero
    adjoint(grad, True)
    for i in range(blocks_here):
        gg += fold(grad[i] * grad[i])
    for slot, i, re, im in forward():
        mine = slice(i * rows, (i + 1) * rows)
        qq += fold(re * re + im * im)
        image0[slot, mine, :half] = re
        image0[slot, mine, half:] = im
        store(i, slot, re.astype(jnp.bfloat16), im.astype(jnp.bfloat16))
    adjoint(hess, False)
    for i in range(blocks_here):
        gh += fold(hess[i] * grad[i])
        hh += fold(hess[i] * hess[i])
    for slot, i, re, im in forward():
        mine = slice(i * rows, (i + 1) * rows)
        ww += fold(re * re + im * im)
        qw += fold(re * image0[slot, mine, :half] + im * image0[slot, mine, half:])
        image1[slot, mine, :half] = re
        image1[slot, mine, half:] = im
    sums = jnp.concatenate([gg, qq, gh, hh, qw, ww, zero, zero], axis=0)
    sums_out[...] = sums
    share_bf = along(sums).astype(jnp.bfloat16)
    share = share_bf.astype(jnp.float32)
    height = blocks_here * rows
    for slot in range(n_src):
        first = image0[slot]
        images[where[slot], :height] = first.astype(jnp.bfloat16)
        images[where[slot], height : 2 * height] = (image1[slot] - share * first).astype(jnp.bfloat16)
        images[where[slot], 2 * height :] = jnp.broadcast_to(share_bf, (SHARE_ROWS, cols))


def combine_kernel(sums, images, grad, hess, start, refl_out, misfit_out):
    n_src, height = images.shape[0], (images.shape[1] - SHARE_ROWS) // 2
    total = jnp.sum(sums[...], axis=1, keepdims=True)
    gg, qq, gh, hh, qw, ww = [total[i : i + 1] for i in range(6)]
    step0 = gg / qq
    grad_next = gg - 2 * step0 * gh + step0 * step0 * hh
    near = 1 + grad_next / gg
    image_sq = near * near * qq - 2 * near * step0 * qw + step0 * step0 * ww
    step1 = grad_next / image_sq
    c1 = step0 + step1 * near
    c2 = -step0 * step1
    blocks_here, rows = grad.shape[0], grad.shape[1] // 2
    half = start.shape[2] // 2
    for i in range(blocks_here):
        for k in range(NEIGH):
            for t in range(2):
                part = (i, slice(t * rows, (t + 1) * rows), slice(k * BLOCK, (k + 1) * BLOCK))
                refl_out[:, i, k, t, :] = c1 * grad[part] + c2 * hess[part]
    for s in range(n_src):
        share = images[s, 2 * height :].astype(jnp.float32)[:1, :1]
        first = images[s, :height].astype(jnp.float32)
        rest = images[s, height : 2 * height].astype(jnp.float32)
        left = start[s].astype(jnp.float32) - ((c1 + c2 * share) * first + c2 * rest)
        for i in range(blocks_here):
            place = slice(i * BLOCK + s * rows, i * BLOCK + (s + 1) * rows)
            mine = left[i * rows : (i + 1) * rows]
            misfit_out[place, 0, :] = mine[:, :half]
            misfit_out[place, 1, :] = mine[:, half:]


def summed(x, axis, count):
    if count & (count - 1):
        return lax.psum(x, axis)
    bit = 1
    while bit < count:
        radix = min(4, count // bit)
        others = [lax.ppermute(x, axis, [(d, d ^ (bit * m)) for d in range(count)]) for m in range(1, radix)]
        x = (x + others[0]) + (others[1] + others[2]) if radix == 4 else x + others[0]
        bit *= radix
    return x


def per_device(n_rcv, n_src, pplus, pminus, band):
    blocks_here = band.shape[0]
    rows = BLOCK // n_src
    cols = 2 * pplus.shape[2]
    order = ring_order(n_src)
    ahead = [(order[p], order[(p + 1) % n_src]) for p in range(n_src)]
    behind = [(d, s) for s, d in ahead]

    def swaps(first):
        pairs = [(r, r + 1) for r in range(first, n_rcv - 1, 2)]
        return pairs + [(d, s) for s, d in pairs]

    start = lax.optimization_barrier(pminus.reshape(blocks_here * BLOCK, cols))
    start = jnp.transpose(start.reshape(blocks_here, n_src, rows, cols), (1, 0, 2, 3))
    start = start.reshape(n_src, blocks_here * rows, cols)
    field = lax.all_to_all(start, "src", 0, 0, tiled=True)

    own = pplus.reshape(blocks_here * BLOCK, cols)
    chunks, shifts = [own], [0]
    fwd = bwd = own
    for step in range(1, n_src // 2 + 1):
        fwd = lax.ppermute(fwd, "src", ahead)
        chunks.append(fwd)
        shifts.append(-step)
        if len(chunks) < n_src:
            bwd = lax.ppermute(bwd, "src", behind)
            chunks.append(bwd)
            shifts.append(step)
    near = [lax.ppermute(c, "rcv", swaps(0)) for c in chunks]
    far = [lax.ppermute(c, "rcv", swaps(1)) for c in chunks]
    near[-1], far[-1] = [pltpu.with_memory_space_constraint(x, pltpu.VMEM) for x in (near[-1], far[-1])]
    any_spec = pl.BlockSpec(memory_space=pl.ANY)
    vmem = pl.BlockSpec(memory_space=pltpu.VMEM)
    band_cols = NEIGH * BLOCK
    grad, hess, images, sums = pl.pallas_call(
        functools.partial(maps_kernel, n_src, shifts),
        out_shape=(
            jax.ShapeDtypeStruct((blocks_here, 2 * rows, band_cols), jnp.float32),
            jax.ShapeDtypeStruct((blocks_here, 2 * rows, band_cols), jnp.float32),
            jax.ShapeDtypeStruct((n_src, 2 * blocks_here * rows + SHARE_ROWS, cols), jnp.bfloat16),
            jax.ShapeDtypeStruct((8, 128), jnp.float32),
        ),
        in_specs=[any_spec, vmem] + [any_spec] * n_src + 2 * ([any_spec] * (n_src - 1) + [vmem]),
        out_specs=[vmem] * 4,
        scratch_shapes=[
            pltpu.SMEM(band.shape, jnp.int32),
            pltpu.VMEM((3, n_src, blocks_here * BLOCK, cols), jnp.bfloat16),
            pltpu.VMEM((blocks_here * 2 * rows, n_src * cols), jnp.bfloat16),
            pltpu.VMEM((3 * blocks_here, blocks_here * 2 * rows, BLOCK), jnp.float32),
            pltpu.VMEM((3 * blocks_here, blocks_here * 2 * rows, BLOCK), jnp.bfloat16),
            pltpu.VMEM((n_src, blocks_here * rows, cols), jnp.float32),
            pltpu.VMEM((n_src, blocks_here * rows, cols), jnp.float32),
            pltpu.SemaphoreType.DMA((3, n_src)),
            pltpu.SemaphoreType.DMA,
        ],
        compiler_params=pltpu.CompilerParams(vmem_limit_bytes=60 << 20),
        name="maps",
    )(band, field, *chunks, *near, *far)

    images = lax.all_to_all(images, "src", 0, 0, tiled=True)
    sums = summed(summed(sums, "rcv", n_rcv), "src", n_src)
    return tuple(
        pl.pallas_call(
            combine_kernel,
            out_shape=(
                jax.ShapeDtypeStruct((rows, blocks_here, NEIGH, 2, BLOCK), jnp.float32),
                jax.ShapeDtypeStruct(pminus.shape, jnp.float32),
            ),
            in_specs=[vmem] * 5,
            out_specs=[vmem] * 2,
            compiler_params=pltpu.CompilerParams(vmem_limit_bytes=16 << 20),
            name="combine",
        )(sums, images, grad, hess, start)
    )


def solution(mesh):
    return jax.shard_map(
        functools.partial(per_device, mesh.shape["rcv"], mesh.shape["src"]),
        mesh=mesh,
        in_specs=(P("rcv", None, "src"), P("rcv", None, "src"), P("rcv", None)),
        out_specs=(P("src", "rcv", None, None, None), P("rcv", None, "src")),
        check_vma=False,
    )
```

```python
import functools

import jax
import jax.numpy as jnp
from jax import lax
from jax.experimental import pallas as pl
from jax.experimental.pallas import tpu as pltpu
from jax.sharding import PartitionSpec as P

BLOCK = 256
NEIGH = 3
HALO_BLK = 2
ROWS_X = 2
SHARE_ROWS = 16
PAIR = 2


def ring_order(count):
    if count % ROWS_X or count < 2 * ROWS_X:
        return list(range(count))
    half = count // ROWS_X
    return [ROWS_X * p for p in range(half)] + [ROWS_X * p + 1 for p in reversed(range(half))]


def ring_place(count, index, shift):
    if count % ROWS_X or count < 2 * ROWS_X:
        return lax.rem(index + shift + count, count)
    half, odd = count // ROWS_X, lax.rem(index, ROWS_X)
    step = (index - odd) // ROWS_X
    place = lax.rem(jnp.where(odd == 1, count - 1 - step, step) + shift + count, count)
    return jnp.where(place < half, ROWS_X * place, ROWS_X * (count - 1 - place) + 1)


def along(sums):
    total = jnp.sum(sums, axis=1, keepdims=True)
    qq, qw = total[1:2], total[4:5]
    return jnp.where(qq > 0, qw / jnp.where(qq > 0, qq, 1.0), 0.0)


def maps_kernel(n_src, shifts, *refs):
    band_in, field = refs[:2]
    ends = [2, 2 + n_src, 2 + 2 * n_src, 2 + 3 * n_src]
    sources = [refs[a:b] for a, b in zip(ends[:-1], ends[1:])]
    grad, hess, images, sums_out = refs[ends[3] : ends[3] + 4]
    band, held, lhs, every, factors, image0, image1, sems, band_sem = refs[ends[3] + 4 :]
    blocks_here = grad.shape[0]
    rows = grad.shape[1] // 2
    cols = field.shape[2]
    half = cols // 2
    window = blocks_here * len(sources)
    me_rcv, me_src = lax.axis_index("rcv"), lax.axis_index("src")
    odd = lax.rem(me_rcv, 2)
    where = [ring_place(n_src, me_src, shift) for shift in shifts]

    fetches = [
        [pltpu.make_async_copy(chunk, held.at[g, slot], sems.at[g, slot]) for slot, chunk in enumerate(group)]
        for g, group in enumerate(sources)
    ]
    band_fetch = pltpu.make_async_copy(band_in, band, band_sem)
    band_fetch.start()
    for fetch in sum(fetches, []):
        fetch.start()
    band_fetch.wait()

    places = {}
    for i in range(blocks_here):
        for k in range(NEIGH):
            offset = band[i, k] - me_rcv * blocks_here
            before, here = offset < 0, (offset >= 0) & (offset < blocks_here)
            group = jnp.where(here, 0, jnp.where(jnp.where(before, 1, 0) == odd, 1, 2))
            inside = jnp.where(before, offset + blocks_here, jnp.where(here, offset, offset - blocks_here))
            places[i, k] = group * blocks_here + inside

    def store(i, slot, re_bf, im_bf):
        top, low = slice(2 * i * rows, (2 * i + 1) * rows), slice((2 * i + 1) * rows, (2 * i + 2) * rows)
        left, right = slice(slot * cols, slot * cols + half), slice(slot * cols + half, (slot + 1) * cols)
        lhs[top, left] = re_bf
        lhs[top, right] = im_bf
        lhs[low, left] = im_bf
        lhs[low, right] = -re_bf

    def fold(x):
        total = x[:, :128]
        for c in range(128, x.shape[1], 128):
            total = total + x[:, c : c + 128]
        return jnp.sum(total, axis=0, keepdims=True)

    def adjoint(out, first):
        for g in range(len(sources)):
            if first:
                for fetch in fetches[g]:
                    fetch.wait()
            chunks = jnp.concatenate([held[g, slot] for slot in range(n_src)], axis=1)
            both = lax.dot_general(lhs[...], chunks, (((1,), (1,)), ((), ())), preferred_element_type=jnp.float32)
            for inside in range(blocks_here):
                every[g * blocks_here + inside] = both[:, inside * BLOCK : (inside + 1) * BLOCK]
        for i in range(blocks_here):
            mine = slice(2 * i * rows, 2 * (i + 1) * rows)
            for k in range(NEIGH):
                part = every[places[i, k], mine, :]
                out[i, :, k * BLOCK : (k + 1) * BLOCK] = part
                factors[places[i, k], mine, :] = part.astype(jnp.bfloat16)

    def forward():
        wide = jnp.concatenate([factors[place] for place in range(window)], axis=1)
        for base in range(0, n_src, PAIR):
            slots = range(base, min(base + PAIR, n_src))
            columns = [
                jnp.concatenate([held[g, slot] for g in range(len(sources))], axis=0) for slot in slots
            ]
            prod = jnp.dot(wide, jnp.concatenate(columns, axis=1), preferred_element_type=jnp.float32)
            for slot in slots:
                left = (slot - base) * cols
                for i in range(blocks_here):
                    top = prod[2 * i * rows : (2 * i + 1) * rows, left : left + cols]
                    low = prod[(2 * i + 1) * rows : 2 * (i + 1) * rows, left : left + cols]
                    yield slot, i, top[:, :half] - low[:, half:], top[:, half:] + low[:, :half]

    factors[...] = jnp.zeros_like(factors)
    for slot in range(n_src):
        for i in range(blocks_here):
            rows_bf = field[where[slot], i * rows : (i + 1) * rows, :]
            store(i, slot, rows_bf[:, :half], rows_bf[:, half:])

    zero = jnp.zeros((1, 128), jnp.float32)
    gg, qq, gh, hh, qw, ww = zero, zero, zero, zero, zero, zero
    adjoint(grad, True)
    for i in range(blocks_here):
        gg += fold(grad[i] * grad[i])
    for slot, i, re, im in forward():
        mine = slice(i * rows, (i + 1) * rows)
        qq += fold(re * re + im * im)
        image0[slot, mine, :half] = re
        image0[slot, mine, half:] = im
        store(i, slot, re.astype(jnp.bfloat16), im.astype(jnp.bfloat16))
    adjoint(hess, False)
    for i in range(blocks_here):
        gh += fold(hess[i] * grad[i])
        hh += fold(hess[i] * hess[i])
    for slot, i, re, im in forward():
        mine = slice(i * rows, (i + 1) * rows)
        ww += fold(re * re + im * im)
        qw += fold(re * image0[slot, mine, :half] + im * image0[slot, mine, half:])
        image1[slot, mine, :half] = re
        image1[slot, mine, half:] = im
    sums = jnp.concatenate([gg, qq, gh, hh, qw, ww, zero, zero], axis=0)
    sums_out[...] = sums
    share_bf = along(sums).astype(jnp.bfloat16)
    share = share_bf.astype(jnp.float32)
    height = blocks_here * rows
    for slot in range(n_src):
        first = image0[slot]
        images[where[slot], :height] = first.astype(jnp.bfloat16)
        images[where[slot], height : 2 * height] = (image1[slot] - share * first).astype(jnp.bfloat16)
        images[where[slot], 2 * height :] = jnp.broadcast_to(share_bf, (SHARE_ROWS, cols))


def combine_kernel(sums, images, grad, hess, start, refl_out, misfit_out):
    n_src, height = images.shape[0], (images.shape[1] - SHARE_ROWS) // 2
    total = jnp.sum(sums[...], axis=1, keepdims=True)
    gg, qq, gh, hh, qw, ww = [total[i : i + 1] for i in range(6)]
    step0 = gg / qq
    grad_next = gg - 2 * step0 * gh + step0 * step0 * hh
    near = 1 + grad_next / gg
    image_sq = near * near * qq - 2 * near * step0 * qw + step0 * step0 * ww
    step1 = grad_next / image_sq
    c1 = step0 + step1 * near
    c2 = -step0 * step1
    blocks_here, rows = grad.shape[0], grad.shape[1] // 2
    half = start.shape[2] // 2
    for i in range(blocks_here):
        for k in range(NEIGH):
            for t in range(2):
                part = (i, slice(t * rows, (t + 1) * rows), slice(k * BLOCK, (k + 1) * BLOCK))
                refl_out[:, i, k, t, :] = c1 * grad[part] + c2 * hess[part]
    for s in range(n_src):
        share = images[s, 2 * height :].astype(jnp.float32)[:1, :1]
        first = images[s, :height].astype(jnp.float32)
        rest = images[s, height : 2 * height].astype(jnp.float32)
        left = start[s].astype(jnp.float32) - ((c1 + c2 * share) * first + c2 * rest)
        for i in range(blocks_here):
            place = slice(i * BLOCK + s * rows, i * BLOCK + (s + 1) * rows)
            mine = left[i * rows : (i + 1) * rows]
            misfit_out[place, 0, :] = mine[:, :half]
            misfit_out[place, 1, :] = mine[:, half:]


def summed(x, axis, count):
    if count & (count - 1):
        return lax.psum(x, axis)
    bit = 1
    while bit < count:
        radix = min(4, count // bit)
        others = [lax.ppermute(x, axis, [(d, d ^ (bit * m)) for d in range(count)]) for m in range(1, radix)]
        x = (x + others[0]) + (others[1] + others[2]) if radix == 4 else x + others[0]
        bit *= radix
    return x


def per_device(n_rcv, n_src, pplus, pminus, band):
    blocks_here = band.shape[0]
    rows = BLOCK // n_src
    cols = 2 * pplus.shape[2]
    order = ring_order(n_src)
    ahead = [(order[p], order[(p + 1) % n_src]) for p in range(n_src)]
    behind = [(d, s) for s, d in ahead]

    def swaps(first):
        pairs = [(r, r + 1) for r in range(first, n_rcv - 1, 2)]
        return pairs + [(d, s) for s, d in pairs]

    start = lax.optimization_barrier(pminus.reshape(blocks_here * BLOCK, cols))
    start = jnp.transpose(start.reshape(blocks_here, n_src, rows, cols), (1, 0, 2, 3))
    start = start.reshape(n_src, blocks_here * rows, cols)
    field = lax.all_to_all(start, "src", 0, 0, tiled=True)

    own = pplus.reshape(blocks_here * BLOCK, cols)
    chunks, shifts = [own], [0]
    fwd = bwd = own
    for step in range(1, n_src // 2 + 1):
        fwd = lax.ppermute(fwd, "src", ahead)
        chunks.append(fwd)
        shifts.append(-step)
        if len(chunks) < n_src:
            bwd = lax.ppermute(bwd, "src", behind)
            chunks.append(bwd)
            shifts.append(step)
    last, field = lax.optimization_barrier((chunks[-1], field))
    near = [lax.ppermute(c, "rcv", swaps(0)) for c in chunks[:-1] + [last]]
    far = [lax.ppermute(c, "rcv", swaps(1)) for c in chunks]
    near[-1], far[-1] = [pltpu.with_memory_space_constraint(x, pltpu.VMEM) for x in (near[-1], far[-1])]
    any_spec = pl.BlockSpec(memory_space=pl.ANY)
    vmem = pl.BlockSpec(memory_space=pltpu.VMEM)
    band_cols = NEIGH * BLOCK
    grad, hess, images, sums = pl.pallas_call(
        functools.partial(maps_kernel, n_src, shifts),
        out_shape=(
            jax.ShapeDtypeStruct((blocks_here, 2 * rows, band_cols), jnp.float32),
            jax.ShapeDtypeStruct((blocks_here, 2 * rows, band_cols), jnp.float32),
            jax.ShapeDtypeStruct((n_src, 2 * blocks_here * rows + SHARE_ROWS, cols), jnp.bfloat16),
            jax.ShapeDtypeStruct((8, 128), jnp.float32),
        ),
        in_specs=[any_spec, vmem] + [any_spec] * n_src + 2 * ([any_spec] * (n_src - 1) + [vmem]),
        out_specs=[vmem] * 4,
        scratch_shapes=[
            pltpu.SMEM(band.shape, jnp.int32),
            pltpu.VMEM((3, n_src, blocks_here * BLOCK, cols), jnp.bfloat16),
            pltpu.VMEM((blocks_here * 2 * rows, n_src * cols), jnp.bfloat16),
            pltpu.VMEM((3 * blocks_here, blocks_here * 2 * rows, BLOCK), jnp.float32),
            pltpu.VMEM((3 * blocks_here, blocks_here * 2 * rows, BLOCK), jnp.bfloat16),
            pltpu.VMEM((n_src, blocks_here * rows, cols), jnp.float32),
            pltpu.VMEM((n_src, blocks_here * rows, cols), jnp.float32),
            pltpu.SemaphoreType.DMA((3, n_src)),
            pltpu.SemaphoreType.DMA,
        ],
        compiler_params=pltpu.CompilerParams(vmem_limit_bytes=60 << 20),
        name="maps",
    )(band, field, *chunks, *near, *far)

    images = lax.all_to_all(images, "src", 0, 0, tiled=True)
    sums = summed(summed(sums, "rcv", n_rcv), "src", n_src)
    return tuple(
        pl.pallas_call(
            combine_kernel,
            out_shape=(
                jax.ShapeDtypeStruct((rows, blocks_here, NEIGH, 2, BLOCK), jnp.float32),
                jax.ShapeDtypeStruct(pminus.shape, jnp.float32),
            ),
            in_specs=[vmem] * 5,
            out_specs=[vmem] * 2,
            compiler_params=pltpu.CompilerParams(vmem_limit_bytes=16 << 20),
            name="combine",
        )(sums, images, grad, hess, start)
    )


def solution(mesh):
    return jax.shard_map(
        functools.partial(per_device, mesh.shape["rcv"], mesh.shape["src"]),
        mesh=mesh,
        in_specs=(P("rcv", None, "src"), P("rcv", None, "src"), P("rcv", None)),
        out_specs=(P("src", "rcv", None, None, None), P("rcv", None, "src")),
        check_vma=False,
    )
```

```python
import functools

import jax
import jax.numpy as jnp
from jax import lax
from jax.experimental import pallas as pl
from jax.experimental.pallas import tpu as pltpu
from jax.sharding import PartitionSpec as P

BLOCK = 256
NEIGH = 3
HALO_BLK = 2
ROWS_X = 2
SHARE_ROWS = 16
PAIR = 2
IN_PLACE = 8


def ring_order(count):
    if count % ROWS_X or count < 2 * ROWS_X:
        return list(range(count))
    half = count // ROWS_X
    return [ROWS_X * p for p in range(half)] + [ROWS_X * p + 1 for p in reversed(range(half))]


def ring_place(count, index, shift):
    if count % ROWS_X or count < 2 * ROWS_X:
        return lax.rem(index + shift + count, count)
    half, odd = count // ROWS_X, lax.rem(index, ROWS_X)
    step = (index - odd) // ROWS_X
    place = lax.rem(jnp.where(odd == 1, count - 1 - step, step) + shift + count, count)
    return jnp.where(place < half, ROWS_X * place, ROWS_X * (count - 1 - place) + 1)


def along(sums):
    total = jnp.sum(sums, axis=1, keepdims=True)
    qq, qw = total[1:2], total[4:5]
    return jnp.where(qq > 0, qw / jnp.where(qq > 0, qq, 1.0), 0.0)


def maps_kernel(n_src, shifts, *refs):
    band_in, field = refs[:2]
    ends = [2, 2 + n_src, 2 + 2 * n_src, 2 + 3 * n_src]
    sources = [refs[a:b] for a, b in zip(ends[:-1], ends[1:])]
    grad, hess, images, sums_out = refs[ends[3] : ends[3] + 4]
    band, held, lhs, every, factors, image0, image1, sems, band_sem = refs[ends[3] + 4 :]
    blocks_here = grad.shape[0]
    rows = grad.shape[1] // 2
    cols = field.shape[2]
    half = cols // 2
    window = blocks_here * len(sources)
    me_rcv, me_src = lax.axis_index("rcv"), lax.axis_index("src")
    odd = lax.rem(me_rcv, 2)
    where = [ring_place(n_src, me_src, shift) for shift in shifts]

    fetches = [
        [
            pltpu.make_async_copy(source, held.at[g, slot], sems.at[g, slot])
            for slot, source in enumerate(group)
            if g or slot >= IN_PLACE
        ]
        for g, group in enumerate(sources)
    ]

    def chunk(g, slot):
        return held[g, slot] if g or slot >= IN_PLACE else sources[0][slot][...]

    band_fetch = pltpu.make_async_copy(band_in, band, band_sem)
    band_fetch.start()
    for fetch in sum(fetches, []):
        fetch.start()
    band_fetch.wait()

    places = {}
    for i in range(blocks_here):
        for k in range(NEIGH):
            offset = band[i, k] - me_rcv * blocks_here
            before, here = offset < 0, (offset >= 0) & (offset < blocks_here)
            group = jnp.where(here, 0, jnp.where(jnp.where(before, 1, 0) == odd, 1, 2))
            inside = jnp.where(before, offset + blocks_here, jnp.where(here, offset, offset - blocks_here))
            places[i, k] = group * blocks_here + inside

    def store(i, slot, re_bf, im_bf):
        top, low = slice(2 * i * rows, (2 * i + 1) * rows), slice((2 * i + 1) * rows, (2 * i + 2) * rows)
        left, right = slice(slot * cols, slot * cols + half), slice(slot * cols + half, (slot + 1) * cols)
        lhs[top, left] = re_bf
        lhs[top, right] = im_bf
        lhs[low, left] = im_bf
        lhs[low, right] = -re_bf

    def fold(x):
        total = x[:, :128]
        for c in range(128, x.shape[1], 128):
            total = total + x[:, c : c + 128]
        return jnp.sum(total, axis=0, keepdims=True)

    def adjoint(out, first):
        for g in range(len(sources)):
            if first:
                for fetch in fetches[g]:
                    fetch.wait()
            chunks = jnp.concatenate([chunk(g, slot) for slot in range(n_src)], axis=1)
            both = lax.dot_general(lhs[...], chunks, (((1,), (1,)), ((), ())), preferred_element_type=jnp.float32)
            for inside in range(blocks_here):
                every[g * blocks_here + inside] = both[:, inside * BLOCK : (inside + 1) * BLOCK]
        for i in range(blocks_here):
            mine = slice(2 * i * rows, 2 * (i + 1) * rows)
            for k in range(NEIGH):
                part = every[places[i, k], mine, :]
                out[i, :, k * BLOCK : (k + 1) * BLOCK] = part
                factors[places[i, k], mine, :] = part.astype(jnp.bfloat16)

    def forward():
        wide = jnp.concatenate([factors[place] for place in range(window)], axis=1)
        for base in range(0, n_src, PAIR):
            slots = range(base, min(base + PAIR, n_src))
            columns = [
                jnp.concatenate([chunk(g, slot) for g in range(len(sources))], axis=0) for slot in slots
            ]
            prod = jnp.dot(wide, jnp.concatenate(columns, axis=1), preferred_element_type=jnp.float32)
            for slot in slots:
                left = (slot - base) * cols
                for i in range(blocks_here):
                    top = prod[2 * i * rows : (2 * i + 1) * rows, left : left + cols]
                    low = prod[(2 * i + 1) * rows : 2 * (i + 1) * rows, left : left + cols]
                    yield slot, i, top[:, :half] - low[:, half:], top[:, half:] + low[:, :half]

    factors[...] = jnp.zeros_like(factors)
    for slot in range(n_src):
        for i in range(blocks_here):
            rows_bf = field[where[slot], i * rows : (i + 1) * rows, :]
            store(i, slot, rows_bf[:, :half], rows_bf[:, half:])

    zero = jnp.zeros((1, 128), jnp.float32)
    gg, qq, gh, hh, qw, ww = zero, zero, zero, zero, zero, zero
    adjoint(grad, True)
    for i in range(blocks_here):
        gg += fold(grad[i] * grad[i])
    for slot, i, re, im in forward():
        mine = slice(i * rows, (i + 1) * rows)
        qq += fold(re * re + im * im)
        image0[slot, mine, :half] = re
        image0[slot, mine, half:] = im
        store(i, slot, re.astype(jnp.bfloat16), im.astype(jnp.bfloat16))
    adjoint(hess, False)
    for i in range(blocks_here):
        gh += fold(hess[i] * grad[i])
        hh += fold(hess[i] * hess[i])
    for slot, i, re, im in forward():
        mine = slice(i * rows, (i + 1) * rows)
        ww += fold(re * re + im * im)
        qw += fold(re * image0[slot, mine, :half] + im * image0[slot, mine, half:])
        image1[slot, mine, :half] = re
        image1[slot, mine, half:] = im
    sums = jnp.concatenate([gg, qq, gh, hh, qw, ww, zero, zero], axis=0)
    sums_out[...] = sums
    share_bf = along(sums).astype(jnp.bfloat16)
    share = share_bf.astype(jnp.float32)
    height = blocks_here * rows
    for slot in range(n_src):
        first = image0[slot]
        images[where[slot], :height] = first.astype(jnp.bfloat16)
        images[where[slot], height : 2 * height] = (image1[slot] - share * first).astype(jnp.bfloat16)
        images[where[slot], 2 * height :] = jnp.broadcast_to(share_bf, (SHARE_ROWS, cols))


def combine_kernel(sums, images, grad, hess, start, refl_out, misfit_out):
    n_src, height = images.shape[0], (images.shape[1] - SHARE_ROWS) // 2
    total = jnp.sum(sums[...], axis=1, keepdims=True)
    gg, qq, gh, hh, qw, ww = [total[i : i + 1] for i in range(6)]
    step0 = gg / qq
    grad_next = gg - 2 * step0 * gh + step0 * step0 * hh
    near = 1 + grad_next / gg
    image_sq = near * near * qq - 2 * near * step0 * qw + step0 * step0 * ww
    step1 = grad_next / image_sq
    c1 = step0 + step1 * near
    c2 = -step0 * step1
    blocks_here, rows = grad.shape[0], grad.shape[1] // 2
    half = start.shape[2] // 2
    for i in range(blocks_here):
        for k in range(NEIGH):
            for t in range(2):
                part = (i, slice(t * rows, (t + 1) * rows), slice(k * BLOCK, (k + 1) * BLOCK))
                refl_out[:, i, k, t, :] = c1 * grad[part] + c2 * hess[part]
    for s in range(n_src):
        share = images[s, 2 * height :].astype(jnp.float32)[:1, :1]
        first = images[s, :height].astype(jnp.float32)
        rest = images[s, height : 2 * height].astype(jnp.float32)
        left = start[s].astype(jnp.float32) - ((c1 + c2 * share) * first + c2 * rest)
        for i in range(blocks_here):
            place = slice(i * BLOCK + s * rows, i * BLOCK + (s + 1) * rows)
            mine = left[i * rows : (i + 1) * rows]
            misfit_out[place, 0, :] = mine[:, :half]
            misfit_out[place, 1, :] = mine[:, half:]


def summed(x, axis, count):
    if count & (count - 1):
        return lax.psum(x, axis)
    bit = 1
    while bit < count:
        radix = min(4, count // bit)
        others = [lax.ppermute(x, axis, [(d, d ^ (bit * m)) for d in range(count)]) for m in range(1, radix)]
        x = (x + others[0]) + (others[1] + others[2]) if radix == 4 else x + others[0]
        bit *= radix
    return x


def per_device(n_rcv, n_src, pplus, pminus, band):
    blocks_here = band.shape[0]
    rows = BLOCK // n_src
    cols = 2 * pplus.shape[2]
    order = ring_order(n_src)
    ahead = [(order[p], order[(p + 1) % n_src]) for p in range(n_src)]
    behind = [(d, s) for s, d in ahead]

    def swaps(first):
        pairs = [(r, r + 1) for r in range(first, n_rcv - 1, 2)]
        return pairs + [(d, s) for s, d in pairs]

    start = lax.optimization_barrier(pminus.reshape(blocks_here * BLOCK, cols))
    start = jnp.transpose(start.reshape(blocks_here, n_src, rows, cols), (1, 0, 2, 3))
    start = start.reshape(n_src, blocks_here * rows, cols)
    field = lax.all_to_all(start, "src", 0, 0, tiled=True)

    own = pplus.reshape(blocks_here * BLOCK, cols)
    chunks, shifts = [own], [0]
    fwd = bwd = own
    for step in range(1, n_src // 2 + 1):
        fwd = lax.ppermute(fwd, "src", ahead)
        chunks.append(fwd)
        shifts.append(-step)
        if len(chunks) < n_src:
            bwd = lax.ppermute(bwd, "src", behind)
            chunks.append(bwd)
            shifts.append(step)
    near = [lax.ppermute(c, "rcv", swaps(0)) for c in chunks]
    far = [lax.ppermute(c, "rcv", swaps(1)) for c in chunks]
    near[-1], far[-1] = [pltpu.with_memory_space_constraint(x, pltpu.VMEM) for x in (near[-1], far[-1])]
    any_spec = pl.BlockSpec(memory_space=pl.ANY)
    vmem = pl.BlockSpec(memory_space=pltpu.VMEM)
    band_cols, kept = NEIGH * BLOCK, min(IN_PLACE, n_src)
    grad, hess, images, sums = pl.pallas_call(
        functools.partial(maps_kernel, n_src, shifts),
        out_shape=(
            jax.ShapeDtypeStruct((blocks_here, 2 * rows, band_cols), jnp.float32),
            jax.ShapeDtypeStruct((blocks_here, 2 * rows, band_cols), jnp.float32),
            jax.ShapeDtypeStruct((n_src, 2 * blocks_here * rows + SHARE_ROWS, cols), jnp.bfloat16),
            jax.ShapeDtypeStruct((8, 128), jnp.float32),
        ),
        in_specs=[any_spec, vmem] + [vmem] * kept + [any_spec] * (n_src - kept) + 2 * ([any_spec] * (n_src - 1) + [vmem]),
        out_specs=[vmem] * 4,
        scratch_shapes=[
            pltpu.SMEM(band.shape, jnp.int32),
            pltpu.VMEM((3, n_src, blocks_here * BLOCK, cols), jnp.bfloat16),
            pltpu.VMEM((blocks_here * 2 * rows, n_src * cols), jnp.bfloat16),
            pltpu.VMEM((3 * blocks_here, blocks_here * 2 * rows, BLOCK), jnp.float32),
            pltpu.VMEM((3 * blocks_here, blocks_here * 2 * rows, BLOCK), jnp.bfloat16),
            pltpu.VMEM((n_src, blocks_here * rows, cols), jnp.float32),
            pltpu.VMEM((n_src, blocks_here * rows, cols), jnp.float32),
            pltpu.SemaphoreType.DMA((3, n_src)),
            pltpu.SemaphoreType.DMA,
        ],
        compiler_params=pltpu.CompilerParams(vmem_limit_bytes=58 << 20),
        name="maps",
    )(band, field, *[pltpu.with_memory_space_constraint(c, pltpu.VMEM) for c in chunks[:kept]], *chunks[kept:], *near, *far)

    images = lax.all_to_all(images, "src", 0, 0, tiled=True)
    sums = summed(summed(sums, "rcv", n_rcv), "src", n_src)
    return tuple(
        pl.pallas_call(
            combine_kernel,
            out_shape=(
                jax.ShapeDtypeStruct((rows, blocks_here, NEIGH, 2, BLOCK), jnp.float32),
                jax.ShapeDtypeStruct(pminus.shape, jnp.float32),
            ),
            in_specs=[vmem] * 5,
            out_specs=[vmem] * 2,
            compiler_params=pltpu.CompilerParams(vmem_limit_bytes=16 << 20),
            name="combine",
        )(sums, images, grad, hess, start)
    )


def solution(mesh):
    return jax.shard_map(
        functools.partial(per_device, mesh.shape["rcv"], mesh.shape["src"]),
        mesh=mesh,
        in_specs=(P("rcv", None, "src"), P("rcv", None, "src"), P("rcv", None)),
        out_specs=(P("src", "rcv", None, None, None), P("rcv", None, "src")),
        check_vma=False,
    )
```

```python
import functools

import jax
import jax.numpy as jnp
from jax import lax
from jax.experimental import pallas as pl
from jax.experimental.pallas import tpu as pltpu
from jax.sharding import PartitionSpec as P

BLOCK = 256
NEIGH = 3
HALO_BLK = 2
ROWS_X = 2
SHARE_ROWS = 16
PAIR = 2
IN_PLACE = 8
LATE = 3


def ring_order(count):
    if count % ROWS_X or count < 2 * ROWS_X:
        return list(range(count))
    half = count // ROWS_X
    return [ROWS_X * p for p in range(half)] + [ROWS_X * p + 1 for p in reversed(range(half))]


def ring_place(count, index, shift):
    if count % ROWS_X or count < 2 * ROWS_X:
        return lax.rem(index + shift + count, count)
    half, odd = count // ROWS_X, lax.rem(index, ROWS_X)
    step = (index - odd) // ROWS_X
    place = lax.rem(jnp.where(odd == 1, count - 1 - step, step) + shift + count, count)
    return jnp.where(place < half, ROWS_X * place, ROWS_X * (count - 1 - place) + 1)


def along(sums):
    total = jnp.sum(sums, axis=1, keepdims=True)
    qq, qw = total[1:2], total[4:5]
    return jnp.where(qq > 0, qw / jnp.where(qq > 0, qq, 1.0), 0.0)


def in_place(n_src, g, slot):
    return slot >= n_src - LATE if g else slot < IN_PLACE


def maps_kernel(n_src, shifts, *refs):
    band_in, field = refs[:2]
    ends = [2, 2 + n_src, 2 + 2 * n_src, 2 + 3 * n_src]
    sources = [refs[a:b] for a, b in zip(ends[:-1], ends[1:])]
    grad, hess, images, sums_out = refs[ends[3] : ends[3] + 4]
    band, held, lhs, every, factors, image0, image1, sems, band_sem = refs[ends[3] + 4 :]
    blocks_here = grad.shape[0]
    rows = grad.shape[1] // 2
    cols = field.shape[2]
    half = cols // 2
    window = blocks_here * len(sources)
    me_rcv, me_src = lax.axis_index("rcv"), lax.axis_index("src")
    odd = lax.rem(me_rcv, 2)
    where = [ring_place(n_src, me_src, shift) for shift in shifts]

    fetches = [
        [
            pltpu.make_async_copy(source, held.at[g, slot], sems.at[g, slot])
            for slot, source in enumerate(group)
            if not in_place(n_src, g, slot)
        ]
        for g, group in enumerate(sources)
    ]

    def chunk(g, slot):
        return sources[g][slot][...] if in_place(n_src, g, slot) else held[g, slot]

    band_fetch = pltpu.make_async_copy(band_in, band, band_sem)
    band_fetch.start()
    for fetch in sum(fetches, []):
        fetch.start()
    band_fetch.wait()

    places = {}
    for i in range(blocks_here):
        for k in range(NEIGH):
            offset = band[i, k] - me_rcv * blocks_here
            before, here = offset < 0, (offset >= 0) & (offset < blocks_here)
            group = jnp.where(here, 0, jnp.where(jnp.where(before, 1, 0) == odd, 1, 2))
            inside = jnp.where(before, offset + blocks_here, jnp.where(here, offset, offset - blocks_here))
            places[i, k] = group * blocks_here + inside

    def store(i, slot, re_bf, im_bf):
        top, low = slice(2 * i * rows, (2 * i + 1) * rows), slice((2 * i + 1) * rows, (2 * i + 2) * rows)
        left, right = slice(slot * cols, slot * cols + half), slice(slot * cols + half, (slot + 1) * cols)
        lhs[top, left] = re_bf
        lhs[top, right] = im_bf
        lhs[low, left] = im_bf
        lhs[low, right] = -re_bf

    def fold(x):
        total = x[:, :128]
        for c in range(128, x.shape[1], 128):
            total = total + x[:, c : c + 128]
        return jnp.sum(total, axis=0, keepdims=True)

    def adjoint(out, first):
        for g in range(len(sources)):
            if first:
                for fetch in fetches[g]:
                    fetch.wait()
            chunks = jnp.concatenate([chunk(g, slot) for slot in range(n_src)], axis=1)
            both = lax.dot_general(lhs[...], chunks, (((1,), (1,)), ((), ())), preferred_element_type=jnp.float32)
            for inside in range(blocks_here):
                every[g * blocks_here + inside] = both[:, inside * BLOCK : (inside + 1) * BLOCK]
        for i in range(blocks_here):
            mine = slice(2 * i * rows, 2 * (i + 1) * rows)
            for k in range(NEIGH):
                part = every[places[i, k], mine, :]
                out[i, :, k * BLOCK : (k + 1) * BLOCK] = part
                factors[places[i, k], mine, :] = part.astype(jnp.bfloat16)

    def forward():
        wide = jnp.concatenate([factors[place] for place in range(window)], axis=1)
        for base in range(0, n_src, PAIR):
            slots = range(base, min(base + PAIR, n_src))
            columns = [
                jnp.concatenate([chunk(g, slot) for g in range(len(sources))], axis=0) for slot in slots
            ]
            prod = jnp.dot(wide, jnp.concatenate(columns, axis=1), preferred_element_type=jnp.float32)
            for slot in slots:
                left = (slot - base) * cols
                for i in range(blocks_here):
                    top = prod[2 * i * rows : (2 * i + 1) * rows, left : left + cols]
                    low = prod[(2 * i + 1) * rows : 2 * (i + 1) * rows, left : left + cols]
                    yield slot, i, top[:, :half] - low[:, half:], top[:, half:] + low[:, :half]

    factors[...] = jnp.zeros_like(factors)
    for slot in range(n_src):
        for i in range(blocks_here):
            rows_bf = field[where[slot], i * rows : (i + 1) * rows, :]
            store(i, slot, rows_bf[:, :half], rows_bf[:, half:])

    zero = jnp.zeros((1, 128), jnp.float32)
    gg, qq, gh, hh, qw, ww = zero, zero, zero, zero, zero, zero
    adjoint(grad, True)
    for i in range(blocks_here):
        gg += fold(grad[i] * grad[i])
    for slot, i, re, im in forward():
        mine = slice(i * rows, (i + 1) * rows)
        qq += fold(re * re + im * im)
        image0[slot, mine, :half] = re
        image0[slot, mine, half:] = im
        store(i, slot, re.astype(jnp.bfloat16), im.astype(jnp.bfloat16))
    adjoint(hess, False)
    for i in range(blocks_here):
        gh += fold(hess[i] * grad[i])
        hh += fold(hess[i] * hess[i])
    for slot, i, re, im in forward():
        mine = slice(i * rows, (i + 1) * rows)
        ww += fold(re * re + im * im)
        qw += fold(re * image0[slot, mine, :half] + im * image0[slot, mine, half:])
        image1[slot, mine, :half] = re
        image1[slot, mine, half:] = im
    sums = jnp.concatenate([gg, qq, gh, hh, qw, ww, zero, zero], axis=0)
    sums_out[...] = sums
    share_bf = along(sums).astype(jnp.bfloat16)
    share = share_bf.astype(jnp.float32)
    height = blocks_here * rows
    for slot in range(n_src):
        first = image0[slot]
        images[where[slot], :height] = first.astype(jnp.bfloat16)
        images[where[slot], height : 2 * height] = (image1[slot] - share * first).astype(jnp.bfloat16)
        images[where[slot], 2 * height :] = jnp.broadcast_to(share_bf, (SHARE_ROWS, cols))


def combine_kernel(sums, images, grad, hess, start, refl_out, misfit_out):
    n_src, height = images.shape[0], (images.shape[1] - SHARE_ROWS) // 2
    total = jnp.sum(sums[...], axis=1, keepdims=True)
    gg, qq, gh, hh, qw, ww = [total[i : i + 1] for i in range(6)]
    step0 = gg / qq
    grad_next = gg - 2 * step0 * gh + step0 * step0 * hh
    near = 1 + grad_next / gg
    image_sq = near * near * qq - 2 * near * step0 * qw + step0 * step0 * ww
    step1 = grad_next / image_sq
    c1 = step0 + step1 * near
    c2 = -step0 * step1
    blocks_here, rows = grad.shape[0], grad.shape[1] // 2
    half = start.shape[2] // 2
    for i in range(blocks_here):
        for k in range(NEIGH):
            for t in range(2):
                part = (i, slice(t * rows, (t + 1) * rows), slice(k * BLOCK, (k + 1) * BLOCK))
                refl_out[:, i, k, t, :] = c1 * grad[part] + c2 * hess[part]
    for s in range(n_src):
        share = images[s, 2 * height :].astype(jnp.float32)[:1, :1]
        first = images[s, :height].astype(jnp.float32)
        rest = images[s, height : 2 * height].astype(jnp.float32)
        left = start[s].astype(jnp.float32) - ((c1 + c2 * share) * first + c2 * rest)
        for i in range(blocks_here):
            place = slice(i * BLOCK + s * rows, i * BLOCK + (s + 1) * rows)
            mine = left[i * rows : (i + 1) * rows]
            misfit_out[place, 0, :] = mine[:, :half]
            misfit_out[place, 1, :] = mine[:, half:]


def summed(x, axis, count):
    if count & (count - 1):
        return lax.psum(x, axis)
    bit = 1
    while bit < count:
        radix = min(4, count // bit)
        others = [lax.ppermute(x, axis, [(d, d ^ (bit * m)) for d in range(count)]) for m in range(1, radix)]
        x = (x + others[0]) + (others[1] + others[2]) if radix == 4 else x + others[0]
        bit *= radix
    return x


def per_device(n_rcv, n_src, pplus, pminus, band):
    blocks_here = band.shape[0]
    rows = BLOCK // n_src
    cols = 2 * pplus.shape[2]
    order = ring_order(n_src)
    ahead = [(order[p], order[(p + 1) % n_src]) for p in range(n_src)]
    behind = [(d, s) for s, d in ahead]

    def swaps(first):
        pairs = [(r, r + 1) for r in range(first, n_rcv - 1, 2)]
        return pairs + [(d, s) for s, d in pairs]

    start = lax.optimization_barrier(pminus.reshape(blocks_here * BLOCK, cols))
    start = jnp.transpose(start.reshape(blocks_here, n_src, rows, cols), (1, 0, 2, 3))
    start = start.reshape(n_src, blocks_here * rows, cols)
    field = lax.all_to_all(start, "src", 0, 0, tiled=True)

    own = pplus.reshape(blocks_here * BLOCK, cols)
    chunks, shifts = [own], [0]
    fwd = bwd = own
    for step in range(1, n_src // 2 + 1):
        fwd = lax.ppermute(fwd, "src", ahead)
        chunks.append(fwd)
        shifts.append(-step)
        if len(chunks) < n_src:
            bwd = lax.ppermute(bwd, "src", behind)
            chunks.append(bwd)
            shifts.append(step)
    near = [lax.ppermute(c, "rcv", swaps(0)) for c in chunks]
    far = [lax.ppermute(c, "rcv", swaps(1)) for c in chunks]
    gathered = [
        pltpu.with_memory_space_constraint(x, pltpu.VMEM) if in_place(n_src, g, slot) else x
        for g, group in enumerate((chunks, near, far))
        for slot, x in enumerate(group)
    ]
    any_spec = pl.BlockSpec(memory_space=pl.ANY)
    vmem = pl.BlockSpec(memory_space=pltpu.VMEM)
    band_cols = NEIGH * BLOCK
    grad, hess, images, sums = pl.pallas_call(
        functools.partial(maps_kernel, n_src, shifts),
        out_shape=(
            jax.ShapeDtypeStruct((blocks_here, 2 * rows, band_cols), jnp.float32),
            jax.ShapeDtypeStruct((blocks_here, 2 * rows, band_cols), jnp.float32),
            jax.ShapeDtypeStruct((n_src, 2 * blocks_here * rows + SHARE_ROWS, cols), jnp.bfloat16),
            jax.ShapeDtypeStruct((8, 128), jnp.float32),
        ),
        in_specs=[any_spec, vmem]
        + [vmem if in_place(n_src, g, slot) else any_spec for g in range(3) for slot in range(n_src)],
        out_specs=[vmem] * 4,
        scratch_shapes=[
            pltpu.SMEM(band.shape, jnp.int32),
            pltpu.VMEM((3, n_src, blocks_here * BLOCK, cols), jnp.bfloat16),
            pltpu.VMEM((blocks_here * 2 * rows, n_src * cols), jnp.bfloat16),
            pltpu.VMEM((3 * blocks_here, blocks_here * 2 * rows, BLOCK), jnp.float32),
            pltpu.VMEM((3 * blocks_here, blocks_here * 2 * rows, BLOCK), jnp.bfloat16),
            pltpu.VMEM((n_src, blocks_here * rows, cols), jnp.float32),
            pltpu.VMEM((n_src, blocks_here * rows, cols), jnp.float32),
            pltpu.SemaphoreType.DMA((3, n_src)),
            pltpu.SemaphoreType.DMA,
        ],
        compiler_params=pltpu.CompilerParams(vmem_limit_bytes=56 << 20),
        name="maps",
    )(band, field, *gathered)

    images = lax.all_to_all(images, "src", 0, 0, tiled=True)
    sums = summed(summed(sums, "rcv", n_rcv), "src", n_src)
    return tuple(
        pl.pallas_call(
            combine_kernel,
            out_shape=(
                jax.ShapeDtypeStruct((rows, blocks_here, NEIGH, 2, BLOCK), jnp.float32),
                jax.ShapeDtypeStruct(pminus.shape, jnp.float32),
            ),
            in_specs=[vmem] * 5,
            out_specs=[vmem] * 2,
            compiler_params=pltpu.CompilerParams(vmem_limit_bytes=16 << 20),
            name="combine",
        )(sums, images, grad, hess, start)
    )


def solution(mesh):
    return jax.shard_map(
        functools.partial(per_device, mesh.shape["rcv"], mesh.shape["src"]),
        mesh=mesh,
        in_specs=(P("rcv", None, "src"), P("rcv", None, "src"), P("rcv", None)),
        out_specs=(P("src", "rcv", None, None, None), P("rcv", None, "src")),
        check_vma=False,
    )
```

```python
import functools

import jax
import jax.numpy as jnp
from jax import lax
from jax.experimental import pallas as pl
from jax.experimental.pallas import tpu as pltpu
from jax.sharding import PartitionSpec as P

BLOCK = 256
NEIGH = 3
HALO_BLK = 2
ROWS_X = 2
SHARE_ROWS = 16
PAIR = 2
IN_PLACE = 8
LATE = 4


def ring_order(count):
    if count % ROWS_X or count < 2 * ROWS_X:
        return list(range(count))
    half = count // ROWS_X
    return [ROWS_X * p for p in range(half)] + [ROWS_X * p + 1 for p in reversed(range(half))]


def ring_place(count, index, shift):
    if count % ROWS_X or count < 2 * ROWS_X:
        return lax.rem(index + shift + count, count)
    half, odd = count // ROWS_X, lax.rem(index, ROWS_X)
    step = (index - odd) // ROWS_X
    place = lax.rem(jnp.where(odd == 1, count - 1 - step, step) + shift + count, count)
    return jnp.where(place < half, ROWS_X * place, ROWS_X * (count - 1 - place) + 1)


def along(sums):
    total = jnp.sum(sums, axis=1, keepdims=True)
    qq, qw = total[1:2], total[4:5]
    return jnp.where(qq > 0, qw / jnp.where(qq > 0, qq, 1.0), 0.0)


def in_place(n_src, g, slot):
    return slot >= n_src - LATE if g else slot < IN_PLACE


def maps_kernel(n_src, shifts, *refs):
    band_in, field = refs[:2]
    ends = [2, 2 + n_src, 2 + 2 * n_src, 2 + 3 * n_src]
    sources = [refs[a:b] for a, b in zip(ends[:-1], ends[1:])]
    grad, hess, images, sums_out = refs[ends[3] : ends[3] + 4]
    band, held, lhs, every, factors, image0, image1, sems, band_sem = refs[ends[3] + 4 :]
    blocks_here = grad.shape[0]
    rows = grad.shape[1] // 2
    cols = field.shape[2]
    half = cols // 2
    window = blocks_here * len(sources)
    me_rcv, me_src = lax.axis_index("rcv"), lax.axis_index("src")
    odd = lax.rem(me_rcv, 2)
    where = [ring_place(n_src, me_src, shift) for shift in shifts]

    fetches = [
        [
            pltpu.make_async_copy(source, held.at[g, slot], sems.at[g, slot])
            for slot, source in enumerate(group)
            if not in_place(n_src, g, slot)
        ]
        for g, group in enumerate(sources)
    ]

    def chunk(g, slot):
        return sources[g][slot][...] if in_place(n_src, g, slot) else held[g, slot]

    band_fetch = pltpu.make_async_copy(band_in, band, band_sem)
    band_fetch.start()
    for fetch in sum(fetches, []):
        fetch.start()
    band_fetch.wait()

    places = {}
    for i in range(blocks_here):
        for k in range(NEIGH):
            offset = band[i, k] - me_rcv * blocks_here
            before, here = offset < 0, (offset >= 0) & (offset < blocks_here)
            group = jnp.where(here, 0, jnp.where(jnp.where(before, 1, 0) == odd, 1, 2))
            inside = jnp.where(before, offset + blocks_here, jnp.where(here, offset, offset - blocks_here))
            places[i, k] = group * blocks_here + inside

    def store(i, slot, re_bf, im_bf):
        top, low = slice(2 * i * rows, (2 * i + 1) * rows), slice((2 * i + 1) * rows, (2 * i + 2) * rows)
        left, right = slice(slot * cols, slot * cols + half), slice(slot * cols + half, (slot + 1) * cols)
        lhs[top, left] = re_bf
        lhs[top, right] = im_bf
        lhs[low, left] = im_bf
        lhs[low, right] = -re_bf

    def fold(x):
        total = x[:, :128]
        for c in range(128, x.shape[1], 128):
            total = total + x[:, c : c + 128]
        return jnp.sum(total, axis=0, keepdims=True)

    def adjoint(out, first):
        for g in range(len(sources)):
            if first:
                for fetch in fetches[g]:
                    fetch.wait()
            chunks = jnp.concatenate([chunk(g, slot) for slot in range(n_src)], axis=1)
            both = lax.dot_general(lhs[...], chunks, (((1,), (1,)), ((), ())), preferred_element_type=jnp.float32)
            for inside in range(blocks_here):
                every[g * blocks_here + inside] = both[:, inside * BLOCK : (inside + 1) * BLOCK]
        for i in range(blocks_here):
            mine = slice(2 * i * rows, 2 * (i + 1) * rows)
            for k in range(NEIGH):
                part = every[places[i, k], mine, :]
                out[i, :, k * BLOCK : (k + 1) * BLOCK] = part
                factors[places[i, k], mine, :] = part.astype(jnp.bfloat16)

    def forward():
        wide = jnp.concatenate([factors[place] for place in range(window)], axis=1)
        for base in range(0, n_src, PAIR):
            slots = range(base, min(base + PAIR, n_src))
            columns = [
                jnp.concatenate([chunk(g, slot) for g in range(len(sources))], axis=0) for slot in slots
            ]
            prod = jnp.dot(wide, jnp.concatenate(columns, axis=1), preferred_element_type=jnp.float32)
            for slot in slots:
                left = (slot - base) * cols
                for i in range(blocks_here):
                    top = prod[2 * i * rows : (2 * i + 1) * rows, left : left + cols]
                    low = prod[(2 * i + 1) * rows : 2 * (i + 1) * rows, left : left + cols]
                    yield slot, i, top[:, :half] - low[:, half:], top[:, half:] + low[:, :half]

    factors[...] = jnp.zeros_like(factors)
    for slot in range(n_src):
        for i in range(blocks_here):
            rows_bf = field[where[slot], i * rows : (i + 1) * rows, :]
            store(i, slot, rows_bf[:, :half], rows_bf[:, half:])

    zero = jnp.zeros((1, 128), jnp.float32)
    gg, qq, gh, hh, qw, ww = zero, zero, zero, zero, zero, zero
    adjoint(grad, True)
    for i in range(blocks_here):
        gg += fold(grad[i] * grad[i])
    for slot, i, re, im in forward():
        mine = slice(i * rows, (i + 1) * rows)
        qq += fold(re * re + im * im)
        image0[slot, mine, :half] = re
        image0[slot, mine, half:] = im
        store(i, slot, re.astype(jnp.bfloat16), im.astype(jnp.bfloat16))
    adjoint(hess, False)
    for i in range(blocks_here):
        gh += fold(hess[i] * grad[i])
        hh += fold(hess[i] * hess[i])
    for slot, i, re, im in forward():
        mine = slice(i * rows, (i + 1) * rows)
        ww += fold(re * re + im * im)
        qw += fold(re * image0[slot, mine, :half] + im * image0[slot, mine, half:])
        image1[slot, mine, :half] = re
        image1[slot, mine, half:] = im
    sums = jnp.concatenate([gg, qq, gh, hh, qw, ww, zero, zero], axis=0)
    sums_out[...] = sums
    share_bf = along(sums).astype(jnp.bfloat16)
    share = share_bf.astype(jnp.float32)
    height = blocks_here * rows
    for slot in range(n_src):
        first = image0[slot]
        images[where[slot], :height] = first.astype(jnp.bfloat16)
        images[where[slot], height : 2 * height] = (image1[slot] - share * first).astype(jnp.bfloat16)
        images[where[slot], 2 * height :] = jnp.broadcast_to(share_bf, (SHARE_ROWS, cols))


def combine_kernel(sums, images, grad, hess, start, refl_out, misfit_out):
    n_src, height = images.shape[0], (images.shape[1] - SHARE_ROWS) // 2
    total = jnp.sum(sums[...], axis=1, keepdims=True)
    gg, qq, gh, hh, qw, ww = [total[i : i + 1] for i in range(6)]
    step0 = gg / qq
    grad_next = gg - 2 * step0 * gh + step0 * step0 * hh
    near = 1 + grad_next / gg
    image_sq = near * near * qq - 2 * near * step0 * qw + step0 * step0 * ww
    step1 = grad_next / image_sq
    c1 = step0 + step1 * near
    c2 = -step0 * step1
    blocks_here, rows = grad.shape[0], grad.shape[1] // 2
    half = start.shape[2] // 2
    for i in range(blocks_here):
        for k in range(NEIGH):
            for t in range(2):
                part = (i, slice(t * rows, (t + 1) * rows), slice(k * BLOCK, (k + 1) * BLOCK))
                refl_out[:, i, k, t, :] = c1 * grad[part] + c2 * hess[part]
    for s in range(n_src):
        share = images[s, 2 * height :].astype(jnp.float32)[:1, :1]
        first = images[s, :height].astype(jnp.float32)
        rest = images[s, height : 2 * height].astype(jnp.float32)
        left = start[s].astype(jnp.float32) - ((c1 + c2 * share) * first + c2 * rest)
        for i in range(blocks_here):
            place = slice(i * BLOCK + s * rows, i * BLOCK + (s + 1) * rows)
            mine = left[i * rows : (i + 1) * rows]
            misfit_out[place, 0, :] = mine[:, :half]
            misfit_out[place, 1, :] = mine[:, half:]


def summed(x, axis, count):
    if count & (count - 1):
        return lax.psum(x, axis)
    bit = 1
    while bit < count:
        radix = min(4, count // bit)
        others = [lax.ppermute(x, axis, [(d, d ^ (bit * m)) for d in range(count)]) for m in range(1, radix)]
        x = (x + others[0]) + (others[1] + others[2]) if radix == 4 else x + others[0]
        bit *= radix
    return x


def per_device(n_rcv, n_src, pplus, pminus, band):
    blocks_here = band.shape[0]
    rows = BLOCK // n_src
    cols = 2 * pplus.shape[2]
    order = ring_order(n_src)
    ahead = [(order[p], order[(p + 1) % n_src]) for p in range(n_src)]
    behind = [(d, s) for s, d in ahead]

    def swaps(first):
        pairs = [(r, r + 1) for r in range(first, n_rcv - 1, 2)]
        return pairs + [(d, s) for s, d in pairs]

    start = lax.optimization_barrier(pminus.reshape(blocks_here * BLOCK, cols))
    start = jnp.transpose(start.reshape(blocks_here, n_src, rows, cols), (1, 0, 2, 3))
    start = start.reshape(n_src, blocks_here * rows, cols)
    field = lax.all_to_all(start, "src", 0, 0, tiled=True)

    own = pplus.reshape(blocks_here * BLOCK, cols)
    chunks, shifts = [own], [0]
    fwd = bwd = own
    for step in range(1, n_src // 2 + 1):
        fwd = lax.ppermute(fwd, "src", ahead)
        chunks.append(fwd)
        shifts.append(-step)
        if len(chunks) < n_src:
            bwd = lax.ppermute(bwd, "src", behind)
            chunks.append(bwd)
            shifts.append(step)
    near = [lax.ppermute(c, "rcv", swaps(0)) for c in chunks]
    far = [lax.ppermute(c, "rcv", swaps(1)) for c in chunks]
    gathered = [
        pltpu.with_memory_space_constraint(x, pltpu.VMEM) if in_place(n_src, g, slot) else x
        for g, group in enumerate((chunks, near, far))
        for slot, x in enumerate(group)
    ]
    any_spec = pl.BlockSpec(memory_space=pl.ANY)
    vmem = pl.BlockSpec(memory_space=pltpu.VMEM)
    band_cols = NEIGH * BLOCK
    grad, hess, images, sums = pl.pallas_call(
        functools.partial(maps_kernel, n_src, shifts),
        out_shape=(
            jax.ShapeDtypeStruct((blocks_here, 2 * rows, band_cols), jnp.float32),
            jax.ShapeDtypeStruct((blocks_here, 2 * rows, band_cols), jnp.float32),
            jax.ShapeDtypeStruct((n_src, 2 * blocks_here * rows + SHARE_ROWS, cols), jnp.bfloat16),
            jax.ShapeDtypeStruct((8, 128), jnp.float32),
        ),
        in_specs=[any_spec, vmem]
        + [vmem if in_place(n_src, g, slot) else any_spec for g in range(3) for slot in range(n_src)],
        out_specs=[vmem] * 4,
        scratch_shapes=[
            pltpu.SMEM(band.shape, jnp.int32),
            pltpu.VMEM((3, n_src, blocks_here * BLOCK, cols), jnp.bfloat16),
            pltpu.VMEM((blocks_here * 2 * rows, n_src * cols), jnp.bfloat16),
            pltpu.VMEM((3 * blocks_here, blocks_here * 2 * rows, BLOCK), jnp.float32),
            pltpu.VMEM((3 * blocks_here, blocks_here * 2 * rows, BLOCK), jnp.bfloat16),
            pltpu.VMEM((n_src, blocks_here * rows, cols), jnp.float32),
            pltpu.VMEM((n_src, blocks_here * rows, cols), jnp.float32),
            pltpu.SemaphoreType.DMA((3, n_src)),
            pltpu.SemaphoreType.DMA,
        ],
        compiler_params=pltpu.CompilerParams(vmem_limit_bytes=55 << 20),
        name="maps",
    )(band, field, *gathered)

    images = lax.all_to_all(images, "src", 0, 0, tiled=True)
    sums = summed(summed(sums, "rcv", n_rcv), "src", n_src)
    return tuple(
        pl.pallas_call(
            combine_kernel,
            out_shape=(
                jax.ShapeDtypeStruct((rows, blocks_here, NEIGH, 2, BLOCK), jnp.float32),
                jax.ShapeDtypeStruct(pminus.shape, jnp.float32),
            ),
            in_specs=[vmem] * 5,
            out_specs=[vmem] * 2,
            compiler_params=pltpu.CompilerParams(vmem_limit_bytes=16 << 20),
            name="combine",
        )(sums, images, grad, hess, start)
    )


def solution(mesh):
    return jax.shard_map(
        functools.partial(per_device, mesh.shape["rcv"], mesh.shape["src"]),
        mesh=mesh,
        in_specs=(P("rcv", None, "src"), P("rcv", None, "src"), P("rcv", None)),
        out_specs=(P("src", "rcv", None, None, None), P("rcv", None, "src")),
        check_vma=False,
    )
```
